256 devices in a mesh: dp: 32 (over z_hi, y, core), tm: 4 (over x), tile: 2 (over z_lo).
Axes of the slice: x: 4, y: 4, z: 8 (z_hi: 4, z_lo: 2; z = z_hi * 2 + z_lo), core: 2. Of those that a mesh axis runs over, the one named last changes fastest.
Arguments:
- activations: bfloat16 [32, 32, 16, 32, 128], P('dp', 'tm', 'tile'), may hold values from -6 to 6
- kernel: bfloat16 [3456, 128], replicated, may hold values from -0.109375 to 0.109375
- conv_bias: float32 [128], replicated, may hold values from -3 to 3
- cotangent: bfloat16 [32, 32, 16, 32, 128], P('dp', 'tm', 'tile'), may hold values from -6 to 6
Outputs:
- block_out: bfloat16 [32, 32, 16, 32, 128], P('dp', 'tm', 'tile')
- grad_input: bfloat16 [32, 32, 16, 32, 128], P('dp', 'tm', 'tile')
- weight_grad: float32 [3456, 128], P('dp')
- bias_grad: float32 [128], P('dp')
The draws below stay inside these ranges and needn't reach their ends.
All inputs are finite; a program needn't handle non-finite values.
Results may differ from the reference program's by a relative error of at most 0.0095.
Values may be sent and summed in bfloat16 or wider, within the bound.
A program may use at most 64 MiB of HBM per device.

```python
import jax
import jax.numpy as jnp
from jax import lax

C = 128
COLS = 32
CLIPS = 32
FRAMES = 32
ROWS = 16
POSITIONS = 524288


def steps_of(key, extent, cuts, low, high):
    loudness = 1.0
    for dim, shards_of in cuts:
        steps = jax.random.uniform(jax.random.fold_in(jax.random.fold_in(key, 6), dim), (shards_of,), jnp.float32, low / len(cuts), high / len(cuts))
        loudness = loudness * jnp.repeat(jnp.exp(steps), extent[dim] // shards_of).reshape((-1,) + (1,) * (len(extent) - 1 - dim))
    return loudness


def gaussian(key, extent, scale, bound, cuts=(), kind=jnp.bfloat16):
    values = scale * jax.random.normal(key, extent, jnp.float32)
    if cuts:
        values = values * steps_of(key, extent, cuts, -0.22, 0.18)
    return jnp.clip(values, -bound, bound).astype(kind)


def setup_inputs(seed: int = 0) -> dict:
    seeds = jax.random.split(jax.random.key(seed), 5)
    return {
        "activations": gaussian(seeds[0], (CLIPS, FRAMES, ROWS, COLS, C), 1.0, 6.0, ((0, 32), (1, 4), (2, 2))),
        "kernel": gaussian(seeds[1], (27 * C, C), (27 * C) ** -0.5, 0.109375),
        "conv_bias": gaussian(seeds[2], (C,), 0.5, 3.0, (), jnp.float32),
        "cotangent": gaussian(seeds[3], (CLIPS, FRAMES, ROWS, COLS, C), 1.0, 6.0, ((0, 32), (1, 4), (2, 2))),
    }


def reference(activations, kernel, conv_bias, cotangent):
    channels = kernel.shape[1]
    taps = kernel.astype(jnp.float32).reshape(3, 3, 3, channels, channels)
    frames = activations.shape[1]
    height = activations.shape[2]
    breadth = activations.shape[3]
    scale = float(POSITIONS) ** -0.5

    def one_clip(carry, pair):
        weight_sum, bias_sum = carry
        video, upstream = pair
        padded = jnp.pad(video, ((2, 0), (1, 1), (1, 1), (0, 0))).astype(jnp.float32)
        running = jnp.zeros((frames, height, breadth, channels), jnp.float32) + conv_bias
        for tap_time in range(3):
            for tap_row in range(3):
                for tap_col in range(3):
                    window = padded[tap_time:tap_time + frames, tap_row:tap_row + height, tap_col:tap_col + breadth]
                    running = running + jnp.einsum("frwc,cd->frwd", window, taps[tap_time, tap_row, tap_col])
        sigma = jax.nn.sigmoid(running)
        output = (video.astype(jnp.float32) + running * sigma).astype(jnp.bfloat16)
        grad_pre = (upstream.astype(jnp.float32) * sigma * (1.0 + running * (1.0 - sigma))).astype(jnp.bfloat16)
        grad_float = grad_pre.astype(jnp.float32)
        grad_padded = jnp.pad(grad_float, ((0, 2), (1, 1), (1, 1), (0, 0)))
        back = upstream.astype(jnp.float32)
        pieces = []
        for tap_time in range(3):
            for tap_row in range(3):
                for tap_col in range(3):
                    window = grad_padded[2 - tap_time:2 - tap_time + frames, 2 - tap_row:2 - tap_row + height, 2 - tap_col:2 - tap_col + breadth]
                    back = back + jnp.einsum("frwd,cd->frwc", window, taps[tap_time, tap_row, tap_col])
                    source = padded[tap_time:tap_time + frames, tap_row:tap_row + height, tap_col:tap_col + breadth]
                    pieces.append(jnp.einsum("frwc,frwd->cd", source, grad_float))
        weight_sum = weight_sum + jnp.stack(pieces).reshape(27 * channels, channels)
        bias_sum = bias_sum + jnp.sum(grad_float, axis=(0, 1, 2))
        return (weight_sum, bias_sum), (output, back.astype(jnp.bfloat16))

    start = (jnp.zeros((27 * channels, channels), jnp.float32), jnp.zeros((channels,), jnp.float32))
    (weight_sum, bias_sum), (block_out, grad_input) = lax.scan(one_clip, start, (activations, cotangent))
    return block_out, grad_input, weight_sum * scale, bias_sum * scale
```

```python
import math

import jax
import jax.numpy as jnp
from jax import lax
from jax.experimental import pallas as pl
from jax.experimental.pallas import tpu as pltpu
from jax.sharding import PartitionSpec as P

F32 = jnp.float32
BF = jnp.bfloat16
MESH = pl.DeviceIdType.MESH

C = 128
FRAMES, ROWS, COLS = 8, 8, 32
AREA = ROWS * COLS
POSITIONS = FRAMES * AREA
TAPS_AB = [(a, b) for a in range(3) for b in range(3)]
SHARD = 108
BLOCK = 112
SCALE = 1.0 / math.sqrt(524288.0)


def shift_columns(values, by):
    rows = values.shape[0]
    rolled = pltpu.roll(values, by % rows, 0)
    column = lax.broadcasted_iota(jnp.int32, values.shape, 0) & (COLS - 1)
    return jnp.where(column == (0 if by == 1 else COLS - 1), 0.0, rolled)


def forward_frame(t, xp, wf, bias, ctv, bov, gp, gt, bsum, first):
    lhs = jnp.concatenate(
        [xp[t + a, b : b + ROWS].reshape(AREA, C) for a, b in TAPS_AB], axis=1
    )
    y = jnp.dot(lhs, wf[...].reshape(9 * C, 3 * C), preferred_element_type=F32)
    pre = y[:, C : 2 * C] + shift_columns(y[:, :C], 1) + shift_columns(y[:, 2 * C :], -1)
    pre = pre + bias[...]
    sig = 0.5 * jnp.tanh(0.5 * pre) + 0.5
    center = xp[t + 2, 1 : 1 + ROWS].reshape(AREA, C).astype(F32)
    bov[t] = (center + pre * sig).astype(BF).reshape(ROWS, COLS, C)
    grad = ctv[t].reshape(AREA, C).astype(F32) * (sig * (1.0 + pre * (1.0 - sig)))
    grad = grad.astype(BF)
    gp[t, 1 : 1 + ROWS] = grad.reshape(ROWS, COLS, C)
    grad = grad.astype(F32)
    part = jnp.sum(grad.reshape(AREA // 8, 8, C), axis=0)
    if first:
        bsum[...] = part
    else:
        bsum[...] += part
    turned = jnp.transpose(grad)
    lane = lax.broadcasted_iota(jnp.int32, (C, C), 1) & (COLS - 1)
    start = t * AREA
    gt[C : 2 * C, start : start + AREA] = turned.astype(BF)
    for half in range(2):
        piece = turned[:, half * C : half * C + C]
        at = start + half * C
        ahead = jnp.where(lane == COLS - 1, 0.0, pltpu.roll(piece, C - 1, 1))
        behind = jnp.where(lane == 0, 0.0, pltpu.roll(piece, 1, 1))
        gt[0:C, at : at + C] = ahead.astype(BF)
        gt[2 * C : 3 * C, at : at + C] = behind.astype(BF)


def weight_taps(d, xp, gt, dw):
    pairs = TAPS_AB[2 * d : 2 * d + 2]
    rhs = jnp.concatenate(
        [xp[a : a + FRAMES, b : b + ROWS].reshape(POSITIONS, C) for a, b in pairs], axis=1
    )
    out = jnp.dot(gt[...], rhs, preferred_element_type=F32)
    for j in range(len(pairs)):
        for e in range(3):
            tap = (2 * d + j) * 3 + e
            dw[tap * C : tap * C + C] = jnp.transpose(
                out[e * C : e * C + C, j * C : j * C + C]
            )


def backward_frames(t, n, gp, wt, ctv, giv):
    rows = n * AREA
    lhs = jnp.concatenate(
        [gp[t + 2 - a : t + 2 - a + n, 2 - b : 2 - b + ROWS].reshape(rows, C) for a, b in TAPS_AB],
        axis=1,
    )
    y = lax.dot_general(
        lhs,
        wt[...].reshape(3 * C, 9 * C),
        (((1,), (1,)), ((), ())),
        preferred_element_type=F32,
    )
    out = y[:, C : 2 * C] + shift_columns(y[:, :C], -1) + shift_columns(y[:, 2 * C :], 1)
    out = out + ctv[t : t + n].reshape(rows, C).astype(F32)
    giv[t : t + n] = out.astype(BF).reshape(n, ROWS, COLS, C)


def kernel(
    act, ker, bias, cot, block_out, grad_input, weight_grad, bias_grad,
    xp, gp, wf, wt, ctv, bov, giv, gt, dw, bsum,
    pk, cr, ys, yr, yown, zs, zr, zown, fr,
    load_sem, out_sem, halo_send, halo_recv, ghalo_send, ghalo_recv,
    core_send, core_recv, y_send, y_recv, z_send, z_recv, f_send, f_recv,
):
    dp = lax.axis_index("dp")
    x = lax.axis_index("tm")
    zl = lax.axis_index("tile")
    core = lax.rem(dp, 2)
    y = lax.rem(dp // 2, 4)
    zh = dp // 8
    other = 1 - zl

    def dp_at(zh_, y_, core_):
        return (zh_ * 4 + y_) * 2 + core_

    loads = [pltpu.make_async_copy(act.at[0], xp.at[2:10, 1:9], load_sem.at[0])]
    for e in range(3):
        loads.append(
            pltpu.make_async_copy(
                ker.at[:, e], wf.at[:, :, e * C : e * C + C], load_sem.at[1 + e]
            )
        )
    loads.append(pltpu.make_async_copy(cot.at[0], ctv, load_sem.at[4]))
    for load in loads:
        load.start()
    late = [
        pltpu.make_async_copy(ker.at[i], wt.at[:, :, i * C : i * C + C], load_sem.at[5 + i])
        for i in range(9)
    ]
    for load in late:
        load.start()

    barrier = pltpu.get_barrier_semaphore()
    group = x * 2 + zl
    for k in range(1, 8):
        to = lax.rem(group + k, 8)
        pl.semaphore_signal(
            barrier, inc=1,
            device_id={"dp": dp, "tm": to // 2, "tile": lax.rem(to, 2)},
            device_id_type=MESH,
        )
    pl.semaphore_signal(
        barrier, inc=1,
        device_id={"dp": dp_at(zh, y, 1 - core), "tm": x, "tile": zl}, device_id_type=MESH,
    )
    for k in range(1, 4):
        pl.semaphore_signal(
            barrier, inc=1,
            device_id={"dp": dp_at(zh, lax.rem(y + k, 4), core), "tm": x, "tile": zl},
            device_id_type=MESH,
        )
        pl.semaphore_signal(
            barrier, inc=1,
            device_id={"dp": dp_at(lax.rem(zh + k, 4), y, core), "tm": x, "tile": zl},
            device_id_type=MESH,
        )

    edge = 9 * zl
    row_zeros = jnp.zeros((10, COLS, C), BF)
    xp[:, edge] = row_zeros
    gp[:, edge] = row_zeros

    @pl.when(x == 0)
    def _():
        xp[0:2] = jnp.zeros((2, 10, COLS, C), BF)

    @pl.when(x == 3)
    def _():
        gp[8:10] = jnp.zeros((2, 10, COLS, C), BF)

    pl.semaphore_wait(barrier, 14)

    out_row = 7 * other
    into_row = 9 * zl
    recv_row = 9 * other

    def remote(src, dst, send, recv, where):
        return pltpu.make_async_remote_copy(
            src_ref=src, dst_ref=dst, send_sem=send, recv_sem=recv,
            device_id=where, device_id_type=MESH,
        )

    here_dp = {"dp": dp}
    halo_rows = remote(
        act.at[0, :, out_row], xp.at[2:10, into_row], halo_send.at[0], halo_recv.at[0],
        {**here_dp, "tm": x, "tile": other},
    )
    later = jnp.minimum(x + 1, 3)
    halo_frames = remote(
        act.at[0, 6:8], xp.at[0:2, 1:9], halo_send.at[1], halo_recv.at[1],
        {**here_dp, "tm": later, "tile": zl},
    )
    halo_corner = remote(
        act.at[0, 6:8, out_row], xp.at[0:2, into_row], halo_send.at[2], halo_recv.at[2],
        {**here_dp, "tm": later, "tile": other},
    )
    halo_rows.start()

    @pl.when(x < 3)
    def _():
        halo_frames.start()
        halo_corner.start()

    for load in loads:
        load.wait()
    remote(
        act.at[0, :, out_row], xp.at[2:10, recv_row], halo_send.at[0], halo_recv.at[0],
        {**here_dp, "tm": x, "tile": other},
    ).wait_recv()

    outs = []
    for i, t in enumerate((2, 3, 4, 5, 6, 7, 0, 1)):
        if t == 0:

            @pl.when(x > 0)
            def _():
                remote(
                    act.at[0, 6:8], xp.at[0:2, 1:9], halo_send.at[1], halo_recv.at[1],
                    {**here_dp, "tm": x - 1, "tile": zl},
                ).wait_recv()
                remote(
                    act.at[0, 6:8, out_row], xp.at[0:2, recv_row], halo_send.at[2], halo_recv.at[2],
                    {**here_dp, "tm": x - 1, "tile": other},
                ).wait_recv()

        forward_frame(t, xp, wf, bias, ctv, bov, gp, gt, bsum, i == 0)
    outs.append(pltpu.make_async_copy(bov, block_out.at[0], out_sem.at[0]))
    outs[-1].start()

    row_own = 1 + out_row
    earlier = jnp.maximum(x - 1, 0)
    ghalo_rows = remote(
        gp.at[0:8, row_own], gp.at[0:8, into_row], ghalo_send.at[0], ghalo_recv.at[0],
        {**here_dp, "tm": x, "tile": other},
    )
    ghalo_frames = remote(
        gp.at[0:2, 1:9], gp.at[8:10, 1:9], ghalo_send.at[1], ghalo_recv.at[1],
        {**here_dp, "tm": earlier, "tile": zl},
    )
    ghalo_corner = remote(
        gp.at[0:2, row_own], gp.at[8:10, into_row], ghalo_send.at[2], ghalo_recv.at[2],
        {**here_dp, "tm": earlier, "tile": other},
    )
    ghalo_rows.start()

    @pl.when(x > 0)
    def _():
        ghalo_frames.start()
        ghalo_corner.start()

    total_bias = jnp.sum(bsum[...], axis=0, keepdims=True)
    bias_hi = total_bias.astype(BF).astype(F32)
    bias_lo = total_bias - bias_hi
    row = lax.broadcasted_iota(jnp.int32, (BLOCK, C), 0)
    tail = jnp.where(row == SHARD, bias_hi, jnp.where(row == SHARD + 1, bias_lo, 0.0))

    def pack(i):
        q, y_, core_ = i // 8, (i // 2) % 4, i % 2
        rows = dw[SHARD * i : SHARD * i + BLOCK]
        pk[q, core_, y_] = jnp.where(row < SHARD, rows, tail).astype(BF)

    def core_copy(q):
        return remote(
            pk.at[q, 1 - core], cr.at[q], core_send.at[q], core_recv.at[q],
            {"dp": dp_at(zh, y, 1 - core), "tm": x, "tile": zl},
        )

    def y_copy(q, k):
        return remote(
            ys.at[q, k - 1], yr.at[q, k - 1], y_send.at[q, k - 1], y_recv.at[q, k - 1],
            {"dp": dp_at(zh, lax.rem(y + k, 4), core), "tm": x, "tile": zl},
        )

    def y_stage(q):
        core_copy(q).wait_recv()
        for k in range(1, 4):
            to = lax.rem(y + k, 4)
            ys[q, k - 1] = (pk[q, core, to].astype(F32) + cr[q, to].astype(F32)).astype(BF)
            y_copy(q, k).start()
        yown[q] = pk[q, core, y].astype(F32) + cr[q, y].astype(F32)

    def z_copy(q):
        slot = lax.rem(q - zh + 3, 4)
        return remote(
            zs.at[q], zr.at[slot], z_send.at[q], z_recv.at[slot],
            {"dp": dp_at(q, y, core), "tm": x, "tile": zl},
        )

    def z_stage(q):
        total = yown[q]
        for k in range(1, 4):
            y_copy(q, k).wait_recv()
            total = total + yr[q, k - 1].astype(F32)

        @pl.when(zh == q)
        def _():
            zown[...] = total

        @pl.when(zh != q)
        def _():
            zs[q] = total.astype(BF)
            z_copy(q).start()

    packed, sent = 0, 0
    for d in range(5):
        weight_taps(d, xp, gt, dw)
        ready = min(9, 2 * d + 2) * 3 * C
        while packed < 32 and SHARD * (packed + 1) <= ready:
            pack(packed)
            packed += 1
        while sent < 4 and packed >= 8 * (sent + 1):
            core_copy(sent).start()
            sent += 1
        if d >= 2:
            y_stage(d - 2)

    for load in late:
        load.wait()
    remote(
        gp.at[0:8, row_own], gp.at[0:8, recv_row], ghalo_send.at[0], ghalo_recv.at[0],
        {**here_dp, "tm": x, "tile": other},
    ).wait_recv()
    backward_frames(0, 2, gp, wt, ctv, giv)
    y_stage(3)
    z_stage(0)
    backward_frames(2, 2, gp, wt, ctv, giv)
    z_stage(1)
    backward_frames(4, 2, gp, wt, ctv, giv)
    z_stage(2)

    @pl.when(x < 3)
    def _():
        remote(
            gp.at[0:2, 1:9], gp.at[8:10, 1:9], ghalo_send.at[1], ghalo_recv.at[1],
            {**here_dp, "tm": x + 1, "tile": zl},
        ).wait_recv()
        remote(
            gp.at[0:2, row_own], gp.at[8:10, recv_row], ghalo_send.at[2], ghalo_recv.at[2],
            {**here_dp, "tm": x + 1, "tile": other},
        ).wait_recv()

    backward_frames(6, 2, gp, wt, ctv, giv)
    outs.append(pltpu.make_async_copy(giv, grad_input.at[0], out_sem.at[1]))
    outs[-1].start()
    z_stage(3)

    total = zown[...]
    for slot in range(3):
        remote(
            zs.at[0], zr.at[slot], z_send.at[0], z_recv.at[slot],
            {"dp": dp_at(lax.rem(zh + 1, 4), y, core), "tm": x, "tile": zl},
        ).wait_recv()
        total = total + zr[slot].astype(F32)
    fr[group] = total.astype(BF)

    def f_copy(k, slot):
        to = lax.rem(group + k, 8)
        return remote(
            fr.at[group], fr.at[slot], f_send.at[k - 1], f_recv.at[slot],
            {**here_dp, "tm": to // 2, "tile": lax.rem(to, 2)},
        )

    for k in range(1, 8):
        f_copy(k, group).start()
    for k in range(1, 8):
        f_copy(k, lax.rem(group + k, 8)).wait_recv()
    total = fr[0].astype(F32)
    for g in range(1, 8):
        total = total + fr[g].astype(F32)
    weight_grad[...] = total[:SHARD] * SCALE
    whole_bias = (total[SHARD : SHARD + 1] + total[SHARD + 1 : SHARD + 2]) * SCALE
    whole_bias = jnp.broadcast_to(whole_bias, (8, C))
    bias_grad[...] = pltpu.roll(whole_bias, lax.rem(C - 4 * dp, C), 1)

    halo_rows.wait_send()
    ghalo_rows.wait_send()

    @pl.when(x < 3)
    def _():
        halo_frames.wait_send()
        halo_corner.wait_send()

    @pl.when(x > 0)
    def _():
        ghalo_frames.wait_send()
        ghalo_corner.wait_send()

    for q in range(4):
        core_copy(q).wait_send()
        for k in range(1, 4):
            y_copy(q, k).wait_send()

        @pl.when(zh != q)
        def _():
            z_copy(q).wait_send()

    for k in range(1, 8):
        f_copy(k, group).wait_send()
    for out in outs:
        out.wait()


def body(activations, weights, conv_bias, cotangent):
    hbm = pl.BlockSpec(memory_space=pl.ANY)
    vmem = pl.BlockSpec(memory_space=pltpu.VMEM)
    dma = pltpu.SemaphoreType.DMA
    shape = (1, FRAMES, ROWS, COLS, C)
    block_out, grad_input, weight_grad, bias_grad = pl.pallas_call(
        kernel,
        out_shape=[
            jax.ShapeDtypeStruct(shape, BF),
            jax.ShapeDtypeStruct(shape, BF),
            jax.ShapeDtypeStruct((SHARD, C), F32),
            jax.ShapeDtypeStruct((8, C), F32),
        ],
        in_specs=[hbm, hbm, vmem, hbm],
        out_specs=[hbm, hbm, vmem, vmem],
        scratch_shapes=[
            pltpu.VMEM((10, 10, COLS, C), BF),
            pltpu.VMEM((10, 10, COLS, C), BF),
            pltpu.VMEM((9, C, 3 * C), BF),
            pltpu.VMEM((3, C, 9 * C), BF),
            pltpu.VMEM((FRAMES, ROWS, COLS, C), BF),
            pltpu.VMEM((FRAMES, ROWS, COLS, C), BF),
            pltpu.VMEM((FRAMES, ROWS, COLS, C), BF),
            pltpu.VMEM((3 * C, POSITIONS), BF),
            pltpu.VMEM((27 * C + 8, C), F32),
            pltpu.VMEM((8, C), F32),
            pltpu.VMEM((4, 2, 4, BLOCK, C), BF),
            pltpu.VMEM((4, 4, BLOCK, C), BF),
            pltpu.VMEM((4, 3, BLOCK, C), BF),
            pltpu.VMEM((4, 3, BLOCK, C), BF),
            pltpu.VMEM((4, BLOCK, C), F32),
            pltpu.VMEM((4, BLOCK, C), BF),
            pltpu.VMEM((3, BLOCK, C), BF),
            pltpu.VMEM((BLOCK, C), F32),
            pltpu.VMEM((8, BLOCK, C), BF),
            dma((14,)),
            dma((2,)),
            dma((3,)),
            dma((3,)),
            dma((3,)),
            dma((3,)),
            dma((4,)),
            dma((4,)),
            dma((4, 3)),
            dma((4, 3)),
            dma((4,)),
            dma((3,)),
            dma((7,)),
            dma((8,)),
        ],
        compiler_params=pltpu.CompilerParams(
            collective_id=0, has_side_effects=True, vmem_limit_bytes=48 * 2**20
        ),
    )(activations, weights.reshape(9, 3, C, C), conv_bias.reshape(1, C), cotangent)
    return block_out, grad_input, weight_grad, bias_grad[0, :4]


def solution(mesh):
    return jax.shard_map(
        body,
        mesh=mesh,
        in_specs=(P("dp", "tm", "tile", None, None), P(), P(), P("dp", "tm", "tile", None, None)),
        out_specs=(
            P("dp", "tm", "tile", None, None),
            P("dp", "tm", "tile", None, None),
            P("dp", None),
            P("dp"),
        ),
        check_vma=False,
    )
```

```python
import math

import jax
import jax.numpy as jnp
from jax import lax
from jax.experimental import pallas as pl
from jax.experimental.pallas import tpu as pltpu
from jax.sharding import PartitionSpec as P

F32 = jnp.float32
BF = jnp.bfloat16
MESH = pl.DeviceIdType.MESH

C = 128
FRAMES, ROWS, COLS = 8, 8, 32
AREA = ROWS * COLS
POSITIONS = FRAMES * AREA
TAPS_AB = [(a, b) for a in range(3) for b in range(3)]
SHARD = 108
BLOCK = 112
SCALE = 1.0 / math.sqrt(524288.0)


def shift_columns(values, by):
    rows = values.shape[0]
    rolled = pltpu.roll(values, by % rows, 0)
    column = lax.broadcasted_iota(jnp.int32, values.shape, 0) & (COLS - 1)
    return jnp.where(column == (0 if by == 1 else COLS - 1), 0.0, rolled)


def forward_frame(t, xp, wf, bias, ctv, bov, gp, gt, bsum, first):
    lhs = jnp.concatenate(
        [xp[t + a, b : b + ROWS].reshape(AREA, C) for a, b in TAPS_AB], axis=1
    )
    y = jnp.dot(lhs, wf[...].reshape(9 * C, 3 * C), preferred_element_type=F32)
    pre = y[:, C : 2 * C] + shift_columns(y[:, :C], 1) + shift_columns(y[:, 2 * C :], -1)
    pre = pre + bias[...]
    sig = 0.5 * jnp.tanh(0.5 * pre) + 0.5
    center = xp[t + 2, 1 : 1 + ROWS].reshape(AREA, C).astype(F32)
    bov[t] = (center + pre * sig).astype(BF).reshape(ROWS, COLS, C)
    grad = ctv[t].reshape(AREA, C).astype(F32) * (sig * (1.0 + pre * (1.0 - sig)))
    grad = grad.astype(BF)
    gp[t, 1 : 1 + ROWS] = grad.reshape(ROWS, COLS, C)
    grad = grad.astype(F32)
    part = jnp.sum(grad.reshape(AREA // 8, 8, C), axis=0)
    if first:
        bsum[...] = part
    else:
        bsum[...] += part
    turned = jnp.transpose(grad)
    lane = lax.broadcasted_iota(jnp.int32, (C, C), 1) & (COLS - 1)
    start = t * AREA
    gt[C : 2 * C, start : start + AREA] = turned.astype(BF)
    for half in range(2):
        piece = turned[:, half * C : half * C + C]
        at = start + half * C
        ahead = jnp.where(lane == COLS - 1, 0.0, pltpu.roll(piece, C - 1, 1))
        behind = jnp.where(lane == 0, 0.0, pltpu.roll(piece, 1, 1))
        gt[0:C, at : at + C] = ahead.astype(BF)
        gt[2 * C : 3 * C, at : at + C] = behind.astype(BF)


def weight_taps(d, xp, gt, dw):
    pairs = TAPS_AB[2 * d : 2 * d + 2]
    rhs = jnp.concatenate(
        [xp[a : a + FRAMES, b : b + ROWS].reshape(POSITIONS, C) for a, b in pairs], axis=1
    )
    out = jnp.dot(gt[...], rhs, preferred_element_type=F32)
    for j in range(len(pairs)):
        for e in range(3):
            tap = (2 * d + j) * 3 + e
            dw[tap * C : tap * C + C] = jnp.transpose(
                out[e * C : e * C + C, j * C : j * C + C]
            )


def backward_frames(t, n, gp, wt, ctv, giv):
    rows = n * AREA
    lhs = jnp.concatenate(
        [gp[t + 2 - a : t + 2 - a + n, 2 - b : 2 - b + ROWS].reshape(rows, C) for a, b in TAPS_AB],
        axis=1,
    )
    y = lax.dot_general(
        lhs,
        wt[...].reshape(3 * C, 9 * C),
        (((1,), (1,)), ((), ())),
        preferred_element_type=F32,
    )
    out = y[:, C : 2 * C] + shift_columns(y[:, :C], -1) + shift_columns(y[:, 2 * C :], 1)
    out = out + ctv[t : t + n].reshape(rows, C).astype(F32)
    giv[t : t + n] = out.astype(BF).reshape(n, ROWS, COLS, C)


def kernel(
    act, ker, bias, cot, block_out, grad_input, weight_grad, bias_grad,
    xp, gp, wf, wt, ctv, bov, giv, gt, dw, bsum,
    pk, cr, ys, yr, yown, zs, zr, zown, fr,
    load_sem, out_sem, halo_send, halo_recv, ghalo_send, ghalo_recv,
    core_send, core_recv, y_send, y_recv, z_send, z_recv, f_send, f_recv,
):
    dp = lax.axis_index("dp")
    x = lax.axis_index("tm")
    zl = lax.axis_index("tile")
    core = lax.rem(dp, 2)
    y = lax.rem(dp // 2, 4)
    zh = dp // 8
    other = 1 - zl

    def dp_at(zh_, y_, core_):
        return (zh_ * 4 + y_) * 2 + core_

    loads = [pltpu.make_async_copy(act.at[0], xp.at[2:10, 1:9], load_sem.at[0])]
    for e in range(3):
        loads.append(
            pltpu.make_async_copy(
                ker.at[:, e], wf.at[:, :, e * C : e * C + C], load_sem.at[1 + e]
            )
        )
    loads.append(pltpu.make_async_copy(cot.at[0], ctv, load_sem.at[4]))
    for load in loads:
        load.start()
    late = [
        pltpu.make_async_copy(ker.at[i], wt.at[:, :, i * C : i * C + C], load_sem.at[5 + i])
        for i in range(9)
    ]
    for load in late:
        load.start()

    barrier = pltpu.get_barrier_semaphore()
    group = x * 2 + zl
    for k in range(1, 8):
        to = lax.rem(group + k, 8)
        pl.semaphore_signal(
            barrier, inc=1,
            device_id={"dp": dp, "tm": to // 2, "tile": lax.rem(to, 2)},
            device_id_type=MESH,
        )
    pl.semaphore_signal(
        barrier, inc=1,
        device_id={"dp": dp_at(zh, y, 1 - core), "tm": x, "tile": zl}, device_id_type=MESH,
    )
    for k in range(1, 4):
        pl.semaphore_signal(
            barrier, inc=1,
            device_id={"dp": dp_at(zh, lax.rem(y + k, 4), core), "tm": x, "tile": zl},
            device_id_type=MESH,
        )
        pl.semaphore_signal(
            barrier, inc=1,
            device_id={"dp": dp_at(lax.rem(zh + k, 4), y, core), "tm": x, "tile": zl},
            device_id_type=MESH,
        )

    edge = 9 * zl
    row_zeros = jnp.zeros((10, COLS, C), BF)
    xp[:, edge] = row_zeros
    gp[:, edge] = row_zeros

    @pl.when(x == 0)
    def _():
        xp[0:2] = jnp.zeros((2, 10, COLS, C), BF)

    @pl.when(x == 3)
    def _():
        gp[8:10] = jnp.zeros((2, 10, COLS, C), BF)

    pl.semaphore_wait(barrier, 14)

    out_row = 7 * other
    into_row = 9 * zl
    recv_row = 9 * other

    def remote(src, dst, send, recv, where):
        return pltpu.make_async_remote_copy(
            src_ref=src, dst_ref=dst, send_sem=send, recv_sem=recv,
            device_id=where, device_id_type=MESH,
        )

    here_dp = {"dp": dp}
    halo_rows = remote(
        act.at[0, :, out_row], xp.at[2:10, into_row], halo_send.at[0], halo_recv.at[0],
        {**here_dp, "tm": x, "tile": other},
    )
    later = jnp.minimum(x + 1, 3)
    halo_frames = remote(
        act.at[0, 6:8], xp.at[0:2, 1:9], halo_send.at[1], halo_recv.at[1],
        {**here_dp, "tm": later, "tile": zl},
    )
    halo_corner = remote(
        act.at[0, 6:8, out_row], xp.at[0:2, into_row], halo_send.at[2], halo_recv.at[2],
        {**here_dp, "tm": later, "tile": other},
    )
    halo_rows.start()

    @pl.when(x < 3)
    def _():
        halo_frames.start()
        halo_corner.start()

    for load in loads:
        load.wait()
    remote(
        act.at[0, :, out_row], xp.at[2:10, recv_row], halo_send.at[0], halo_recv.at[0],
        {**here_dp, "tm": x, "tile": other},
    ).wait_recv()

    outs = []
    for i, t in enumerate((2, 3, 4, 5, 6, 7, 0, 1)):
        if t == 0:

            @pl.when(x > 0)
            def _():
                remote(
                    act.at[0, 6:8], xp.at[0:2, 1:9], halo_send.at[1], halo_recv.at[1],
                    {**here_dp, "tm": x - 1, "tile": zl},
                ).wait_recv()
                remote(
                    act.at[0, 6:8, out_row], xp.at[0:2, recv_row], halo_send.at[2], halo_recv.at[2],
                    {**here_dp, "tm": x - 1, "tile": other},
                ).wait_recv()

        forward_frame(t, xp, wf, bias, ctv, bov, gp, gt, bsum, i == 0)
    outs.append(pltpu.make_async_copy(bov, block_out.at[0], out_sem.at[0]))
    outs[-1].start()

    row_own = 1 + out_row
    earlier = jnp.maximum(x - 1, 0)
    ghalo_rows = remote(
        gp.at[0:8, row_own], gp.at[0:8, into_row], ghalo_send.at[0], ghalo_recv.at[0],
        {**here_dp, "tm": x, "tile": other},
    )
    ghalo_frames = remote(
        gp.at[0:2, 1:9], gp.at[8:10, 1:9], ghalo_send.at[1], ghalo_recv.at[1],
        {**here_dp, "tm": earlier, "tile": zl},
    )
    ghalo_corner = remote(
        gp.at[0:2, row_own], gp.at[8:10, into_row], ghalo_send.at[2], ghalo_recv.at[2],
        {**here_dp, "tm": earlier, "tile": other},
    )
    ghalo_rows.start()

    @pl.when(x > 0)
    def _():
        ghalo_frames.start()
        ghalo_corner.start()

    total_bias = jnp.sum(bsum[...], axis=0, keepdims=True)
    bias_hi = total_bias.astype(BF).astype(F32)
    bias_lo = total_bias - bias_hi
    row = lax.broadcasted_iota(jnp.int32, (BLOCK, C), 0)
    tail = jnp.where(row == SHARD, bias_hi, jnp.where(row == SHARD + 1, bias_lo, 0.0))

    def pack(i):
        q, y_, core_ = i // 8, (i // 2) % 4, i % 2
        rows = dw[SHARD * i : SHARD * i + BLOCK]
        pk[q, core_, y_] = jnp.where(row < SHARD, rows, tail).astype(BF)

    def core_copy(q):
        return remote(
            pk.at[q, 1 - core], cr.at[q], core_send.at[q], core_recv.at[q],
            {"dp": dp_at(zh, y, 1 - core), "tm": x, "tile": zl},
        )

    def y_copy(q, k):
        return remote(
            ys.at[q, k - 1], yr.at[q, k - 1], y_send.at[q, k - 1], y_recv.at[q, k - 1],
            {"dp": dp_at(zh, lax.rem(y + k, 4), core), "tm": x, "tile": zl},
        )

    def y_stage(q):
        core_copy(q).wait_recv()
        for k in range(1, 4):
            to = lax.rem(y + k, 4)
            ys[q, k - 1] = (pk[q, core, to].astype(F32) + cr[q, to].astype(F32)).astype(BF)
            y_copy(q, k).start()
        yown[q] = pk[q, core, y].astype(F32) + cr[q, y].astype(F32)

    def z_copy(q):
        slot = lax.rem(q - zh + 3, 4)
        return remote(
            zs.at[q], zr.at[slot], z_send.at[q], z_recv.at[slot],
            {"dp": dp_at(q, y, core), "tm": x, "tile": zl},
        )

    def z_stage(q):
        total = yown[q]
        for k in range(1, 4):
            y_copy(q, k).wait_recv()
            total = total + yr[q, k - 1].astype(F32)

        @pl.when(zh == q)
        def _():
            zown[...] = total

        @pl.when(zh != q)
        def _():
            zs[q] = total.astype(BF)
            z_copy(q).start()

    packed, sent = 0, 0
    for d in range(5):
        weight_taps(d, xp, gt, dw)
        ready = min(9, 2 * d + 2) * 3 * C
        while packed < 32 and SHARD * (packed + 1) <= ready:
            pack(packed)
            packed += 1
        while sent < 4 and packed >= 8 * (sent + 1):
            core_copy(sent).start()
            sent += 1
        if d >= 2:
            y_stage(d - 2)

    for load in late:
        load.wait()
    remote(
        gp.at[0:8, row_own], gp.at[0:8, recv_row], ghalo_send.at[0], ghalo_recv.at[0],
        {**here_dp, "tm": x, "tile": other},
    ).wait_recv()
    backward_frames(0, 2, gp, wt, ctv, giv)
    y_stage(3)
    z_stage(0)
    backward_frames(2, 2, gp, wt, ctv, giv)
    z_stage(1)
    backward_frames(4, 2, gp, wt, ctv, giv)
    z_stage(2)

    @pl.when(x < 3)
    def _():
        remote(
            gp.at[0:2, 1:9], gp.at[8:10, 1:9], ghalo_send.at[1], ghalo_recv.at[1],
            {**here_dp, "tm": x + 1, "tile": zl},
        ).wait_recv()
        remote(
            gp.at[0:2, row_own], gp.at[8:10, recv_row], ghalo_send.at[2], ghalo_recv.at[2],
            {**here_dp, "tm": x + 1, "tile": other},
        ).wait_recv()

    backward_frames(6, 2, gp, wt, ctv, giv)
    outs.append(pltpu.make_async_copy(giv, grad_input.at[0], out_sem.at[1]))
    outs[-1].start()
    z_stage(3)

    total = zown[...]
    for slot in range(3):
        remote(
            zs.at[0], zr.at[slot], z_send.at[0], z_recv.at[slot],
            {"dp": dp_at(lax.rem(zh + 1, 4), y, core), "tm": x, "tile": zl},
        ).wait_recv()
        total = total + zr[slot].astype(F32)
    fr[group] = total.astype(BF)

    def f_copy(k, slot):
        to = lax.rem(group + k, 8)
        return remote(
            fr.at[group], fr.at[slot], f_send.at[k - 1], f_recv.at[slot],
            {**here_dp, "tm": to // 2, "tile": lax.rem(to, 2)},
        )

    for k in range(1, 8):
        f_copy(k, group).start()
    for k in range(1, 8):
        f_copy(k, lax.rem(group + k, 8)).wait_recv()
    total = fr[0].astype(F32)
    for g in range(1, 8):
        total = total + fr[g].astype(F32)
    weight_grad[...] = total[:SHARD] * SCALE
    whole_bias = (total[SHARD : SHARD + 1] + total[SHARD + 1 : SHARD + 2]) * SCALE
    whole_bias = jnp.broadcast_to(whole_bias, (8, C))
    bias_grad[...] = pltpu.roll(whole_bias, lax.rem(C - 4 * dp, C), 1)[0:1]

    halo_rows.wait_send()
    ghalo_rows.wait_send()

    @pl.when(x < 3)
    def _():
        halo_frames.wait_send()
        halo_corner.wait_send()

    @pl.when(x > 0)
    def _():
        ghalo_frames.wait_send()
        ghalo_corner.wait_send()

    for q in range(4):
        core_copy(q).wait_send()
        for k in range(1, 4):
            y_copy(q, k).wait_send()

        @pl.when(zh != q)
        def _():
            z_copy(q).wait_send()

    for k in range(1, 8):
        f_copy(k, group).wait_send()
    for out in outs:
        out.wait()


def hand_over(*refs):
    sem = refs[8]
    copies = [pltpu.make_async_copy(refs[i], refs[4 + i], sem.at[i]) for i in range(3)]
    refs[7][...] = refs[3][0, 0:4]
    for copy in copies:
        copy.start()
    for copy in copies:
        copy.wait()


def body(activations, weights, conv_bias, cotangent):
    hbm = pl.BlockSpec(memory_space=pltpu.HBM)
    anywhere = pl.BlockSpec(memory_space=pl.ANY)
    vmem = pl.BlockSpec(memory_space=pltpu.VMEM)
    dma = pltpu.SemaphoreType.DMA
    shape = (1, FRAMES, ROWS, COLS, C)
    results = pl.pallas_call(
        kernel,
        out_shape=[
            jax.ShapeDtypeStruct(shape, BF),
            jax.ShapeDtypeStruct(shape, BF),
            jax.ShapeDtypeStruct((SHARD, C), F32),
            jax.ShapeDtypeStruct((1, C), F32),
        ],
        in_specs=[hbm, hbm, vmem, hbm],
        out_specs=[anywhere, anywhere, vmem, vmem],
        scratch_shapes=[
            pltpu.VMEM((10, 10, COLS, C), BF),
            pltpu.VMEM((10, 10, COLS, C), BF),
            pltpu.VMEM((9, C, 3 * C), BF),
            pltpu.VMEM((3, C, 9 * C), BF),
            pltpu.VMEM((FRAMES, ROWS, COLS, C), BF),
            pltpu.VMEM((FRAMES, ROWS, COLS, C), BF),
            pltpu.VMEM((FRAMES, ROWS, COLS, C), BF),
            pltpu.VMEM((3 * C, POSITIONS), BF),
            pltpu.VMEM((27 * C + 8, C), F32),
            pltpu.VMEM((8, C), F32),
            pltpu.VMEM((4, 2, 4, BLOCK, C), BF),
            pltpu.VMEM((4, 4, BLOCK, C), BF),
            pltpu.VMEM((4, 3, BLOCK, C), BF),
            pltpu.VMEM((4, 3, BLOCK, C), BF),
            pltpu.VMEM((4, BLOCK, C), F32),
            pltpu.VMEM((4, BLOCK, C), BF),
            pltpu.VMEM((3, BLOCK, C), BF),
            pltpu.VMEM((BLOCK, C), F32),
            pltpu.VMEM((8, BLOCK, C), BF),
            dma((14,)),
            dma((2,)),
            dma((3,)),
            dma((3,)),
            dma((3,)),
            dma((3,)),
            dma((4,)),
            dma((4,)),
            dma((4, 3)),
            dma((4, 3)),
            dma((4,)),
            dma((3,)),
            dma((7,)),
            dma((8,)),
        ],
        compiler_params=pltpu.CompilerParams(
            collective_id=0, has_side_effects=True, vmem_limit_bytes=63 * 2**20+512*1024
        ),
    )(activations, weights.reshape(9, 3, C, C), conv_bias.reshape(1, C), cotangent)
    block_out, grad_input, weight_grad, bias_grad = pl.pallas_call(
        hand_over,
        out_shape=[
            jax.ShapeDtypeStruct(shape, BF),
            jax.ShapeDtypeStruct(shape, BF),
            jax.ShapeDtypeStruct((SHARD, C), F32),
            jax.ShapeDtypeStruct((4,), F32),
        ],
        in_specs=[anywhere, anywhere, anywhere, vmem],
        out_specs=[hbm, hbm, hbm, vmem],
        scratch_shapes=[dma((3,))],
        compiler_params=pltpu.CompilerParams(vmem_limit_bytes=63 * 2**20 + 512 * 1024),
    )(*results)
    return block_out, grad_input, weight_grad, bias_grad


def solution(mesh):
    return jax.shard_map(
        body,
        mesh=mesh,
        in_specs=(P("dp", "tm", "tile", None, None), P(), P(), P("dp", "tm", "tile", None, None)),
        out_specs=(
            P("dp", "tm", "tile", None, None),
            P("dp", "tm", "tile", None, None),
            P("dp", None),
            P("dp"),
        ),
        check_vma=False,
    )
```

```python
import math

import jax
import jax.numpy as jnp
from jax import lax
from jax.experimental import pallas as pl
from jax.experimental.pallas import tpu as pltpu
from jax.sharding import PartitionSpec as P

F32 = jnp.float32
BF = jnp.bfloat16
MESH = pl.DeviceIdType.MESH

C = 128
FRAMES, ROWS, COLS = 8, 8, 32
AREA = ROWS * COLS
POSITIONS = FRAMES * AREA
TAPS_AB = [(a, b) for a in range(3) for b in range(3)]
SHARD = 108
BLOCK = 112
EARLY = 3 * AREA
SCALE = 1.0 / math.sqrt(524288.0)


def shift_columns(values, by):
    rows = values.shape[0]
    rolled = pltpu.roll(values, by % rows, 0)
    column = lax.broadcasted_iota(jnp.int32, values.shape, 0) & (COLS - 1)
    return jnp.where(column == (0 if by == 1 else COLS - 1), 0.0, rolled)


def forward_block(lhs, center, upstream, wf, bias):
    y = jnp.dot(lhs, wf[...].reshape(9 * C, 3 * C), preferred_element_type=F32)
    pre = y[:, C : 2 * C] + shift_columns(y[:, :C], 1) + shift_columns(y[:, 2 * C :], -1)
    pre = pre + bias[...]
    sig = 0.5 * jnp.tanh(0.5 * pre) + 0.5
    out = (center.astype(F32) + pre * sig).astype(BF)
    grad = upstream.astype(F32) * (sig * (1.0 + pre * (1.0 - sig)))
    return out, grad.astype(BF)


def keep_turned(grad, start, gt, bsum, first):
    part = jnp.sum(grad.reshape(AREA // 8, 8, C), axis=0)
    if first:
        bsum[...] = part
    else:
        bsum[...] += part
    turned = jnp.transpose(grad)
    lane = lax.broadcasted_iota(jnp.int32, (C, C), 1) & (COLS - 1)
    gt[C : 2 * C, start : start + AREA] = turned.astype(BF)
    for half in range(2):
        piece = turned[:, half * C : half * C + C]
        at = start + half * C
        ahead = jnp.where(lane == COLS - 1, 0.0, pltpu.roll(piece, C - 1, 1))
        behind = jnp.where(lane == 0, 0.0, pltpu.roll(piece, 1, 1))
        gt[0:C, at : at + C] = ahead.astype(BF)
        gt[2 * C : 3 * C, at : at + C] = behind.astype(BF)


def forward_frame(t, xp, wf, bias, ctv, bov, gp, gt, bsum, row, first):
    lhs = jnp.concatenate(
        [xp[t + a, b : b + ROWS].reshape(AREA, C) for a, b in TAPS_AB], axis=1
    )
    out, grad = forward_block(
        lhs, xp[t + 2, 1 : 1 + ROWS].reshape(AREA, C), ctv[t].reshape(AREA, C), wf, bias
    )
    bov[t] = out.reshape(ROWS, COLS, C)
    gp[t, 1 : 1 + ROWS] = grad.reshape(ROWS, COLS, C)
    at_row = lax.broadcasted_iota(jnp.int32, (AREA, C), 0) // COLS
    start = t * AREA if t < 2 else EARLY + (t - 2) * AREA
    keep_turned(jnp.where(at_row == row, 0.0, grad.astype(F32)), start, gt, bsum, first)


def forward_seam(xp, wf, bias, ctv, bov, gp, gt, bsum, row):
    lhs = jnp.concatenate(
        [xp[a : a + FRAMES, row + b].reshape(AREA, C) for a, b in TAPS_AB], axis=1
    )
    out, grad = forward_block(
        lhs, xp[2 : 2 + FRAMES, row + 1].reshape(AREA, C), ctv[:, row].reshape(AREA, C), wf, bias
    )
    bov[:, row] = out.reshape(FRAMES, COLS, C)
    gp[0:FRAMES, row + 1] = grad.reshape(FRAMES, COLS, C)
    keep_turned(grad.astype(F32), 2 * AREA, gt, bsum, False)


def early_taps(d, xp, gt, wacc):
    pairs = TAPS_AB[2 * d : 2 * d + 2]
    rhs = jnp.concatenate(
        [xp[a + 2 : a + FRAMES, b : b + ROWS].reshape(6 * AREA, C) for a, b in pairs], axis=1
    )
    lhs = gt[:, EARLY : EARLY + 6 * AREA]
    wacc[:, 2 * C * d : 2 * C * d + len(pairs) * C] = jnp.dot(
        lhs, rhs, preferred_element_type=F32
    )


def late_taps(d, xp, gt, wacc, dw, row):
    pairs = TAPS_AB[2 * d : 2 * d + 2]
    rhs = jnp.concatenate(
        [
            jnp.concatenate(
                [
                    xp[a : a + 2, b : b + ROWS].reshape(2 * AREA, C),
                    xp[a : a + FRAMES, row + b].reshape(AREA, C),
                ],
                axis=0,
            )
            for a, b in pairs
        ],
        axis=1,
    )
    out = jnp.dot(gt[:, :EARLY], rhs, preferred_element_type=F32)
    out = out + wacc[:, 2 * C * d : 2 * C * d + len(pairs) * C]
    for j in range(len(pairs)):
        for e in range(3):
            tap = (2 * d + j) * 3 + e
            dw[tap * C : tap * C + C] = jnp.transpose(
                out[e * C : e * C + C, j * C : j * C + C]
            )


def backward_frames(t, n, gp, wt, ctv, giv):
    rows = n * AREA
    lhs = jnp.concatenate(
        [gp[t + 2 - a : t + 2 - a + n, 2 - b : 2 - b + ROWS].reshape(rows, C) for a, b in TAPS_AB],
        axis=1,
    )
    y = lax.dot_general(
        lhs,
        wt[...].reshape(3 * C, 9 * C),
        (((1,), (1,)), ((), ())),
        preferred_element_type=F32,
    )
    out = y[:, C : 2 * C] + shift_columns(y[:, :C], -1) + shift_columns(y[:, 2 * C :], 1)
    out = out + ctv[t : t + n].reshape(rows, C).astype(F32)
    giv[t : t + n] = out.astype(BF).reshape(n, ROWS, COLS, C)


def kernel(
    act, ker, bias, cot, block_out, grad_input, weight_grad, bias_grad,
    xp, gp, wf, wt, ctv, bov, giv, gt, wacc, dw, bsum, hrow, hframes, hcorner,
    pk, cr, ys, yr, yown, zs, zr, zown, fr,
    load_sem, out_sem, halo_send, halo_recv, ghalo_send, ghalo_recv,
    core_send, core_recv, y_send, y_recv, z_send, z_recv, f_send, f_recv,
):
    dp = lax.axis_index("dp")
    x = lax.axis_index("tm")
    zl = lax.axis_index("tile")
    core = lax.rem(dp, 2)
    y = lax.rem(dp // 2, 4)
    zh = dp // 8
    other = 1 - zl

    def at(zh_=None, y_=None, core_=None, x_=None, zl_=None):
        zh_ = zh if zh_ is None else zh_
        y_ = y if y_ is None else y_
        core_ = core if core_ is None else core_
        return {
            "dp": (zh_ * 4 + y_) * 2 + core_,
            "tm": x if x_ is None else x_,
            "tile": zl if zl_ is None else zl_,
        }

    def remote(src, dst, send, recv, where):
        return pltpu.make_async_remote_copy(
            src_ref=src, dst_ref=dst, send_sem=send, recv_sem=recv,
            device_id=where, device_id_type=MESH,
        )

    barrier = pltpu.get_barrier_semaphore()
    group = x * 2 + zl

    def in_group(k):
        to = lax.rem(group + k, 8)
        return at(x_=to // 2, zl_=lax.rem(to, 2))

    partners = [at(zh_=lax.rem(zh + k, 4)) for k in (2, 1, 3)]
    partners += [in_group(k) for k in (4, 5, 3, 2, 6, 1, 7)]
    partners += [at(y_=lax.rem(y + k, 4)) for k in (2, 1, 3)]
    partners += [at(core_=1 - core)]
    for partner in partners:
        pl.semaphore_signal(barrier, inc=1, device_id=partner, device_id_type=MESH)

    loads = [pltpu.make_async_copy(act.at[0], xp.at[2:10, 1:9], load_sem.at[0])]
    for e in range(3):
        loads.append(
            pltpu.make_async_copy(
                ker.at[:, e], wf.at[:, :, e * C : e * C + C], load_sem.at[1 + e]
            )
        )
    loads.append(pltpu.make_async_copy(cot.at[0], ctv, load_sem.at[4]))
    late = [
        pltpu.make_async_copy(ker.at[i], wt.at[:, :, i * C : i * C + C], load_sem.at[5 + i])
        for i in range(9)
    ]
    for load in loads + late:
        load.start()

    row_zeros = jnp.zeros((10, COLS, C), BF)
    xp[:, 0] = row_zeros
    xp[:, 9] = row_zeros
    gp[:, 9 * zl] = row_zeros
    xp[0:2, 1:9] = jnp.zeros((2, 8, COLS, C), BF)

    @pl.when(x == 3)
    def _():
        gp[8:10] = jnp.zeros((2, 10, COLS, C), BF)

    for load in loads:
        load.wait()

    row = 7 * other
    forward = (xp, wf, bias, ctv, bov, gp, gt, bsum, row)
    for t in range(2, 8):
        forward_frame(t, *forward, t == 2)

    into_row = 9 * zl
    recv_row = 9 * other
    pl.semaphore_wait(barrier, len(partners))
    later = jnp.minimum(x + 1, 3)
    halo_rows = remote(act.at[0, :, row], hrow, halo_send.at[0], halo_recv.at[0], at(zl_=other))
    halo_frames = remote(
        act.at[0, 6:8], hframes, halo_send.at[1], halo_recv.at[1], at(x_=later)
    )
    halo_corner = remote(
        act.at[0, 6:8, row], hcorner, halo_send.at[2], halo_recv.at[2], at(x_=later, zl_=other)
    )

    @pl.when(x < 3)
    def _():
        halo_frames.start()
        halo_corner.start()

    halo_rows.start()

    for d in range(5):
        early_taps(d, xp, gt, wacc)

    halo_rows.wait_recv()
    xp[2:10, recv_row] = hrow[...]

    @pl.when(x > 0)
    def _():
        halo_frames.wait_recv()
        halo_corner.wait_recv()
        xp[0:2, 1:9] = hframes[...]
        xp[0:2, recv_row] = hcorner[...]

    forward_seam(*forward)
    forward_frame(0, *forward, False)
    forward_frame(1, *forward, False)
    outs = [pltpu.make_async_copy(bov, block_out.at[0], out_sem.at[0])]
    outs[-1].start()

    earlier = jnp.maximum(x - 1, 0)
    ghalo_rows = remote(
        gp.at[0:8, 1 + row], gp.at[0:8, into_row], ghalo_send.at[0], ghalo_recv.at[0],
        at(zl_=other),
    )
    ghalo_frames = remote(
        gp.at[0:2, 1:9], gp.at[8:10, 1:9], ghalo_send.at[1], ghalo_recv.at[1], at(x_=earlier)
    )
    ghalo_corner = remote(
        gp.at[0:2, 1 + row], gp.at[8:10, into_row], ghalo_send.at[2], ghalo_recv.at[2],
        at(x_=earlier, zl_=other),
    )

    @pl.when(x > 0)
    def _():
        ghalo_frames.start()
        ghalo_corner.start()

    ghalo_rows.start()

    total_bias = jnp.sum(bsum[...], axis=0, keepdims=True)
    bias_hi = total_bias.astype(BF).astype(F32)
    bias_lo = total_bias - bias_hi
    line = lax.broadcasted_iota(jnp.int32, (BLOCK, C), 0)
    tail = jnp.where(line == SHARD, bias_hi, jnp.where(line == SHARD + 1, bias_lo, 0.0))

    def pack(i):
        q, y_, core_ = i // 8, (i // 2) % 4, i % 2
        rows = jnp.where(line < SHARD, dw[SHARD * i : SHARD * i + BLOCK], tail)
        pk[q, core_, y_] = rows.astype(BF)

    def core_copy(q):
        return remote(
            pk.at[q, 1 - core], cr.at[q], core_send.at[q], core_recv.at[q], at(core_=1 - core)
        )

    def y_copy(q, k):
        return remote(
            ys.at[q, k - 1], yr.at[q, k - 1], y_send.at[q, k - 1], y_recv.at[q, k - 1],
            at(y_=lax.rem(y + k, 4)),
        )

    def y_stage(q):
        core_copy(q).wait_recv()
        for k in (2, 1, 3):
            to = lax.rem(y + k, 4)
            ys[q, k - 1] = (pk[q, core, to].astype(F32) + cr[q, to].astype(F32)).astype(BF)
            y_copy(q, k).start()
        yown[q] = pk[q, core, y].astype(F32) + cr[q, y].astype(F32)

    def z_copy(q):
        slot = lax.rem(q - zh + 3, 4)
        return remote(
            zs.at[q], zr.at[slot], z_send.at[q], z_recv.at[slot], at(zh_=q)
        )

    def z_stage(q):
        total = yown[q]
        for k in (1, 3, 2):
            y_copy(q, k).wait_recv()
            total = total + yr[q, k - 1].astype(F32)

        @pl.when(zh == q)
        def _():
            zown[...] = total

        @pl.when(zh != q)
        def _():
            zs[q] = total.astype(BF)
            z_copy(q).start()

    packed, sent = 0, 0
    for d in range(5):
        late_taps(d, xp, gt, wacc, dw, row)
        ready = min(9, 2 * d + 2) * 3 * C
        while packed < 32 and SHARD * (packed + 1) <= ready:
            pack(packed)
            packed += 1
        while sent < 4 and packed >= 8 * (sent + 1):
            core_copy(sent).start()
            sent += 1
        if d >= 2:
            y_stage(d - 2)
    y_stage(3)

    for load in late:
        load.wait()
    remote(
        gp.at[0:8, 1 + row], gp.at[0:8, recv_row], ghalo_send.at[0], ghalo_recv.at[0],
        at(zl_=other),
    ).wait_recv()
    backward_frames(0, 2, gp, wt, ctv, giv)
    z_stage(0)
    backward_frames(2, 2, gp, wt, ctv, giv)
    z_stage(1)
    z_stage(2)
    z_stage(3)

    @pl.when(x < 3)
    def _():
        ghalo_frames.wait_recv()
        remote(
            gp.at[0:2, 1 + row], gp.at[8:10, recv_row], ghalo_send.at[2], ghalo_recv.at[2],
            at(x_=later, zl_=other),
        ).wait_recv()

    backward_frames(4, 2, gp, wt, ctv, giv)
    backward_frames(6, 2, gp, wt, ctv, giv)
    outs.append(pltpu.make_async_copy(giv, grad_input.at[0], out_sem.at[1]))
    outs[-1].start()

    total = zown[...]
    for slot in range(3):
        remote(
            zs.at[0], zr.at[slot], z_send.at[0], z_recv.at[slot], at(zh_=lax.rem(zh + 1, 4))
        ).wait_recv()
        total = total + zr[slot].astype(F32)
    fr[group] = total.astype(BF)

    def f_copy(k, slot):
        return remote(fr.at[group], fr.at[slot], f_send.at[k - 1], f_recv.at[slot], in_group(k))

    for k in (4, 5, 3, 2, 6, 1, 7):
        f_copy(k, group).start()
    for k in range(1, 8):
        f_copy(k, lax.rem(group + k, 8)).wait_recv()
    total = fr[0].astype(F32)
    for g in range(1, 8):
        total = total + fr[g].astype(F32)
    weight_grad[...] = total[:SHARD] * SCALE
    whole_bias = (total[SHARD : SHARD + 1] + total[SHARD + 1 : SHARD + 2]) * SCALE
    whole_bias = jnp.broadcast_to(whole_bias, (8, C))
    bias_grad[...] = pltpu.roll(whole_bias, lax.rem(C - 4 * dp, C), 1)[0:1]

    halo_rows.wait_send()
    ghalo_rows.wait_send()

    @pl.when(x < 3)
    def _():
        halo_frames.wait_send()
        halo_corner.wait_send()

    @pl.when(x > 0)
    def _():
        ghalo_frames.wait_send()
        ghalo_corner.wait_send()

    for q in range(4):
        core_copy(q).wait_send()
        for k in range(1, 4):
            y_copy(q, k).wait_send()

        @pl.when(zh != q)
        def _():
            z_copy(q).wait_send()

    for k in range(1, 8):
        f_copy(k, group).wait_send()
    for out in outs:
        out.wait()


def hand_over(*refs):
    inner, sem = refs[8:11], refs[11]
    parts = []
    for i in range(2):
        for f in range(0, FRAMES, 2):
            parts.append((refs[i].at[0, f : f + 2], inner[i].at[f : f + 2], refs[4 + i].at[0, f : f + 2]))
    parts.append((refs[2], inner[2], refs[6]))
    ins = [pltpu.make_async_copy(a, b, sem.at[0, n]) for n, (a, b, _) in enumerate(parts)]
    outs = [pltpu.make_async_copy(b, c, sem.at[1, n]) for n, (_, b, c) in enumerate(parts)]
    for copy in ins:
        copy.start()
    refs[7][...] = refs[3][0, 0:4]
    for into, out in zip(ins, outs):
        into.wait()
        out.start()
    for copy in outs:
        copy.wait()


def body(activations, weights, conv_bias, cotangent):
    hbm = pl.BlockSpec(memory_space=pltpu.HBM)
    anywhere = pl.BlockSpec(memory_space=pl.ANY)
    vmem = pl.BlockSpec(memory_space=pltpu.VMEM)
    dma = pltpu.SemaphoreType.DMA
    shape = (1, FRAMES, ROWS, COLS, C)
    results = pl.pallas_call(
        kernel,
        out_shape=[
            jax.ShapeDtypeStruct(shape, BF),
            jax.ShapeDtypeStruct(shape, BF),
            jax.ShapeDtypeStruct((SHARD, C), F32),
            jax.ShapeDtypeStruct((1, C), F32),
        ],
        in_specs=[hbm, hbm, vmem, hbm],
        out_specs=[anywhere, anywhere, vmem, vmem],
        scratch_shapes=[
            pltpu.VMEM((10, 10, COLS, C), BF),
            pltpu.VMEM((10, 10, COLS, C), BF),
            pltpu.VMEM((9, C, 3 * C), BF),
            pltpu.VMEM((3, C, 9 * C), BF),
            pltpu.VMEM((FRAMES, ROWS, COLS, C), BF),
            pltpu.VMEM((FRAMES, ROWS, COLS, C), BF),
            pltpu.VMEM((FRAMES, ROWS, COLS, C), BF),
            pltpu.VMEM((3 * C, EARLY + 6 * AREA), BF),
            pltpu.VMEM((3 * C, 9 * C), F32),
            pltpu.VMEM((27 * C + 24, C), F32),
            pltpu.VMEM((8, C), F32),
            pltpu.VMEM((FRAMES, COLS, C), BF),
            pltpu.VMEM((2, ROWS, COLS, C), BF),
            pltpu.VMEM((2, COLS, C), BF),
            pltpu.VMEM((4, 2, 4, BLOCK, C), BF),
            pltpu.VMEM((4, 4, BLOCK, C), BF),
            pltpu.VMEM((4, 3, BLOCK, C), BF),
            pltpu.VMEM((4, 3, BLOCK, C), BF),
            pltpu.VMEM((4, BLOCK, C), F32),
            pltpu.VMEM((4, BLOCK, C), BF),
            pltpu.VMEM((3, BLOCK, C), BF),
            pltpu.VMEM((BLOCK, C), F32),
            pltpu.VMEM((8, BLOCK, C), BF),
            dma((14,)),
            dma((2,)),
            dma((3,)),
            dma((3,)),
            dma((3,)),
            dma((3,)),
            dma((4,)),
            dma((4,)),
            dma((4, 3)),
            dma((4, 3)),
            dma((4,)),
            dma((3,)),
            dma((7,)),
            dma((8,)),
        ],
        compiler_params=pltpu.CompilerParams(
            collective_id=0, has_side_effects=True, vmem_limit_bytes=63 * 2**20+512*1024
        ),
    )(activations, weights.reshape(9, 3, C, C), conv_bias.reshape(1, C), cotangent)
    block_out, grad_input, weight_grad, bias_grad = pl.pallas_call(
        hand_over,
        out_shape=[
            jax.ShapeDtypeStruct(shape, BF),
            jax.ShapeDtypeStruct(shape, BF),
            jax.ShapeDtypeStruct((SHARD, C), F32),
            jax.ShapeDtypeStruct((4,), F32),
        ],
        in_specs=[anywhere, anywhere, anywhere, vmem],
        out_specs=[hbm, hbm, hbm, vmem],
        scratch_shapes=[
            pltpu.VMEM((FRAMES, ROWS, COLS, C), BF),
            pltpu.VMEM((FRAMES, ROWS, COLS, C), BF),
            pltpu.VMEM((SHARD, C), F32),
            dma((2, 9)),
        ],
        compiler_params=pltpu.CompilerParams(vmem_limit_bytes=63 * 2**20 + 512 * 1024),
    )(*results)
    return block_out, grad_input, weight_grad, bias_grad


def solution(mesh):
    return jax.shard_map(
        body,
        mesh=mesh,
        in_specs=(P("dp", "tm", "tile", None, None), P(), P(), P("dp", "tm", "tile", None, None)),
        out_specs=(
            P("dp", "tm", "tile", None, None),
            P("dp", "tm", "tile", None, None),
            P("dp", None),
            P("dp"),
        ),
        check_vma=False,
    )
```

```python
import math

import jax
import jax.numpy as jnp
from jax import lax
from jax.experimental import pallas as pl
from jax.experimental.pallas import tpu as pltpu
from jax.sharding import PartitionSpec as P

F32 = jnp.float32
BF = jnp.bfloat16
MESH = pl.DeviceIdType.MESH

C = 128
FRAMES, ROWS, COLS = 8, 8, 32
AREA = ROWS * COLS
POSITIONS = FRAMES * AREA
TAPS_AB = [(a, b) for a in range(3) for b in range(3)]
SHARD = 108
BLOCK = 112
EARLY = 3 * AREA
SCALE = 1.0 / math.sqrt(524288.0)


def shift_columns(values, by):
    rows = values.shape[0]
    rolled = pltpu.roll(values, by % rows, 0)
    column = lax.broadcasted_iota(jnp.int32, values.shape, 0) & (COLS - 1)
    return jnp.where(column == (0 if by == 1 else COLS - 1), 0.0, rolled)


def forward_block(lhs, center, upstream, wf, bias):
    y = jnp.dot(lhs, wf[...].reshape(9 * C, 3 * C), preferred_element_type=F32)
    pre = y[:, C : 2 * C] + shift_columns(y[:, :C], 1) + shift_columns(y[:, 2 * C :], -1)
    pre = pre + bias[...]
    sig = 0.5 * jnp.tanh(0.5 * pre) + 0.5
    out = (center.astype(F32) + pre * sig).astype(BF)
    grad = upstream.astype(F32) * (sig * (1.0 + pre * (1.0 - sig)))
    return out, grad.astype(BF)


def keep_turned(grad, start, gt, bsum, first):
    part = jnp.sum(grad.reshape(AREA // 8, 8, C), axis=0)
    if first:
        bsum[...] = part
    else:
        bsum[...] += part
    turned = jnp.transpose(grad)
    lane = lax.broadcasted_iota(jnp.int32, (C, C), 1) & (COLS - 1)
    gt[C : 2 * C, start : start + AREA] = turned.astype(BF)
    for half in range(2):
        piece = turned[:, half * C : half * C + C]
        at = start + half * C
        ahead = jnp.where(lane == COLS - 1, 0.0, pltpu.roll(piece, C - 1, 1))
        behind = jnp.where(lane == 0, 0.0, pltpu.roll(piece, 1, 1))
        gt[0:C, at : at + C] = ahead.astype(BF)
        gt[2 * C : 3 * C, at : at + C] = behind.astype(BF)


def forward_frame(t, xp, wf, bias, ctv, bov, gp, gt, bsum, row, first):
    lhs = jnp.concatenate(
        [xp[t + a, b : b + ROWS].reshape(AREA, C) for a, b in TAPS_AB], axis=1
    )
    out, grad = forward_block(
        lhs, xp[t + 2, 1 : 1 + ROWS].reshape(AREA, C), ctv[t].reshape(AREA, C), wf, bias
    )
    bov[t] = out.reshape(ROWS, COLS, C)
    gp[t, 1 : 1 + ROWS] = grad.reshape(ROWS, COLS, C)
    at_row = lax.broadcasted_iota(jnp.int32, (AREA, C), 0) // COLS
    start = t * AREA if t < 2 else EARLY + (t - 2) * AREA
    keep_turned(jnp.where(at_row == row, 0.0, grad.astype(F32)), start, gt, bsum, first)


def forward_seam(xp, wf, bias, ctv, bov, gp, gt, bsum, row):
    lhs = jnp.concatenate(
        [xp[a : a + FRAMES, row + b].reshape(AREA, C) for a, b in TAPS_AB], axis=1
    )
    out, grad = forward_block(
        lhs, xp[2 : 2 + FRAMES, row + 1].reshape(AREA, C), ctv[:, row].reshape(AREA, C), wf, bias
    )
    bov[:, row] = out.reshape(FRAMES, COLS, C)
    gp[0:FRAMES, row + 1] = grad.reshape(FRAMES, COLS, C)
    keep_turned(grad.astype(F32), 2 * AREA, gt, bsum, False)


def early_taps(d, xp, gt, wacc):
    pairs = TAPS_AB[2 * d : 2 * d + 2]
    rhs = jnp.concatenate(
        [xp[a + 2 : a + FRAMES, b : b + ROWS].reshape(6 * AREA, C) for a, b in pairs], axis=1
    )
    lhs = gt[:, EARLY : EARLY + 6 * AREA]
    wacc[:, 2 * C * d : 2 * C * d + len(pairs) * C] = jnp.dot(
        lhs, rhs, preferred_element_type=F32
    )


def late_taps(d, xp, gt, wacc, dw, row):
    pairs = TAPS_AB[2 * d : 2 * d + 2]
    rhs = jnp.concatenate(
        [
            jnp.concatenate(
                [
                    xp[a : a + 2, b : b + ROWS].reshape(2 * AREA, C),
                    xp[a : a + FRAMES, row + b].reshape(AREA, C),
                ],
                axis=0,
            )
            for a, b in pairs
        ],
        axis=1,
    )
    out = jnp.dot(gt[:, :EARLY], rhs, preferred_element_type=F32)
    out = out + wacc[:, 2 * C * d : 2 * C * d + len(pairs) * C]
    for j in range(len(pairs)):
        for e in range(3):
            tap = (2 * d + j) * 3 + e
            dw[tap * C : tap * C + C] = jnp.transpose(
                out[e * C : e * C + C, j * C : j * C + C]
            )


def backward_frames(t, n, gp, wt, ctv, giv):
    rows = n * AREA
    lhs = jnp.concatenate(
        [gp[t + 2 - a : t + 2 - a + n, 2 - b : 2 - b + ROWS].reshape(rows, C) for a, b in TAPS_AB],
        axis=1,
    )
    y = lax.dot_general(
        lhs,
        wt[...].reshape(3 * C, 9 * C),
        (((1,), (1,)), ((), ())),
        preferred_element_type=F32,
    )
    out = y[:, C : 2 * C] + shift_columns(y[:, :C], -1) + shift_columns(y[:, 2 * C :], 1)
    out = out + ctv[t : t + n].reshape(rows, C).astype(F32)
    giv[t : t + n] = out.astype(BF).reshape(n, ROWS, COLS, C)


def kernel(
    act, ker, bias, cot, block_out, grad_input, weight_grad, bias_grad,
    xp, gp, wf, wt, ctv, bov, giv, gt, wacc, dw, bsum, hrow, hframes, hcorner,
    pk, cr, ys, yr, yown, zs, zr, zown, fr,
    load_sem, out_sem, halo_send, halo_recv, ghalo_send, ghalo_recv,
    core_send, core_recv, y_send, y_recv, z_send, z_recv, f_send, f_recv,
):
    dp = lax.axis_index("dp")
    x = lax.axis_index("tm")
    zl = lax.axis_index("tile")
    core = lax.rem(dp, 2)
    y = lax.rem(dp // 2, 4)
    zh = dp // 8
    other = 1 - zl

    def at(zh_=None, y_=None, core_=None, x_=None, zl_=None):
        zh_ = zh if zh_ is None else zh_
        y_ = y if y_ is None else y_
        core_ = core if core_ is None else core_
        return {
            "dp": (zh_ * 4 + y_) * 2 + core_,
            "tm": x if x_ is None else x_,
            "tile": zl if zl_ is None else zl_,
        }

    def remote(src, dst, send, recv, where):
        return pltpu.make_async_remote_copy(
            src_ref=src, dst_ref=dst, send_sem=send, recv_sem=recv,
            device_id=where, device_id_type=MESH,
        )

    barrier = pltpu.get_barrier_semaphore()
    group = x * 2 + zl

    def in_group(k):
        to = lax.rem(group + k, 8)
        return at(x_=to // 2, zl_=lax.rem(to, 2))

    partners = [at(zh_=lax.rem(zh + k, 4)) for k in (2, 1, 3)]
    partners += [in_group(k) for k in (4, 5, 3, 2, 6, 1, 7)]
    partners += [at(y_=lax.rem(y + k, 4)) for k in (2, 1, 3)]
    partners += [at(core_=1 - core)]
    for partner in partners:
        pl.semaphore_signal(barrier, inc=1, device_id=partner, device_id_type=MESH)

    loads = [pltpu.make_async_copy(act.at[0], xp.at[2:10, 1:9], load_sem.at[0])]
    for e in range(3):
        loads.append(
            pltpu.make_async_copy(
                ker.at[:, e], wf.at[:, :, e * C : e * C + C], load_sem.at[1 + e]
            )
        )
    loads.append(pltpu.make_async_copy(cot.at[0], ctv, load_sem.at[4]))
    late = [
        pltpu.make_async_copy(ker.at[i], wt.at[:, :, i * C : i * C + C], load_sem.at[5 + i])
        for i in range(9)
    ]
    for load in loads + late:
        load.start()

    row_zeros = jnp.zeros((10, COLS, C), BF)
    xp[:, 0] = row_zeros
    xp[:, 9] = row_zeros
    gp[:, 9 * zl] = row_zeros
    xp[0:2, 1:9] = jnp.zeros((2, 8, COLS, C), BF)

    @pl.when(x == 3)
    def _():
        gp[8:10] = jnp.zeros((2, 10, COLS, C), BF)

    row = 7 * other
    into_row = 9 * zl
    recv_row = 9 * other
    later = jnp.minimum(x + 1, 3)
    halo_rows = remote(act.at[0, :, row], hrow, halo_send.at[0], halo_recv.at[0], at(zl_=other))
    halo_frames = remote(
        act.at[0, 6:8], hframes, halo_send.at[1], halo_recv.at[1], at(x_=later)
    )
    halo_corner = remote(
        act.at[0, 6:8, row], hcorner, halo_send.at[2], halo_recv.at[2], at(x_=later, zl_=other)
    )

    z = 2 * zh + zl
    ahead = jnp.maximum(
        2 - jnp.minimum(x, 4 - x),
        jnp.maximum(2 - jnp.minimum(y, 4 - y), 4 - jnp.minimum(z, 8 - z)),
    )

    def greet_and_send(mine):
        @pl.when(mine)
        def _():
            pl.semaphore_wait(barrier, len(partners))

            @pl.when(x < 3)
            def _():
                halo_frames.start()
                halo_corner.start()

            halo_rows.start()

    greet_and_send(ahead <= 1)
    for load in loads:
        load.wait()

    forward = (xp, wf, bias, ctv, bov, gp, gt, bsum, row)
    for t in range(2, 8):
        forward_frame(t, *forward, t == 2)
        if t == 5:
            greet_and_send(ahead == 2)
    greet_and_send(ahead >= 3)

    for d in range(5):
        early_taps(d, xp, gt, wacc)

    halo_rows.wait_recv()
    xp[2:10, recv_row] = hrow[...]

    @pl.when(x > 0)
    def _():
        halo_frames.wait_recv()
        halo_corner.wait_recv()
        xp[0:2, 1:9] = hframes[...]
        xp[0:2, recv_row] = hcorner[...]

    forward_seam(*forward)
    forward_frame(0, *forward, False)
    forward_frame(1, *forward, False)
    outs = [pltpu.make_async_copy(bov, block_out.at[0], out_sem.at[0])]
    outs[-1].start()

    earlier = jnp.maximum(x - 1, 0)
    ghalo_rows = remote(
        gp.at[0:8, 1 + row], gp.at[0:8, into_row], ghalo_send.at[0], ghalo_recv.at[0],
        at(zl_=other),
    )
    ghalo_frames = remote(
        gp.at[0:2, 1:9], gp.at[8:10, 1:9], ghalo_send.at[1], ghalo_recv.at[1], at(x_=earlier)
    )
    ghalo_corner = remote(
        gp.at[0:2, 1 + row], gp.at[8:10, into_row], ghalo_send.at[2], ghalo_recv.at[2],
        at(x_=earlier, zl_=other),
    )

    @pl.when(x > 0)
    def _():
        ghalo_frames.start()
        ghalo_corner.start()

    ghalo_rows.start()

    total_bias = jnp.sum(bsum[...], axis=0, keepdims=True)
    bias_hi = total_bias.astype(BF).astype(F32)
    bias_lo = total_bias - bias_hi
    line = lax.broadcasted_iota(jnp.int32, (BLOCK, C), 0)
    tail = jnp.where(line == SHARD, bias_hi, jnp.where(line == SHARD + 1, bias_lo, 0.0))

    def pack(i):
        q, y_, core_ = i // 8, (i // 2) % 4, i % 2
        rows = jnp.where(line < SHARD, dw[SHARD * i : SHARD * i + BLOCK], tail)
        pk[q, core_, y_] = rows.astype(BF)

    def core_copy(q):
        return remote(
            pk.at[q, 1 - core], cr.at[q], core_send.at[q], core_recv.at[q], at(core_=1 - core)
        )

    def y_copy(q, k):
        return remote(
            ys.at[q, k - 1], yr.at[q, k - 1], y_send.at[q, k - 1], y_recv.at[q, k - 1],
            at(y_=lax.rem(y + k, 4)),
        )

    def y_stage(q):
        core_copy(q).wait_recv()
        for k in (2, 1, 3):
            to = lax.rem(y + k, 4)
            ys[q, k - 1] = (pk[q, core, to].astype(F32) + cr[q, to].astype(F32)).astype(BF)
            y_copy(q, k).start()
        yown[q] = pk[q, core, y].astype(F32) + cr[q, y].astype(F32)

    def z_copy(q):
        slot = lax.rem(q - zh + 3, 4)
        return remote(
            zs.at[q], zr.at[slot], z_send.at[q], z_recv.at[slot], at(zh_=q)
        )

    def z_stage(q):
        total = yown[q]
        for k in (1, 3, 2):
            y_copy(q, k).wait_recv()
            total = total + yr[q, k - 1].astype(F32)

        @pl.when(zh == q)
        def _():
            zown[...] = total

        @pl.when(zh != q)
        def _():
            zs[q] = total.astype(BF)
            z_copy(q).start()

    packed, sent = 0, 0
    for d in range(5):
        late_taps(d, xp, gt, wacc, dw, row)
        ready = min(9, 2 * d + 2) * 3 * C
        while packed < 32 and SHARD * (packed + 1) <= ready:
            pack(packed)
            packed += 1
        while sent < 4 and packed >= 8 * (sent + 1):
            core_copy(sent).start()
            sent += 1
        if d >= 2:
            y_stage(d - 2)
    y_stage(3)

    for load in late:
        load.wait()
    remote(
        gp.at[0:8, 1 + row], gp.at[0:8, recv_row], ghalo_send.at[0], ghalo_recv.at[0],
        at(zl_=other),
    ).wait_recv()
    backward_frames(0, 2, gp, wt, ctv, giv)
    z_stage(0)
    backward_frames(2, 2, gp, wt, ctv, giv)
    z_stage(1)
    z_stage(2)
    z_stage(3)

    @pl.when(x < 3)
    def _():
        ghalo_frames.wait_recv()
        remote(
            gp.at[0:2, 1 + row], gp.at[8:10, recv_row], ghalo_send.at[2], ghalo_recv.at[2],
            at(x_=later, zl_=other),
        ).wait_recv()

    backward_frames(4, 2, gp, wt, ctv, giv)
    backward_frames(6, 2, gp, wt, ctv, giv)
    outs.append(pltpu.make_async_copy(giv, grad_input.at[0], out_sem.at[1]))
    outs[-1].start()

    total = zown[...]
    for slot in range(3):
        remote(
            zs.at[0], zr.at[slot], z_send.at[0], z_recv.at[slot], at(zh_=lax.rem(zh + 1, 4))
        ).wait_recv()
        total = total + zr[slot].astype(F32)
    fr[group] = total.astype(BF)

    def f_copy(k, slot):
        return remote(fr.at[group], fr.at[slot], f_send.at[k - 1], f_recv.at[slot], in_group(k))

    for k in (4, 5, 3, 2, 6, 1, 7):
        f_copy(k, group).start()
    for k in range(1, 8):
        f_copy(k, lax.rem(group + k, 8)).wait_recv()
    total = fr[0].astype(F32)
    for g in range(1, 8):
        total = total + fr[g].astype(F32)
    weight_grad[...] = total[:SHARD] * SCALE
    whole_bias = (total[SHARD : SHARD + 1] + total[SHARD + 1 : SHARD + 2]) * SCALE
    whole_bias = jnp.broadcast_to(whole_bias, (8, C))
    bias_grad[...] = pltpu.roll(whole_bias, lax.rem(C - 4 * dp, C), 1)[0:1]

    halo_rows.wait_send()
    ghalo_rows.wait_send()

    @pl.when(x < 3)
    def _():
        halo_frames.wait_send()
        halo_corner.wait_send()

    @pl.when(x > 0)
    def _():
        ghalo_frames.wait_send()
        ghalo_corner.wait_send()

    for q in range(4):
        core_copy(q).wait_send()
        for k in range(1, 4):
            y_copy(q, k).wait_send()

        @pl.when(zh != q)
        def _():
            z_copy(q).wait_send()

    for k in range(1, 8):
        f_copy(k, group).wait_send()
    for out in outs:
        out.wait()


def hand_over(*refs):
    inner, sem = refs[8:11], refs[11]
    parts = []
    for i in range(2):
        for f in range(0, FRAMES, 2):
            parts.append((refs[i].at[0, f : f + 2], inner[i].at[f : f + 2], refs[4 + i].at[0, f : f + 2]))
    parts.append((refs[2], inner[2], refs[6]))
    ins = [pltpu.make_async_copy(a, b, sem.at[0, n]) for n, (a, b, _) in enumerate(parts)]
    outs = [pltpu.make_async_copy(b, c, sem.at[1, n]) for n, (_, b, c) in enumerate(parts)]
    for copy in ins:
        copy.start()
    refs[7][...] = refs[3][0, 0:4]
    for into, out in zip(ins, outs):
        into.wait()
        out.start()
    for copy in outs:
        copy.wait()


def body(activations, weights, conv_bias, cotangent):
    hbm = pl.BlockSpec(memory_space=pltpu.HBM)
    anywhere = pl.BlockSpec(memory_space=pl.ANY)
    vmem = pl.BlockSpec(memory_space=pltpu.VMEM)
    dma = pltpu.SemaphoreType.DMA
    shape = (1, FRAMES, ROWS, COLS, C)
    results = pl.pallas_call(
        kernel,
        out_shape=[
            jax.ShapeDtypeStruct(shape, BF),
            jax.ShapeDtypeStruct(shape, BF),
            jax.ShapeDtypeStruct((SHARD, C), F32),
            jax.ShapeDtypeStruct((1, C), F32),
        ],
        in_specs=[hbm, hbm, vmem, hbm],
        out_specs=[anywhere, anywhere, vmem, vmem],
        scratch_shapes=[
            pltpu.VMEM((10, 10, COLS, C), BF),
            pltpu.VMEM((10, 10, COLS, C), BF),
            pltpu.VMEM((9, C, 3 * C), BF),
            pltpu.VMEM((3, C, 9 * C), BF),
            pltpu.VMEM((FRAMES, ROWS, COLS, C), BF),
            pltpu.VMEM((FRAMES, ROWS, COLS, C), BF),
            pltpu.VMEM((FRAMES, ROWS, COLS, C), BF),
            pltpu.VMEM((3 * C, EARLY + 6 * AREA), BF),
            pltpu.VMEM((3 * C, 9 * C), F32),
            pltpu.VMEM((27 * C + 24, C), F32),
            pltpu.VMEM((8, C), F32),
            pltpu.VMEM((FRAMES, COLS, C), BF),
            pltpu.VMEM((2, ROWS, COLS, C), BF),
            pltpu.VMEM((2, COLS, C), BF),
            pltpu.VMEM((4, 2, 4, BLOCK, C), BF),
            pltpu.VMEM((4, 4, BLOCK, C), BF),
            pltpu.VMEM((4, 3, BLOCK, C), BF),
            pltpu.VMEM((4, 3, BLOCK, C), BF),
            pltpu.VMEM((4, BLOCK, C), F32),
            pltpu.VMEM((4, BLOCK, C), BF),
            pltpu.VMEM((3, BLOCK, C), BF),
            pltpu.VMEM((BLOCK, C), F32),
            pltpu.VMEM((8, BLOCK, C), BF),
            dma((14,)),
            dma((2,)),
            dma((3,)),
            dma((3,)),
            dma((3,)),
            dma((3,)),
            dma((4,)),
            dma((4,)),
            dma((4, 3)),
            dma((4, 3)),
            dma((4,)),
            dma((3,)),
            dma((7,)),
            dma((8,)),
        ],
        compiler_params=pltpu.CompilerParams(
            collective_id=0, has_side_effects=True, vmem_limit_bytes=63 * 2**20+512*1024
        ),
    )(activations, weights.reshape(9, 3, C, C), conv_bias.reshape(1, C), cotangent)
    block_out, grad_input, weight_grad, bias_grad = pl.pallas_call(
        hand_over,
        out_shape=[
            jax.ShapeDtypeStruct(shape, BF),
            jax.ShapeDtypeStruct(shape, BF),
            jax.ShapeDtypeStruct((SHARD, C), F32),
            jax.ShapeDtypeStruct((4,), F32),
        ],
        in_specs=[anywhere, anywhere, anywhere, vmem],
        out_specs=[hbm, hbm, hbm, vmem],
        scratch_shapes=[
            pltpu.VMEM((FRAMES, ROWS, COLS, C), BF),
            pltpu.VMEM((FRAMES, ROWS, COLS, C), BF),
            pltpu.VMEM((SHARD, C), F32),
            dma((2, 9)),
        ],
        compiler_params=pltpu.CompilerParams(vmem_limit_bytes=63 * 2**20 + 512 * 1024),
    )(*results)
    return block_out, grad_input, weight_grad, bias_grad


def solution(mesh):
    return jax.shard_map(
        body,
        mesh=mesh,
        in_specs=(P("dp", "tm", "tile", None, None), P(), P(), P("dp", "tm", "tile", None, None)),
        out_specs=(
            P("dp", "tm", "tile", None, None),
            P("dp", "tm", "tile", None, None),
            P("dp", None),
            P("dp"),
        ),
        check_vma=False,
    )
```

```python
import math

import jax
import jax.numpy as jnp
from jax import lax
from jax.experimental import pallas as pl
from jax.experimental.pallas import tpu as pltpu
from jax.sharding import PartitionSpec as P

F32 = jnp.float32
BF = jnp.bfloat16
MESH = pl.DeviceIdType.MESH

C = 128
FRAMES, ROWS, COLS = 8, 8, 32
AREA = ROWS * COLS
POSITIONS = FRAMES * AREA
TAPS_AB = [(a, b) for a in range(3) for b in range(3)]
SHARD = 108
BLOCK = 112
EARLY = 3 * AREA
SCALE = 1.0 / math.sqrt(524288.0)


def shift_columns(values, by):
    rows = values.shape[0]
    rolled = pltpu.roll(values, by % rows, 0)
    column = lax.broadcasted_iota(jnp.int32, values.shape, 0) & (COLS - 1)
    return jnp.where(column == (0 if by == 1 else COLS - 1), 0.0, rolled)


def forward_block(lhs, center, upstream, wf, bias):
    y = jnp.dot(lhs, wf[...].reshape(9 * C, 3 * C), preferred_element_type=F32)
    pre = y[:, C : 2 * C] + shift_columns(y[:, :C], 1) + shift_columns(y[:, 2 * C :], -1)
    pre = pre + bias[...]
    sig = 0.5 * jnp.tanh(0.5 * pre) + 0.5
    out = (center.astype(F32) + pre * sig).astype(BF)
    grad = upstream.astype(F32) * (sig * (1.0 + pre * (1.0 - sig)))
    return out, grad.astype(BF)


def keep_turned(grad, start, gt, bsum, first):
    part = jnp.sum(grad.reshape(AREA // 8, 8, C), axis=0)
    if first:
        bsum[...] = part
    else:
        bsum[...] += part
    turned = jnp.transpose(grad)
    lane = lax.broadcasted_iota(jnp.int32, (C, C), 1) & (COLS - 1)
    gt[C : 2 * C, start : start + AREA] = turned.astype(BF)
    for half in range(2):
        piece = turned[:, half * C : half * C + C]
        at = start + half * C
        ahead = jnp.where(lane == COLS - 1, 0.0, pltpu.roll(piece, C - 1, 1))
        behind = jnp.where(lane == 0, 0.0, pltpu.roll(piece, 1, 1))
        gt[0:C, at : at + C] = ahead.astype(BF)
        gt[2 * C : 3 * C, at : at + C] = behind.astype(BF)


def forward_frame(t, xp, wf, bias, ctv, bov, gp, gt, bsum, row, first):
    lhs = jnp.concatenate(
        [xp[t + a, b : b + ROWS].reshape(AREA, C) for a, b in TAPS_AB], axis=1
    )
    out, grad = forward_block(
        lhs, xp[t + 2, 1 : 1 + ROWS].reshape(AREA, C), ctv[t].reshape(AREA, C), wf, bias
    )
    bov[t] = out.reshape(ROWS, COLS, C)
    gp[t, 1 : 1 + ROWS] = grad.reshape(ROWS, COLS, C)
    at_row = lax.broadcasted_iota(jnp.int32, (AREA, C), 0) // COLS
    start = t * AREA if t < 2 else EARLY + (t - 2) * AREA
    keep_turned(jnp.where(at_row == row, 0.0, grad.astype(F32)), start, gt, bsum, first)


def forward_seam(xp, wf, bias, ctv, bov, gp, gt, bsum, row):
    lhs = jnp.concatenate(
        [xp[a : a + FRAMES, row + b].reshape(AREA, C) for a, b in TAPS_AB], axis=1
    )
    out, grad = forward_block(
        lhs, xp[2 : 2 + FRAMES, row + 1].reshape(AREA, C), ctv[:, row].reshape(AREA, C), wf, bias
    )
    bov[:, row] = out.reshape(FRAMES, COLS, C)
    gp[0:FRAMES, row + 1] = grad.reshape(FRAMES, COLS, C)
    keep_turned(grad.astype(F32), 2 * AREA, gt, bsum, False)


def early_taps(d, xp, gt, wacc):
    pairs = TAPS_AB[2 * d : 2 * d + 2]
    rhs = jnp.concatenate(
        [xp[a + 2 : a + FRAMES, b : b + ROWS].reshape(6 * AREA, C) for a, b in pairs], axis=1
    )
    lhs = gt[:, EARLY : EARLY + 6 * AREA]
    wacc[:, 2 * C * d : 2 * C * d + len(pairs) * C] = jnp.dot(
        lhs, rhs, preferred_element_type=F32
    )


def late_taps(d, xp, gt, wacc, dw, row):
    pairs = TAPS_AB[2 * d : 2 * d + 2]
    rhs = jnp.concatenate(
        [
            jnp.concatenate(
                [
                    xp[a : a + 2, b : b + ROWS].reshape(2 * AREA, C),
                    xp[a : a + FRAMES, row + b].reshape(AREA, C),
                ],
                axis=0,
            )
            for a, b in pairs
        ],
        axis=1,
    )
    out = jnp.dot(gt[:, :EARLY], rhs, preferred_element_type=F32)
    out = out + wacc[:, 2 * C * d : 2 * C * d + len(pairs) * C]
    for j in range(len(pairs)):
        for e in range(3):
            tap = (2 * d + j) * 3 + e
            dw[tap * C : tap * C + C] = jnp.transpose(
                out[e * C : e * C + C, j * C : j * C + C]
            )


def backward_frames(t, n, gp, wt, ctv, giv):
    rows = n * AREA
    lhs = jnp.concatenate(
        [gp[t + 2 - a : t + 2 - a + n, 2 - b : 2 - b + ROWS].reshape(rows, C) for a, b in TAPS_AB],
        axis=1,
    )
    y = lax.dot_general(
        lhs,
        wt[...].reshape(3 * C, 9 * C),
        (((1,), (1,)), ((), ())),
        preferred_element_type=F32,
    )
    out = y[:, C : 2 * C] + shift_columns(y[:, :C], -1) + shift_columns(y[:, 2 * C :], 1)
    out = out + ctv[t : t + n].reshape(rows, C).astype(F32)
    giv[t : t + n] = out.astype(BF).reshape(n, ROWS, COLS, C)


def kernel(
    act, ker, bias, cot, block_out, grad_input, weight_grad, bias_grad,
    xp, gp, wf, wt, ctv, bov, giv, gt, wacc, dw, bsum, hrow, hframes, hcorner,
    pk, cr, ys, yr, yown, zs, zr, fr,
    load_sem, out_sem, halo_send, halo_recv, ghalo_send, ghalo_recv,
    core_send, core_recv, y_send, y_recv, z_send, z_recv, f_send, f_recv,
):
    dp = lax.axis_index("dp")
    x = lax.axis_index("tm")
    zl = lax.axis_index("tile")
    core = lax.rem(dp, 2)
    y = lax.rem(dp // 2, 4)
    zh = dp // 8
    other = 1 - zl

    def at(zh_=None, y_=None, core_=None, x_=None, zl_=None):
        zh_ = zh if zh_ is None else zh_
        y_ = y if y_ is None else y_
        core_ = core if core_ is None else core_
        return {
            "dp": (zh_ * 4 + y_) * 2 + core_,
            "tm": x if x_ is None else x_,
            "tile": zl if zl_ is None else zl_,
        }

    def remote(src, dst, send, recv, where):
        return pltpu.make_async_remote_copy(
            src_ref=src, dst_ref=dst, send_sem=send, recv_sem=recv,
            device_id=where, device_id_type=MESH,
        )

    barrier = pltpu.get_barrier_semaphore()
    column = zh * 2 + zl
    partners = [at(zh_=lax.rem(zh + k, 4), zl_=side) for k in (2, 1, 3) for side in (zl, other)]
    partners += [at(x_=lax.rem(x + k, 4)) for k in (2, 1, 3)]
    partners += [at(x_=lax.rem(x + k, 4), zl_=other) for k in (1, 3)]
    partners += [at(y_=lax.rem(y + k, 4)) for k in (2, 1, 3)]
    partners += [at(zl_=other)]
    partners += [at(core_=1 - core)]
    for partner in partners:
        pl.semaphore_signal(barrier, inc=1, device_id=partner, device_id_type=MESH)

    loads = [pltpu.make_async_copy(act.at[0], xp.at[2:10, 1:9], load_sem.at[0])]
    for e in range(3):
        loads.append(
            pltpu.make_async_copy(
                ker.at[:, e], wf.at[:, :, e * C : e * C + C], load_sem.at[1 + e]
            )
        )
    loads.append(pltpu.make_async_copy(cot.at[0], ctv, load_sem.at[4]))
    late = [
        pltpu.make_async_copy(ker.at[i], wt.at[:, :, i * C : i * C + C], load_sem.at[5 + i])
        for i in range(9)
    ]
    for load in loads + late:
        load.start()

    row_zeros = jnp.zeros((10, COLS, C), BF)
    xp[:, 0] = row_zeros
    xp[:, 9] = row_zeros
    gp[:, 9 * zl] = row_zeros
    xp[0:2, 1:9] = jnp.zeros((2, 8, COLS, C), BF)

    @pl.when(x == 3)
    def _():
        gp[8:10] = jnp.zeros((2, 10, COLS, C), BF)

    for load in loads:
        load.wait()

    row = 7 * other
    forward = (xp, wf, bias, ctv, bov, gp, gt, bsum, row)
    for t in range(2, 8):
        forward_frame(t, *forward, t == 2)

    into_row = 9 * zl
    recv_row = 9 * other
    pl.semaphore_wait(barrier, len(partners))
    later = jnp.minimum(x + 1, 3)
    halo_rows = remote(act.at[0, :, row], hrow, halo_send.at[0], halo_recv.at[0], at(zl_=other))
    halo_frames = remote(
        act.at[0, 6:8], hframes, halo_send.at[1], halo_recv.at[1], at(x_=later)
    )
    halo_corner = remote(
        act.at[0, 6:8, row], hcorner, halo_send.at[2], halo_recv.at[2], at(x_=later, zl_=other)
    )

    @pl.when(x < 3)
    def _():
        halo_frames.start()
        halo_corner.start()

    halo_rows.start()

    for d in range(5):
        early_taps(d, xp, gt, wacc)

    halo_rows.wait_recv()
    xp[2:10, recv_row] = hrow[...]

    @pl.when(x > 0)
    def _():
        halo_frames.wait_recv()
        halo_corner.wait_recv()
        xp[0:2, 1:9] = hframes[...]
        xp[0:2, recv_row] = hcorner[...]

    forward_seam(*forward)
    forward_frame(0, *forward, False)
    forward_frame(1, *forward, False)
    outs = [pltpu.make_async_copy(bov, block_out.at[0], out_sem.at[0])]
    outs[-1].start()

    earlier = jnp.maximum(x - 1, 0)
    ghalo_rows = remote(
        gp.at[0:8, 1 + row], gp.at[0:8, into_row], ghalo_send.at[0], ghalo_recv.at[0],
        at(zl_=other),
    )
    ghalo_frames = remote(
        gp.at[0:2, 1:9], gp.at[8:10, 1:9], ghalo_send.at[1], ghalo_recv.at[1], at(x_=earlier)
    )
    ghalo_corner = remote(
        gp.at[0:2, 1 + row], gp.at[8:10, into_row], ghalo_send.at[2], ghalo_recv.at[2],
        at(x_=earlier, zl_=other),
    )

    @pl.when(x > 0)
    def _():
        ghalo_frames.start()
        ghalo_corner.start()

    ghalo_rows.start()

    total_bias = jnp.sum(bsum[...], axis=0, keepdims=True)
    bias_hi = total_bias.astype(BF).astype(F32)
    bias_lo = total_bias - bias_hi
    line = lax.broadcasted_iota(jnp.int32, (BLOCK, C), 0)
    tail = jnp.where(line == SHARD, bias_hi, jnp.where(line == SHARD + 1, bias_lo, 0.0))

    def pack(i):
        q, y_, core_ = i // 8, (i // 2) % 4, i % 2
        rows = jnp.where(line < SHARD, dw[SHARD * i : SHARD * i + BLOCK], tail)
        pk[q, core_, y_] = rows.astype(BF)

    def core_copy(q):
        return remote(
            pk.at[q, 1 - core], cr.at[q], core_send.at[q], core_recv.at[q], at(core_=1 - core)
        )

    def y_copy(q, k):
        return remote(
            ys.at[q, k - 1], yr.at[q, k - 1], y_send.at[q, k - 1], y_recv.at[q, k - 1],
            at(y_=lax.rem(y + k, 4)),
        )

    def y_stage(q):
        core_copy(q).wait_recv()
        for k in (2, 1, 3):
            to = lax.rem(y + k, 4)
            ys[q, k - 1] = (pk[q, core, to].astype(F32) + cr[q, to].astype(F32)).astype(BF)
            y_copy(q, k).start()
        yown[q] = pk[q, core, y].astype(F32) + cr[q, y].astype(F32)

    def z_copy(q, side):
        return remote(
            zs.at[q], zr.at[column], z_send.at[q, side], z_recv.at[column],
            at(zh_=q, zl_=other if side else zl),
        )

    def z_stage(q):
        total = yown[q]
        for k in (1, 3, 2):
            y_copy(q, k).wait_recv()
            total = total + yr[q, k - 1].astype(F32)
        zs[q] = total.astype(BF)
        z_copy(q, 1).start()

        @pl.when(zh != q)
        def _():
            z_copy(q, 0).start()

        @pl.when(zh == q)
        def _():
            zr[column] = zs[q]

    packed, sent = 0, 0
    for d in range(5):
        late_taps(d, xp, gt, wacc, dw, row)
        ready = min(9, 2 * d + 2) * 3 * C
        while packed < 32 and SHARD * (packed + 1) <= ready:
            pack(packed)
            packed += 1
        while sent < 4 and packed >= 8 * (sent + 1):
            core_copy(sent).start()
            sent += 1
        if d >= 2:
            y_stage(d - 2)
    y_stage(3)

    for load in late:
        load.wait()
    remote(
        gp.at[0:8, 1 + row], gp.at[0:8, recv_row], ghalo_send.at[0], ghalo_recv.at[0],
        at(zl_=other),
    ).wait_recv()
    backward_frames(0, 2, gp, wt, ctv, giv)
    z_stage(0)
    backward_frames(2, 2, gp, wt, ctv, giv)
    z_stage(1)
    z_stage(2)
    z_stage(3)

    @pl.when(x < 3)
    def _():
        ghalo_frames.wait_recv()
        remote(
            gp.at[0:2, 1 + row], gp.at[8:10, recv_row], ghalo_send.at[2], ghalo_recv.at[2],
            at(x_=later, zl_=other),
        ).wait_recv()

    backward_frames(4, 2, gp, wt, ctv, giv)
    backward_frames(6, 2, gp, wt, ctv, giv)
    outs.append(pltpu.make_async_copy(giv, grad_input.at[0], out_sem.at[1]))
    outs[-1].start()

    for k in range(1, 8):
        slot = lax.rem(column + k, 8)
        remote(
            zs.at[0], zr.at[slot], z_send.at[0, 1], z_recv.at[slot], at(zl_=other)
        ).wait_recv()
    total = zr[0].astype(F32)
    for slot in range(1, 8):
        total = total + zr[slot].astype(F32)
    fr[x] = total.astype(BF)

    def f_copy(k, slot):
        return remote(
            fr.at[x], fr.at[slot], f_send.at[k - 1], f_recv.at[slot], at(x_=lax.rem(x + k, 4))
        )

    for k in (2, 1, 3):
        f_copy(k, x).start()
    for k in (1, 3, 2):
        f_copy(k, lax.rem(x + k, 4)).wait_recv()
    total = fr[0].astype(F32)
    for g in range(1, 4):
        total = total + fr[g].astype(F32)
    weight_grad[...] = total[:SHARD] * SCALE
    whole_bias = (total[SHARD : SHARD + 1] + total[SHARD + 1 : SHARD + 2]) * SCALE
    whole_bias = jnp.broadcast_to(whole_bias, (8, C))
    bias_grad[...] = pltpu.roll(whole_bias, lax.rem(C - 4 * dp, C), 1)[0:1]

    halo_rows.wait_send()
    ghalo_rows.wait_send()

    @pl.when(x < 3)
    def _():
        halo_frames.wait_send()
        halo_corner.wait_send()

    @pl.when(x > 0)
    def _():
        ghalo_frames.wait_send()
        ghalo_corner.wait_send()

    for q in range(4):
        core_copy(q).wait_send()
        for k in range(1, 4):
            y_copy(q, k).wait_send()

        z_copy(q, 1).wait_send()

        @pl.when(zh != q)
        def _():
            z_copy(q, 0).wait_send()

    for k in range(1, 4):
        f_copy(k, x).wait_send()
    for out in outs:
        out.wait()


def hand_over(*refs):
    sem = refs[8]
    copies = [pltpu.make_async_copy(refs[i], refs[4 + i], sem.at[i]) for i in range(3)]
    for copy in copies:
        copy.start()
    refs[7][...] = refs[3][0, 0:4]
    for copy in copies:
        copy.wait()


def body(activations, weights, conv_bias, cotangent):
    hbm = pl.BlockSpec(memory_space=pltpu.HBM)
    anywhere = pl.BlockSpec(memory_space=pl.ANY)
    vmem = pl.BlockSpec(memory_space=pltpu.VMEM)
    dma = pltpu.SemaphoreType.DMA
    shape = (1, FRAMES, ROWS, COLS, C)
    results = pl.pallas_call(
        kernel,
        out_shape=[
            jax.ShapeDtypeStruct(shape, BF),
            jax.ShapeDtypeStruct(shape, BF),
            jax.ShapeDtypeStruct((SHARD, C), F32),
            jax.ShapeDtypeStruct((1, C), F32),
        ],
        in_specs=[hbm, hbm, vmem, hbm],
        out_specs=[anywhere, anywhere, vmem, vmem],
        scratch_shapes=[
            pltpu.VMEM((10, 10, COLS, C), BF),
            pltpu.VMEM((10, 10, COLS, C), BF),
            pltpu.VMEM((9, C, 3 * C), BF),
            pltpu.VMEM((3, C, 9 * C), BF),
            pltpu.VMEM((FRAMES, ROWS, COLS, C), BF),
            pltpu.VMEM((FRAMES, ROWS, COLS, C), BF),
            pltpu.VMEM((FRAMES, ROWS, COLS, C), BF),
            pltpu.VMEM((3 * C, EARLY + 6 * AREA), BF),
            pltpu.VMEM((3 * C, 9 * C), F32),
            pltpu.VMEM((27 * C + 24, C), F32),
            pltpu.VMEM((8, C), F32),
            pltpu.VMEM((FRAMES, COLS, C), BF),
            pltpu.VMEM((2, ROWS, COLS, C), BF),
            pltpu.VMEM((2, COLS, C), BF),
            pltpu.VMEM((4, 2, 4, BLOCK, C), BF),
            pltpu.VMEM((4, 4, BLOCK, C), BF),
            pltpu.VMEM((4, 3, BLOCK, C), BF),
            pltpu.VMEM((4, 3, BLOCK, C), BF),
            pltpu.VMEM((4, BLOCK, C), F32),
            pltpu.VMEM((4, BLOCK, C), BF),
            pltpu.VMEM((8, BLOCK, C), BF),
            pltpu.VMEM((4, BLOCK, C), BF),
            dma((14,)),
            dma((2,)),
            dma((3,)),
            dma((3,)),
            dma((3,)),
            dma((3,)),
            dma((4,)),
            dma((4,)),
            dma((4, 3)),
            dma((4, 3)),
            dma((4, 2)),
            dma((8,)),
            dma((3,)),
            dma((4,)),
        ],
        compiler_params=pltpu.CompilerParams(
            collective_id=0, has_side_effects=True, vmem_limit_bytes=54000 * 1024
        ),
    )(activations, weights.reshape(9, 3, C, C), conv_bias.reshape(1, C), cotangent)
    block_out, grad_input, weight_grad, bias_grad = pl.pallas_call(
        hand_over,
        out_shape=[
            jax.ShapeDtypeStruct(shape, BF),
            jax.ShapeDtypeStruct(shape, BF),
            jax.ShapeDtypeStruct((SHARD, C), F32),
            jax.ShapeDtypeStruct((4,), F32),
        ],
        in_specs=[vmem, vmem, vmem, vmem],
        out_specs=[hbm, hbm, hbm, vmem],
        scratch_shapes=[dma((3,))],
        compiler_params=pltpu.CompilerParams(vmem_limit_bytes=8 * 2**20),
    )(*results)
    return block_out, grad_input, weight_grad, bias_grad


def solution(mesh):
    return jax.shard_map(
        body,
        mesh=mesh,
        in_specs=(P("dp", "tm", "tile", None, None), P(), P(), P("dp", "tm", "tile", None, None)),
        out_specs=(
            P("dp", "tm", "tile", None, None),
            P("dp", "tm", "tile", None, None),
            P("dp", None),
            P("dp"),
        ),
        check_vma=False,
    )
```

```python
import math

import jax
import jax.numpy as jnp
from jax import lax
from jax.experimental import pallas as pl
from jax.experimental.pallas import tpu as pltpu
from jax.sharding import PartitionSpec as P

F32 = jnp.float32
BF = jnp.bfloat16
MESH = pl.DeviceIdType.MESH

C = 128
FRAMES, ROWS, COLS = 8, 8, 32
AREA = ROWS * COLS
POSITIONS = FRAMES * AREA
TAPS_AB = [(a, b) for a in range(3) for b in range(3)]
SHARD = 108
BLOCK = 112
EARLY = 3 * AREA
SCALE = 1.0 / math.sqrt(524288.0)


def shift_columns(values, by):
    rows = values.shape[0]
    rolled = pltpu.roll(values, by % rows, 0)
    column = lax.broadcasted_iota(jnp.int32, values.shape, 0) & (COLS - 1)
    return jnp.where(column == (0 if by == 1 else COLS - 1), 0.0, rolled)


def forward_block(lhs, center, upstream, wf, bias):
    y = jnp.dot(lhs, wf[...].reshape(9 * C, 3 * C), preferred_element_type=F32)
    pre = y[:, C : 2 * C] + shift_columns(y[:, :C], 1) + shift_columns(y[:, 2 * C :], -1)
    pre = pre + bias[...]
    sig = 0.5 * jnp.tanh(0.5 * pre) + 0.5
    out = (center.astype(F32) + pre * sig).astype(BF)
    grad = upstream.astype(F32) * (sig * (1.0 + pre * (1.0 - sig)))
    return out, grad.astype(BF)


def keep_turned(grad, start, gt, bsum, first):
    part = jnp.sum(grad.reshape(AREA // 8, 8, C), axis=0)
    if first:
        bsum[...] = part
    else:
        bsum[...] += part
    turned = jnp.transpose(grad)
    lane = lax.broadcasted_iota(jnp.int32, (C, C), 1) & (COLS - 1)
    gt[C : 2 * C, start : start + AREA] = turned.astype(BF)
    for half in range(2):
        piece = turned[:, half * C : half * C + C]
        at = start + half * C
        ahead = jnp.where(lane == COLS - 1, 0.0, pltpu.roll(piece, C - 1, 1))
        behind = jnp.where(lane == 0, 0.0, pltpu.roll(piece, 1, 1))
        gt[0:C, at : at + C] = ahead.astype(BF)
        gt[2 * C : 3 * C, at : at + C] = behind.astype(BF)


def forward_frame(t, xp, wf, bias, ctv, bov, gp, gt, bsum, row, first):
    lhs = jnp.concatenate(
        [xp[t + a, b : b + ROWS].reshape(AREA, C) for a, b in TAPS_AB], axis=1
    )
    out, grad = forward_block(
        lhs, xp[t + 2, 1 : 1 + ROWS].reshape(AREA, C), ctv[t].reshape(AREA, C), wf, bias
    )
    bov[t] = out.reshape(ROWS, COLS, C)
    gp[t, 1 : 1 + ROWS] = grad.reshape(ROWS, COLS, C)
    at_row = lax.broadcasted_iota(jnp.int32, (AREA, C), 0) // COLS
    start = t * AREA if t < 2 else EARLY + (t - 2) * AREA
    keep_turned(jnp.where(at_row == row, 0.0, grad.astype(F32)), start, gt, bsum, first)


def forward_seam(xp, wf, bias, ctv, bov, gp, gt, bsum, row):
    lhs = jnp.concatenate(
        [xp[a : a + FRAMES, row + b].reshape(AREA, C) for a, b in TAPS_AB], axis=1
    )
    out, grad = forward_block(
        lhs, xp[2 : 2 + FRAMES, row + 1].reshape(AREA, C), ctv[:, row].reshape(AREA, C), wf, bias
    )
    bov[:, row] = out.reshape(FRAMES, COLS, C)
    gp[0:FRAMES, row + 1] = grad.reshape(FRAMES, COLS, C)
    keep_turned(grad.astype(F32), 2 * AREA, gt, bsum, False)


def early_taps(d, xp, gt, wacc):
    pairs = TAPS_AB[2 * d : 2 * d + 2]
    rhs = jnp.concatenate(
        [xp[a + 2 : a + FRAMES, b : b + ROWS].reshape(6 * AREA, C) for a, b in pairs], axis=1
    )
    lhs = gt[:, EARLY : EARLY + 6 * AREA]
    wacc[:, 2 * C * d : 2 * C * d + len(pairs) * C] = jnp.dot(
        lhs, rhs, preferred_element_type=F32
    )


def late_taps(d, xp, gt, wacc, dw, row):
    pairs = TAPS_AB[2 * d : 2 * d + 2]
    rhs = jnp.concatenate(
        [
            jnp.concatenate(
                [
                    xp[a : a + 2, b : b + ROWS].reshape(2 * AREA, C),
                    xp[a : a + FRAMES, row + b].reshape(AREA, C),
                ],
                axis=0,
            )
            for a, b in pairs
        ],
        axis=1,
    )
    out = jnp.dot(gt[:, :EARLY], rhs, preferred_element_type=F32)
    out = out + wacc[:, 2 * C * d : 2 * C * d + len(pairs) * C]
    for j in range(len(pairs)):
        for e in range(3):
            tap = (2 * d + j) * 3 + e
            dw[tap * C : tap * C + C] = jnp.transpose(
                out[e * C : e * C + C, j * C : j * C + C]
            )


def backward_frames(t, n, gp, wt, ctv, giv):
    rows = n * AREA
    lhs = jnp.concatenate(
        [gp[t + 2 - a : t + 2 - a + n, 2 - b : 2 - b + ROWS].reshape(rows, C) for a, b in TAPS_AB],
        axis=1,
    )
    y = lax.dot_general(
        lhs,
        wt[...].reshape(3 * C, 9 * C),
        (((1,), (1,)), ((), ())),
        preferred_element_type=F32,
    )
    out = y[:, C : 2 * C] + shift_columns(y[:, :C], -1) + shift_columns(y[:, 2 * C :], 1)
    out = out + ctv[t : t + n].reshape(rows, C).astype(F32)
    giv[t : t + n] = out.astype(BF).reshape(n, ROWS, COLS, C)


def kernel(
    act, ker, bias, cot, block_out, grad_input, weight_grad, bias_grad,
    xp, gp, wf, wt, ctv, bov, giv, gt, wacc, dw, bsum, hrow, hframes, hcorner,
    pk, cr, ys, yr, yown, zs, zr, fr,
    load_sem, out_sem, halo_send, halo_recv, ghalo_send, ghalo_recv,
    core_send, core_recv, y_send, y_recv, z_send, z_recv, f_send, f_recv,
):
    dp = lax.axis_index("dp")
    x = lax.axis_index("tm")
    zl = lax.axis_index("tile")
    core = lax.rem(dp, 2)
    y = lax.rem(dp // 2, 4)
    zh = dp // 8
    other = 1 - zl

    def at(zh_=None, y_=None, core_=None, x_=None, zl_=None):
        zh_ = zh if zh_ is None else zh_
        y_ = y if y_ is None else y_
        core_ = core if core_ is None else core_
        return {
            "dp": (zh_ * 4 + y_) * 2 + core_,
            "tm": x if x_ is None else x_,
            "tile": zl if zl_ is None else zl_,
        }

    def remote(src, dst, send, recv, where):
        return pltpu.make_async_remote_copy(
            src_ref=src, dst_ref=dst, send_sem=send, recv_sem=recv,
            device_id=where, device_id_type=MESH,
        )

    barrier = pltpu.get_barrier_semaphore()
    column = zh * 2 + zl
    partners = [at(zh_=lax.rem(zh + k, 4), zl_=side) for k in (2, 1, 3) for side in (zl, other)]
    partners += [at(x_=lax.rem(x + k, 4)) for k in (2, 1, 3)]
    partners += [at(x_=lax.rem(x + k, 4), zl_=other) for k in (1, 3)]
    partners += [at(y_=lax.rem(y + k, 4)) for k in (2, 1, 3)]
    partners += [at(zl_=other)]
    partners += [at(core_=1 - core)]
    for partner in partners:
        pl.semaphore_signal(barrier, inc=1, device_id=partner, device_id_type=MESH)

    loads = [pltpu.make_async_copy(act.at[0], xp.at[2:10, 1:9], load_sem.at[0])]
    for e in range(3):
        loads.append(
            pltpu.make_async_copy(
                ker.at[:, e], wf.at[:, :, e * C : e * C + C], load_sem.at[1 + e]
            )
        )
    loads.append(pltpu.make_async_copy(cot.at[0], ctv, load_sem.at[4]))
    late = [
        pltpu.make_async_copy(ker.at[i], wt.at[:, :, i * C : i * C + C], load_sem.at[5 + i])
        for i in range(9)
    ]
    for load in loads:
        load.start()

    row_zeros = jnp.zeros((10, COLS, C), BF)
    xp[:, 0] = row_zeros
    xp[:, 9] = row_zeros
    gp[:, 9 * zl] = row_zeros
    xp[0:2, 1:9] = jnp.zeros((2, 8, COLS, C), BF)

    @pl.when(x == 3)
    def _():
        gp[8:10] = jnp.zeros((2, 10, COLS, C), BF)

    row = 7 * other
    into_row = 9 * zl
    recv_row = 9 * other
    later = jnp.minimum(x + 1, 3)
    halo_rows = remote(act.at[0, :, row], hrow, halo_send.at[0], halo_recv.at[0], at(zl_=other))
    halo_frames = remote(
        act.at[0, 6:8], hframes, halo_send.at[1], halo_recv.at[1], at(x_=later)
    )
    halo_corner = remote(
        act.at[0, 6:8, row], hcorner, halo_send.at[2], halo_recv.at[2], at(x_=later, zl_=other)
    )
    for load in loads:
        load.wait()
    for load in late:
        load.start()

    forward = (xp, wf, bias, ctv, bov, gp, gt, bsum, row)
    for t in range(2, 8):
        forward_frame(t, *forward, t == 2)
        if t == 3:
            pl.semaphore_wait(barrier, len(partners))

            @pl.when(x < 3)
            def _():
                halo_frames.start()
                halo_corner.start()

            halo_rows.start()

    for d in range(5):
        early_taps(d, xp, gt, wacc)

    halo_rows.wait_recv()
    xp[2:10, recv_row] = hrow[...]

    @pl.when(x > 0)
    def _():
        halo_frames.wait_recv()
        halo_corner.wait_recv()
        xp[0:2, 1:9] = hframes[...]
        xp[0:2, recv_row] = hcorner[...]

    forward_seam(*forward)
    forward_frame(0, *forward, False)
    forward_frame(1, *forward, False)
    outs = [pltpu.make_async_copy(bov, block_out.at[0], out_sem.at[0])]
    outs[-1].start()

    earlier = jnp.maximum(x - 1, 0)
    ghalo_rows = remote(
        gp.at[0:8, 1 + row], gp.at[0:8, into_row], ghalo_send.at[0], ghalo_recv.at[0],
        at(zl_=other),
    )
    ghalo_frames = remote(
        gp.at[0:2, 1:9], gp.at[8:10, 1:9], ghalo_send.at[1], ghalo_recv.at[1], at(x_=earlier)
    )
    ghalo_corner = remote(
        gp.at[0:2, 1 + row], gp.at[8:10, into_row], ghalo_send.at[2], ghalo_recv.at[2],
        at(x_=earlier, zl_=other),
    )

    @pl.when(x > 0)
    def _():
        ghalo_frames.start()
        ghalo_corner.start()

    ghalo_rows.start()

    total_bias = jnp.sum(bsum[...], axis=0, keepdims=True)
    bias_hi = total_bias.astype(BF).astype(F32)
    bias_lo = total_bias - bias_hi
    line = lax.broadcasted_iota(jnp.int32, (BLOCK, C), 0)
    tail = jnp.where(line == SHARD, bias_hi, jnp.where(line == SHARD + 1, bias_lo, 0.0))

    def pack(i):
        q, y_, core_ = i // 8, (i // 2) % 4, i % 2
        rows = jnp.where(line < SHARD, dw[SHARD * i : SHARD * i + BLOCK], tail)
        pk[q, core_, y_] = rows.astype(BF)

    def core_copy(q):
        return remote(
            pk.at[q, 1 - core], cr.at[q], core_send.at[q], core_recv.at[q], at(core_=1 - core)
        )

    def y_copy(q, k):
        return remote(
            ys.at[q, k - 1], yr.at[q, k - 1], y_send.at[q, k - 1], y_recv.at[q, k - 1],
            at(y_=lax.rem(y + k, 4)),
        )

    def y_stage(q):
        core_copy(q).wait_recv()
        for k in (2, 1, 3):
            to = lax.rem(y + k, 4)
            ys[q, k - 1] = (pk[q, core, to].astype(F32) + cr[q, to].astype(F32)).astype(BF)
            y_copy(q, k).start()
        yown[q] = pk[q, core, y].astype(F32) + cr[q, y].astype(F32)

    def z_copy(q, side):
        return remote(
            zs.at[q], zr.at[column], z_send.at[q, side], z_recv.at[column],
            at(zh_=q, zl_=other if side else zl),
        )

    def z_stage(q):
        total = yown[q]
        for k in (1, 3, 2):
            y_copy(q, k).wait_recv()
            total = total + yr[q, k - 1].astype(F32)
        zs[q] = total.astype(BF)
        z_copy(q, 1).start()

        @pl.when(zh != q)
        def _():
            z_copy(q, 0).start()

        @pl.when(zh == q)
        def _():
            zr[column] = zs[q]

    packed, sent = 0, 0
    for d in range(5):
        late_taps(d, xp, gt, wacc, dw, row)
        ready = min(9, 2 * d + 2) * 3 * C
        while packed < 32 and SHARD * (packed + 1) <= ready:
            pack(packed)
            packed += 1
        while sent < 4 and packed >= 8 * (sent + 1):
            core_copy(sent).start()
            sent += 1
    for q in range(4):
        y_stage(q)

    for load in late:
        load.wait()
    remote(
        gp.at[0:8, 1 + row], gp.at[0:8, recv_row], ghalo_send.at[0], ghalo_recv.at[0],
        at(zl_=other),
    ).wait_recv()
    backward_frames(0, 2, gp, wt, ctv, giv)
    z_stage(0)
    backward_frames(2, 2, gp, wt, ctv, giv)
    z_stage(1)
    z_stage(2)
    z_stage(3)

    @pl.when(x < 3)
    def _():
        ghalo_frames.wait_recv()
        remote(
            gp.at[0:2, 1 + row], gp.at[8:10, recv_row], ghalo_send.at[2], ghalo_recv.at[2],
            at(x_=later, zl_=other),
        ).wait_recv()

    backward_frames(4, 2, gp, wt, ctv, giv)
    backward_frames(6, 2, gp, wt, ctv, giv)
    outs.append(pltpu.make_async_copy(giv, grad_input.at[0], out_sem.at[1]))
    outs[-1].start()

    for k in range(1, 8):
        slot = lax.rem(column + k, 8)
        remote(
            zs.at[0], zr.at[slot], z_send.at[0, 1], z_recv.at[slot], at(zl_=other)
        ).wait_recv()
    total = zr[0].astype(F32)
    for slot in range(1, 8):
        total = total + zr[slot].astype(F32)
    fr[x] = total.astype(BF)

    def f_copy(k, slot):
        return remote(
            fr.at[x], fr.at[slot], f_send.at[k - 1], f_recv.at[slot], at(x_=lax.rem(x + k, 4))
        )

    for k in (2, 1, 3):
        f_copy(k, x).start()
    for k in (1, 3, 2):
        f_copy(k, lax.rem(x + k, 4)).wait_recv()
    total = fr[0].astype(F32)
    for g in range(1, 4):
        total = total + fr[g].astype(F32)
    weight_grad[...] = total[:SHARD] * SCALE
    whole_bias = (total[SHARD : SHARD + 1] + total[SHARD + 1 : SHARD + 2]) * SCALE
    whole_bias = jnp.broadcast_to(whole_bias, (8, C))
    bias_grad[...] = pltpu.roll(whole_bias, lax.rem(C - 4 * dp, C), 1)[0:1]

    halo_rows.wait_send()
    ghalo_rows.wait_send()

    @pl.when(x < 3)
    def _():
        halo_frames.wait_send()
        halo_corner.wait_send()

    @pl.when(x > 0)
    def _():
        ghalo_frames.wait_send()
        ghalo_corner.wait_send()

    for q in range(4):
        core_copy(q).wait_send()
        for k in range(1, 4):
            y_copy(q, k).wait_send()

        z_copy(q, 1).wait_send()

        @pl.when(zh != q)
        def _():
            z_copy(q, 0).wait_send()

    for k in range(1, 4):
        f_copy(k, x).wait_send()
    for out in outs:
        out.wait()


def hand_over(*refs):
    sem = refs[8]
    copies = [pltpu.make_async_copy(refs[i], refs[4 + i], sem.at[i]) for i in range(3)]
    for copy in copies:
        copy.start()
    refs[7][...] = refs[3][0, 0:4]
    for copy in copies:
        copy.wait()


def body(activations, weights, conv_bias, cotangent):
    hbm = pl.BlockSpec(memory_space=pltpu.HBM)
    anywhere = pl.BlockSpec(memory_space=pl.ANY)
    vmem = pl.BlockSpec(memory_space=pltpu.VMEM)
    dma = pltpu.SemaphoreType.DMA
    shape = (1, FRAMES, ROWS, COLS, C)
    results = pl.pallas_call(
        kernel,
        out_shape=[
            jax.ShapeDtypeStruct(shape, BF),
            jax.ShapeDtypeStruct(shape, BF),
            jax.ShapeDtypeStruct((SHARD, C), F32),
            jax.ShapeDtypeStruct((1, C), F32),
        ],
        in_specs=[hbm, hbm, vmem, hbm],
        out_specs=[anywhere, anywhere, vmem, vmem],
        scratch_shapes=[
            pltpu.VMEM((10, 10, COLS, C), BF),
            pltpu.VMEM((10, 10, COLS, C), BF),
            pltpu.VMEM((9, C, 3 * C), BF),
            pltpu.VMEM((3, C, 9 * C), BF),
            pltpu.VMEM((FRAMES, ROWS, COLS, C), BF),
            pltpu.VMEM((FRAMES, ROWS, COLS, C), BF),
            pltpu.VMEM((FRAMES, ROWS, COLS, C), BF),
            pltpu.VMEM((3 * C, EARLY + 6 * AREA), BF),
            pltpu.VMEM((3 * C, 9 * C), F32),
            pltpu.VMEM((27 * C + 24, C), F32),
            pltpu.VMEM((8, C), F32),
            pltpu.VMEM((FRAMES, COLS, C), BF),
            pltpu.VMEM((2, ROWS, COLS, C), BF),
            pltpu.VMEM((2, COLS, C), BF),
            pltpu.VMEM((4, 2, 4, BLOCK, C), BF),
            pltpu.VMEM((4, 4, BLOCK, C), BF),
            pltpu.VMEM((4, 3, BLOCK, C), BF),
            pltpu.VMEM((4, 3, BLOCK, C), BF),
            pltpu.VMEM((4, BLOCK, C), F32),
            pltpu.VMEM((4, BLOCK, C), BF),
            pltpu.VMEM((8, BLOCK, C), BF),
            pltpu.VMEM((4, BLOCK, C), BF),
            dma((14,)),
            dma((2,)),
            dma((3,)),
            dma((3,)),
            dma((3,)),
            dma((3,)),
            dma((4,)),
            dma((4,)),
            dma((4, 3)),
            dma((4, 3)),
            dma((4, 2)),
            dma((8,)),
            dma((3,)),
            dma((4,)),
        ],
        compiler_params=pltpu.CompilerParams(
            collective_id=0, has_side_effects=True, vmem_limit_bytes=54000 * 1024
        ),
    )(activations, weights.reshape(9, 3, C, C), conv_bias.reshape(1, C), cotangent)
    block_out, grad_input, weight_grad, bias_grad = pl.pallas_call(
        hand_over,
        out_shape=[
            jax.ShapeDtypeStruct(shape, BF),
            jax.ShapeDtypeStruct(shape, BF),
            jax.ShapeDtypeStruct((SHARD, C), F32),
            jax.ShapeDtypeStruct((4,), F32),
        ],
        in_specs=[vmem, vmem, vmem, vmem],
        out_specs=[hbm, hbm, hbm, vmem],
        scratch_shapes=[dma((3,))],
        compiler_params=pltpu.CompilerParams(vmem_limit_bytes=8 * 2**20),
    )(*results)
    return block_out, grad_input, weight_grad, bias_grad


def solution(mesh):
    return jax.shard_map(
        body,
        mesh=mesh,
        in_specs=(P("dp", "tm", "tile", None, None), P(), P(), P("dp", "tm", "tile", None, None)),
        out_specs=(
            P("dp", "tm", "tile", None, None),
            P("dp", "tm", "tile", None, None),
            P("dp", None),
            P("dp"),
        ),
        check_vma=False,
    )
```

```python
import math

import jax
import jax.numpy as jnp
from jax import lax
from jax.experimental import pallas as pl
from jax.experimental.pallas import tpu as pltpu
from jax.sharding import PartitionSpec as P

F32 = jnp.float32
BF = jnp.bfloat16
MESH = pl.DeviceIdType.MESH

C = 128
FRAMES, ROWS, COLS = 8, 8, 32
AREA = ROWS * COLS
POSITIONS = FRAMES * AREA
TAPS_AB = [(a, b) for a in range(3) for b in range(3)]
SHARD = 108
BLOCK = 112
HALF = 64
HALF_AT = (0, BLOCK - HALF)
EARLY = 3 * AREA
SCALE = 1.0 / math.sqrt(524288.0)


def shift_columns(values, by):
    rows = values.shape[0]
    rolled = pltpu.roll(values, by % rows, 0)
    column = lax.broadcasted_iota(jnp.int32, values.shape, 0) & (COLS - 1)
    return jnp.where(column == (0 if by == 1 else COLS - 1), 0.0, rolled)


def forward_block(lhs, center, upstream, wf, bias):
    y = jnp.dot(lhs, wf[...].reshape(9 * C, 3 * C), preferred_element_type=F32)
    pre = y[:, C : 2 * C] + shift_columns(y[:, :C], 1) + shift_columns(y[:, 2 * C :], -1)
    pre = pre + bias[...]
    sig = 0.5 * jnp.tanh(0.5 * pre) + 0.5
    out = (center.astype(F32) + pre * sig).astype(BF)
    grad = upstream.astype(F32) * (sig * (1.0 + pre * (1.0 - sig)))
    return out, grad.astype(BF)


def keep_turned(grad, start, gt, bsum, first):
    part = jnp.sum(grad.reshape(AREA // 8, 8, C), axis=0)
    if first:
        bsum[...] = part
    else:
        bsum[...] += part
    turned = jnp.transpose(grad)
    lane = lax.broadcasted_iota(jnp.int32, (C, C), 1) & (COLS - 1)
    gt[C : 2 * C, start : start + AREA] = turned.astype(BF)
    for half in range(2):
        piece = turned[:, half * C : half * C + C]
        at = start + half * C
        ahead = jnp.where(lane == COLS - 1, 0.0, pltpu.roll(piece, C - 1, 1))
        behind = jnp.where(lane == 0, 0.0, pltpu.roll(piece, 1, 1))
        gt[0:C, at : at + C] = ahead.astype(BF)
        gt[2 * C : 3 * C, at : at + C] = behind.astype(BF)


def forward_frame(t, xp, wf, bias, ctv, bov, gp, gt, bsum, row, first):
    lhs = jnp.concatenate(
        [xp[t + a, b : b + ROWS].reshape(AREA, C) for a, b in TAPS_AB], axis=1
    )
    out, grad = forward_block(
        lhs, xp[t + 2, 1 : 1 + ROWS].reshape(AREA, C), ctv[t].reshape(AREA, C), wf, bias
    )
    bov[t] = out.reshape(ROWS, COLS, C)
    gp[t, 1 : 1 + ROWS] = grad.reshape(ROWS, COLS, C)
    at_row = lax.broadcasted_iota(jnp.int32, (AREA, C), 0) // COLS
    start = t * AREA if t < 2 else EARLY + (t - 2) * AREA
    keep_turned(jnp.where(at_row == row, 0.0, grad.astype(F32)), start, gt, bsum, first)


def forward_seam(xp, wf, bias, ctv, bov, gp, gt, bsum, row):
    lhs = jnp.concatenate(
        [xp[a : a + FRAMES, row + b].reshape(AREA, C) for a, b in TAPS_AB], axis=1
    )
    out, grad = forward_block(
        lhs, xp[2 : 2 + FRAMES, row + 1].reshape(AREA, C), ctv[:, row].reshape(AREA, C), wf, bias
    )
    bov[:, row] = out.reshape(FRAMES, COLS, C)
    gp[0:FRAMES, row + 1] = grad.reshape(FRAMES, COLS, C)
    keep_turned(grad.astype(F32), 2 * AREA, gt, bsum, False)


def early_taps(d, xp, gt, wacc):
    pairs = TAPS_AB[2 * d : 2 * d + 2]
    rhs = jnp.concatenate(
        [xp[a + 2 : a + FRAMES, b : b + ROWS].reshape(6 * AREA, C) for a, b in pairs], axis=1
    )
    lhs = gt[:, EARLY : EARLY + 6 * AREA]
    wacc[:, 2 * C * d : 2 * C * d + len(pairs) * C] = jnp.dot(
        lhs, rhs, preferred_element_type=F32
    )


def late_taps(d, xp, gt, wacc, dw, row):
    pairs = TAPS_AB[2 * d : 2 * d + 2]
    rhs = jnp.concatenate(
        [
            jnp.concatenate(
                [
                    xp[a : a + 2, b : b + ROWS].reshape(2 * AREA, C),
                    xp[a : a + FRAMES, row + b].reshape(AREA, C),
                ],
                axis=0,
            )
            for a, b in pairs
        ],
        axis=1,
    )
    out = jnp.dot(gt[:, :EARLY], rhs, preferred_element_type=F32)
    out = out + wacc[:, 2 * C * d : 2 * C * d + len(pairs) * C]
    for j in range(len(pairs)):
        for e in range(3):
            tap = (2 * d + j) * 3 + e
            dw[tap * C : tap * C + C] = jnp.transpose(
                out[e * C : e * C + C, j * C : j * C + C]
            )


def backward_frames(t, n, gp, wt, ctv, giv):
    rows = n * AREA
    lhs = jnp.concatenate(
        [gp[t + 2 - a : t + 2 - a + n, 2 - b : 2 - b + ROWS].reshape(rows, C) for a, b in TAPS_AB],
        axis=1,
    )
    y = lax.dot_general(
        lhs,
        wt[...].reshape(3 * C, 9 * C),
        (((1,), (1,)), ((), ())),
        preferred_element_type=F32,
    )
    out = y[:, C : 2 * C] + shift_columns(y[:, :C], -1) + shift_columns(y[:, 2 * C :], 1)
    out = out + ctv[t : t + n].reshape(rows, C).astype(F32)
    giv[t : t + n] = out.astype(BF).reshape(n, ROWS, COLS, C)


def kernel(
    act, ker, bias, cot, block_out, grad_input, weight_grad, bias_grad,
    xp, gp, wf, wt, ctv, bov, giv, gt, wacc, dw, bsum, hrow, hframes, hcorner,
    pk, cr, ys, yr, yown, zs, zr, fr,
    load_sem, out_sem, halo_send, halo_recv, ghalo_send, ghalo_recv,
    core_send, core_recv, y_send, y_recv, z_send, z_recv, f_send, f_recv,
):
    dp = lax.axis_index("dp")
    x = lax.axis_index("tm")
    zl = lax.axis_index("tile")
    core = lax.rem(dp, 2)
    y = lax.rem(dp // 2, 4)
    zh = dp // 8
    other = 1 - zl

    def at(zh_=None, y_=None, core_=None, x_=None, zl_=None):
        zh_ = zh if zh_ is None else zh_
        y_ = y if y_ is None else y_
        core_ = core if core_ is None else core_
        return {
            "dp": (zh_ * 4 + y_) * 2 + core_,
            "tm": x if x_ is None else x_,
            "tile": zl if zl_ is None else zl_,
        }

    def remote(src, dst, send, recv, where):
        return pltpu.make_async_remote_copy(
            src_ref=src, dst_ref=dst, send_sem=send, recv_sem=recv,
            device_id=where, device_id_type=MESH,
        )

    barrier = pltpu.get_barrier_semaphore()
    column = zh * 2 + zl
    group = x * 2 + zl
    partners = [at(zh_=lax.rem(zh + k, 4), zl_=side) for k in (2, 1, 3) for side in (zl, other)]
    partners += [at(x_=lax.rem(x + k, 4)) for k in (2, 1, 3)]
    partners += [at(x_=lax.rem(x + k, 4), zl_=other) for k in (2, 1, 3)]
    partners += [at(y_=lax.rem(y + k, 4)) for k in (2, 1, 3)]
    partners += [at(zl_=other)]
    partners += [at(core_=1 - core)]
    for partner in partners:
        pl.semaphore_signal(barrier, inc=1, device_id=partner, device_id_type=MESH)

    loads = [pltpu.make_async_copy(act.at[0], xp.at[2:10, 1:9], load_sem.at[0])]
    for e in range(3):
        loads.append(
            pltpu.make_async_copy(
                ker.at[:, e], wf.at[:, :, e * C : e * C + C], load_sem.at[1 + e]
            )
        )
    loads.append(pltpu.make_async_copy(cot.at[0], ctv, load_sem.at[4]))
    late = [
        pltpu.make_async_copy(ker.at[i], wt.at[:, :, i * C : i * C + C], load_sem.at[5 + i])
        for i in range(9)
    ]
    for load in loads:
        load.start()

    row_zeros = jnp.zeros((10, COLS, C), BF)
    xp[:, 0] = row_zeros
    xp[:, 9] = row_zeros
    gp[:, 9 * zl] = row_zeros
    xp[0:2, 1:9] = jnp.zeros((2, 8, COLS, C), BF)

    @pl.when(x == 3)
    def _():
        gp[8:10] = jnp.zeros((2, 10, COLS, C), BF)

    row = 7 * other
    into_row = 9 * zl
    recv_row = 9 * other
    later = jnp.minimum(x + 1, 3)
    halo_rows = remote(act.at[0, :, row], hrow, halo_send.at[0], halo_recv.at[0], at(zl_=other))
    halo_frames = remote(
        act.at[0, 6:8], hframes, halo_send.at[1], halo_recv.at[1], at(x_=later)
    )
    halo_corner = remote(
        act.at[0, 6:8, row], hcorner, halo_send.at[2], halo_recv.at[2], at(x_=later, zl_=other)
    )
    for load in loads:
        load.wait()
    for load in late:
        load.start()

    forward = (xp, wf, bias, ctv, bov, gp, gt, bsum, row)
    for t in range(2, 8):
        forward_frame(t, *forward, t == 2)
        if t == 3:
            pl.semaphore_wait(barrier, len(partners))

            @pl.when(x < 3)
            def _():
                halo_frames.start()
                halo_corner.start()

            halo_rows.start()

    for d in range(5):
        early_taps(d, xp, gt, wacc)

    halo_rows.wait_recv()
    xp[2:10, recv_row] = hrow[...]

    @pl.when(x > 0)
    def _():
        halo_frames.wait_recv()
        halo_corner.wait_recv()
        xp[0:2, 1:9] = hframes[...]
        xp[0:2, recv_row] = hcorner[...]

    forward_seam(*forward)
    forward_frame(0, *forward, False)
    forward_frame(1, *forward, False)
    outs = [pltpu.make_async_copy(bov, block_out.at[0], out_sem.at[0])]
    outs[-1].start()

    earlier = jnp.maximum(x - 1, 0)
    ghalo_rows = remote(
        gp.at[0:8, 1 + row], gp.at[0:8, into_row], ghalo_send.at[0], ghalo_recv.at[0],
        at(zl_=other),
    )
    ghalo_frames = remote(
        gp.at[0:2, 1:9], gp.at[8:10, 1:9], ghalo_send.at[1], ghalo_recv.at[1], at(x_=earlier)
    )
    ghalo_corner = remote(
        gp.at[0:2, 1 + row], gp.at[8:10, into_row], ghalo_send.at[2], ghalo_recv.at[2],
        at(x_=earlier, zl_=other),
    )

    total_bias = jnp.sum(bsum[...], axis=0, keepdims=True)
    bias_hi = total_bias.astype(BF).astype(F32)
    bias_lo = total_bias - bias_hi
    line = lax.broadcasted_iota(jnp.int32, (BLOCK, C), 0)
    tail = jnp.where(line == SHARD, bias_hi, jnp.where(line == SHARD + 1, bias_lo, 0.0))

    def pack(i):
        q, y_, core_ = i // 8, (i // 2) % 4, i % 2
        rows = jnp.where(line < SHARD, dw[SHARD * i : SHARD * i + BLOCK], tail)
        pk[q, core_, y_] = rows.astype(BF)

    def core_copy(q):
        return remote(
            pk.at[q, 1 - core], cr.at[q], core_send.at[q], core_recv.at[q], at(core_=1 - core)
        )

    def y_copy(q, k):
        return remote(
            ys.at[q, k - 1], yr.at[q, k - 1], y_send.at[q, k - 1], y_recv.at[q, k - 1],
            at(y_=lax.rem(y + k, 4)),
        )

    def y_stage(q):
        core_copy(q).wait_recv()
        for k in (2, 1, 3):
            to = lax.rem(y + k, 4)
            ys[q, k - 1] = (pk[q, core, to].astype(F32) + cr[q, to].astype(F32)).astype(BF)
            y_copy(q, k).start()
        yown[q] = pk[q, core, y].astype(F32) + cr[q, y].astype(F32)

    def z_copy(q, half):
        rows = pl.ds(HALF_AT[half], HALF)
        return remote(
            zs.at[q, rows], zr.at[column], z_send.at[q, half], z_recv.at[column],
            at(zh_=q, zl_=half),
        )

    def away(q, half):
        return jnp.logical_or(zh != q, zl != half)

    def z_stage(q):
        total = yown[q]
        for k in (1, 3, 2):
            y_copy(q, k).wait_recv()
            total = total + yr[q, k - 1].astype(F32)
        zs[q] = total.astype(BF)
        for half in range(2):

            @pl.when(away(q, half))
            def _():
                z_copy(q, half).start()

            @pl.when(jnp.logical_not(away(q, half)))
            def _():
                zr[column] = zs[q, HALF_AT[half] : HALF_AT[half] + HALF]

    packed, sent = 0, 0
    for d in range(5):
        late_taps(d, xp, gt, wacc, dw, row)
        ready = min(9, 2 * d + 2) * 3 * C
        while packed < 32 and SHARD * (packed + 1) <= ready:
            pack(packed)
            packed += 1
        while sent < 4 and packed >= 8 * (sent + 1):
            core_copy(sent).start()
            sent += 1
    @pl.when(x > 0)
    def _():
        ghalo_frames.start()
        ghalo_corner.start()

    ghalo_rows.start()

    for q in range(4):
        y_stage(q)

    for load in late:
        load.wait()
    remote(
        gp.at[0:8, 1 + row], gp.at[0:8, recv_row], ghalo_send.at[0], ghalo_recv.at[0],
        at(zl_=other),
    ).wait_recv()
    backward_frames(0, 2, gp, wt, ctv, giv)
    z_stage(0)
    backward_frames(2, 2, gp, wt, ctv, giv)
    z_stage(1)
    z_stage(2)
    z_stage(3)

    @pl.when(x < 3)
    def _():
        ghalo_frames.wait_recv()
        remote(
            gp.at[0:2, 1 + row], gp.at[8:10, recv_row], ghalo_send.at[2], ghalo_recv.at[2],
            at(x_=later, zl_=other),
        ).wait_recv()

    backward_frames(4, 2, gp, wt, ctv, giv)
    backward_frames(6, 2, gp, wt, ctv, giv)
    outs.append(pltpu.make_async_copy(giv, grad_input.at[0], out_sem.at[1]))
    outs[-1].start()

    for k in range(1, 8):
        slot = lax.rem(column + k, 8)
        remote(
            zs.at[0, 0:HALF], zr.at[slot], z_send.at[0, 1], z_recv.at[slot], at(zl_=other)
        ).wait_recv()
    total = zr[0].astype(F32)
    for slot in range(1, 8):
        total = total + zr[slot].astype(F32)
    fr[group] = total.astype(BF)

    def f_copy(k, slot):
        to = lax.rem(group + k, 8)
        return remote(
            fr.at[group], fr.at[slot], f_send.at[k - 1], f_recv.at[slot],
            at(x_=to // 2, zl_=lax.rem(to, 2)),
        )

    for k in (4, 5, 3, 2, 6, 1, 7):
        f_copy(k, group).start()
    for k in range(1, 8):
        f_copy(k, lax.rem(group + k, 8)).wait_recv()
    halves = []
    for half in range(2):
        total = fr[half].astype(F32)
        for g in range(1, 4):
            total = total + fr[2 * g + half].astype(F32)
        halves.append(total * SCALE)
    low = HALF - HALF_AT[1]
    end = SHARD - HALF_AT[1]
    weight_grad[0:HALF] = halves[0]
    weight_grad[HALF:SHARD] = halves[1][low:end]
    whole_bias = halves[1][end : end + 1] + halves[1][end + 1 : end + 2]
    whole_bias = jnp.broadcast_to(whole_bias, (8, C))
    bias_grad[...] = pltpu.roll(whole_bias, lax.rem(C - 4 * dp, C), 1)[0:1]

    halo_rows.wait_send()
    ghalo_rows.wait_send()

    @pl.when(x < 3)
    def _():
        halo_frames.wait_send()
        halo_corner.wait_send()

    @pl.when(x > 0)
    def _():
        ghalo_frames.wait_send()
        ghalo_corner.wait_send()

    for q in range(4):
        core_copy(q).wait_send()
        for k in range(1, 4):
            y_copy(q, k).wait_send()

        for half in range(2):

            @pl.when(away(q, half))
            def _():
                z_copy(q, half).wait_send()

    for k in range(1, 8):
        f_copy(k, group).wait_send()
    for out in outs:
        out.wait()


def hand_over(*refs):
    sem = refs[8]
    copies = [pltpu.make_async_copy(refs[i], refs[4 + i], sem.at[i]) for i in range(3)]
    for copy in copies:
        copy.start()
    refs[7][...] = refs[3][0, 0:4]
    for copy in copies:
        copy.wait()


def body(activations, weights, conv_bias, cotangent):
    hbm = pl.BlockSpec(memory_space=pltpu.HBM)
    anywhere = pl.BlockSpec(memory_space=pl.ANY)
    vmem = pl.BlockSpec(memory_space=pltpu.VMEM)
    dma = pltpu.SemaphoreType.DMA
    shape = (1, FRAMES, ROWS, COLS, C)
    results = pl.pallas_call(
        kernel,
        out_shape=[
            jax.ShapeDtypeStruct(shape, BF),
            jax.ShapeDtypeStruct(shape, BF),
            jax.ShapeDtypeStruct((SHARD, C), F32),
            jax.ShapeDtypeStruct((1, C), F32),
        ],
        in_specs=[hbm, hbm, vmem, hbm],
        out_specs=[anywhere, anywhere, vmem, vmem],
        scratch_shapes=[
            pltpu.VMEM((10, 10, COLS, C), BF),
            pltpu.VMEM((10, 10, COLS, C), BF),
            pltpu.VMEM((9, C, 3 * C), BF),
            pltpu.VMEM((3, C, 9 * C), BF),
            pltpu.VMEM((FRAMES, ROWS, COLS, C), BF),
            pltpu.VMEM((FRAMES, ROWS, COLS, C), BF),
            pltpu.VMEM((FRAMES, ROWS, COLS, C), BF),
            pltpu.VMEM((3 * C, EARLY + 6 * AREA), BF),
            pltpu.VMEM((3 * C, 9 * C), F32),
            pltpu.VMEM((27 * C + 24, C), F32),
            pltpu.VMEM((8, C), F32),
            pltpu.VMEM((FRAMES, COLS, C), BF),
            pltpu.VMEM((2, ROWS, COLS, C), BF),
            pltpu.VMEM((2, COLS, C), BF),
            pltpu.VMEM((4, 2, 4, BLOCK, C), BF),
            pltpu.VMEM((4, 4, BLOCK, C), BF),
            pltpu.VMEM((4, 3, BLOCK, C), BF),
            pltpu.VMEM((4, 3, BLOCK, C), BF),
            pltpu.VMEM((4, BLOCK, C), F32),
            pltpu.VMEM((4, BLOCK, C), BF),
            pltpu.VMEM((8, HALF, C), BF),
            pltpu.VMEM((8, HALF, C), BF),
            dma((14,)),
            dma((2,)),
            dma((3,)),
            dma((3,)),
            dma((3,)),
            dma((3,)),
            dma((4,)),
            dma((4,)),
            dma((4, 3)),
            dma((4, 3)),
            dma((4, 2)),
            dma((8,)),
            dma((7,)),
            dma((8,)),
        ],
        compiler_params=pltpu.CompilerParams(
            collective_id=0, has_side_effects=True, vmem_limit_bytes=54000 * 1024
        ),
    )(activations, weights.reshape(9, 3, C, C), conv_bias.reshape(1, C), cotangent)
    block_out, grad_input, weight_grad, bias_grad = pl.pallas_call(
        hand_over,
        out_shape=[
            jax.ShapeDtypeStruct(shape, BF),
            jax.ShapeDtypeStruct(shape, BF),
            jax.ShapeDtypeStruct((SHARD, C), F32),
            jax.ShapeDtypeStruct((4,), F32),
        ],
        in_specs=[vmem, vmem, vmem, vmem],
        out_specs=[hbm, hbm, hbm, vmem],
        scratch_shapes=[dma((3,))],
        compiler_params=pltpu.CompilerParams(vmem_limit_bytes=8 * 2**20),
    )(*results)
    return block_out, grad_input, weight_grad, bias_grad


def solution(mesh):
    return jax.shard_map(
        body,
        mesh=mesh,
        in_specs=(P("dp", "tm", "tile", None, None), P(), P(), P("dp", "tm", "tile", None, None)),
        out_specs=(
            P("dp", "tm", "tile", None, None),
            P("dp", "tm", "tile", None, None),
            P("dp", None),
            P("dp"),
        ),
        check_vma=False,
    )
```

```python
import math

import jax
import jax.numpy as jnp
from jax import lax
from jax.experimental import pallas as pl
from jax.experimental.pallas import tpu as pltpu
from jax.sharding import PartitionSpec as P

F32 = jnp.float32
BF = jnp.bfloat16
MESH = pl.DeviceIdType.MESH

C = 128
FRAMES, ROWS, COLS = 8, 8, 32
AREA = ROWS * COLS
POSITIONS = FRAMES * AREA
TAPS_AB = [(a, b) for a in range(3) for b in range(3)]
SHARD = 108
BLOCK = 112
HALF = 64
HALF_AT = (0, BLOCK - HALF)
EARLY = 3 * AREA
SCALE = 1.0 / math.sqrt(524288.0)


def shift_columns(values, by):
    rows = values.shape[0]
    rolled = pltpu.roll(values, by % rows, 0)
    column = lax.broadcasted_iota(jnp.int32, values.shape, 0) & (COLS - 1)
    return jnp.where(column == (0 if by == 1 else COLS - 1), 0.0, rolled)


def forward_block(lhs, center, upstream, wf, bias):
    y = jnp.dot(lhs, wf[...].reshape(9 * C, 3 * C), preferred_element_type=F32)
    pre = y[:, C : 2 * C] + shift_columns(y[:, :C], 1) + shift_columns(y[:, 2 * C :], -1)
    pre = pre + bias[...]
    sig = 0.5 * jnp.tanh(0.5 * pre) + 0.5
    out = (center.astype(F32) + pre * sig).astype(BF)
    grad = upstream.astype(F32) * (sig * (1.0 + pre * (1.0 - sig)))
    return out, grad.astype(BF)


def keep_turned(grad, start, gt, bsum, first):
    part = jnp.sum(grad.reshape(AREA // 8, 8, C), axis=0)
    if first:
        bsum[...] = part
    else:
        bsum[...] += part
    turned = jnp.transpose(grad)
    lane = lax.broadcasted_iota(jnp.int32, (C, C), 1) & (COLS - 1)
    gt[C : 2 * C, start : start + AREA] = turned.astype(BF)
    for half in range(2):
        piece = turned[:, half * C : half * C + C]
        at = start + half * C
        ahead = jnp.where(lane == COLS - 1, 0.0, pltpu.roll(piece, C - 1, 1))
        behind = jnp.where(lane == 0, 0.0, pltpu.roll(piece, 1, 1))
        gt[0:C, at : at + C] = ahead.astype(BF)
        gt[2 * C : 3 * C, at : at + C] = behind.astype(BF)


def forward_frame(t, xp, wf, bias, ctv, bov, gp, gt, bsum, row, first):
    lhs = jnp.concatenate(
        [xp[t + a, b : b + ROWS].reshape(AREA, C) for a, b in TAPS_AB], axis=1
    )
    out, grad = forward_block(
        lhs, xp[t + 2, 1 : 1 + ROWS].reshape(AREA, C), ctv[t].reshape(AREA, C), wf, bias
    )
    bov[t] = out.reshape(ROWS, COLS, C)
    gp[t, 1 : 1 + ROWS] = grad.reshape(ROWS, COLS, C)
    at_row = lax.broadcasted_iota(jnp.int32, (AREA, C), 0) // COLS
    start = t * AREA if t < 2 else EARLY + (t - 2) * AREA
    keep_turned(jnp.where(at_row == row, 0.0, grad.astype(F32)), start, gt, bsum, first)


def forward_seam(xp, wf, bias, ctv, bov, gp, gt, bsum, row):
    lhs = jnp.concatenate(
        [xp[a : a + FRAMES, row + b].reshape(AREA, C) for a, b in TAPS_AB], axis=1
    )
    out, grad = forward_block(
        lhs, xp[2 : 2 + FRAMES, row + 1].reshape(AREA, C), ctv[:, row].reshape(AREA, C), wf, bias
    )
    bov[:, row] = out.reshape(FRAMES, COLS, C)
    gp[0:FRAMES, row + 1] = grad.reshape(FRAMES, COLS, C)
    keep_turned(grad.astype(F32), 2 * AREA, gt, bsum, False)


def early_taps(d, xp, gt, wacc):
    pairs = TAPS_AB[2 * d : 2 * d + 2]
    rhs = jnp.concatenate(
        [xp[a + 2 : a + FRAMES, b : b + ROWS].reshape(6 * AREA, C) for a, b in pairs], axis=1
    )
    lhs = gt[:, EARLY : EARLY + 6 * AREA]
    wacc[:, 2 * C * d : 2 * C * d + len(pairs) * C] = jnp.dot(
        lhs, rhs, preferred_element_type=F32
    )


def late_taps(d, xp, gt, wacc, dw, row):
    pairs = TAPS_AB[2 * d : 2 * d + 2]
    rhs = jnp.concatenate(
        [
            jnp.concatenate(
                [
                    xp[a : a + 2, b : b + ROWS].reshape(2 * AREA, C),
                    xp[a : a + FRAMES, row + b].reshape(AREA, C),
                ],
                axis=0,
            )
            for a, b in pairs
        ],
        axis=1,
    )
    out = jnp.dot(gt[:, :EARLY], rhs, preferred_element_type=F32)
    out = out + wacc[:, 2 * C * d : 2 * C * d + len(pairs) * C]
    for j in range(len(pairs)):
        for e in range(3):
            tap = (2 * d + j) * 3 + e
            dw[tap * C : tap * C + C] = jnp.transpose(
                out[e * C : e * C + C, j * C : j * C + C]
            )


def backward_frames(t, n, gp, wt, ctv, giv):
    rows = n * AREA
    lhs = jnp.concatenate(
        [gp[t + 2 - a : t + 2 - a + n, 2 - b : 2 - b + ROWS].reshape(rows, C) for a, b in TAPS_AB],
        axis=1,
    )
    y = lax.dot_general(
        lhs,
        wt[...].reshape(3 * C, 9 * C),
        (((1,), (1,)), ((), ())),
        preferred_element_type=F32,
    )
    out = y[:, C : 2 * C] + shift_columns(y[:, :C], -1) + shift_columns(y[:, 2 * C :], 1)
    out = out + ctv[t : t + n].reshape(rows, C).astype(F32)
    giv[t : t + n] = out.astype(BF).reshape(n, ROWS, COLS, C)


def kernel(
    act, ker, bias, cot, block_out, grad_input, weight_grad, bias_grad,
    xp, gp, wf, wt, ctv, bov, giv, gt, wacc, dw, bsum, hrow, hframes, hcorner,
    pk, cr, ys, yr, yown, zs, zr, fr,
    load_sem, out_sem, halo_send, halo_recv, ghalo_send, ghalo_recv,
    core_send, core_recv, y_send, y_recv, z_send, z_recv, f_send, f_recv,
):
    dp = lax.axis_index("dp")
    x = lax.axis_index("tm")
    zl = lax.axis_index("tile")
    core = lax.rem(dp, 2)
    y = lax.rem(dp // 2, 4)
    zh = dp // 8
    other = 1 - zl

    def at(zh_=None, y_=None, core_=None, x_=None, zl_=None):
        zh_ = zh if zh_ is None else zh_
        y_ = y if y_ is None else y_
        core_ = core if core_ is None else core_
        return {
            "dp": (zh_ * 4 + y_) * 2 + core_,
            "tm": x if x_ is None else x_,
            "tile": zl if zl_ is None else zl_,
        }

    def remote(src, dst, send, recv, where):
        return pltpu.make_async_remote_copy(
            src_ref=src, dst_ref=dst, send_sem=send, recv_sem=recv,
            device_id=where, device_id_type=MESH,
        )

    loads = []
    for f in range(4):
        part = pl.ds(2 * f, 2)
        loads.append(
            pltpu.make_async_copy(
                act.at[0, part], xp.at[2 + 2 * f : 4 + 2 * f, 1:9], load_sem.at[f]
            )
        )
    for a in range(3):
        for e in range(3):
            loads.append(
                pltpu.make_async_copy(
                    ker.at[3 * a : 3 * a + 3, e],
                    wf.at[3 * a : 3 * a + 3, :, e * C : e * C + C],
                    load_sem.at[4 + 3 * a + e],
                )
            )
    for f in range(4):
        part = pl.ds(2 * f, 2)
        loads.append(pltpu.make_async_copy(cot.at[0, part], ctv.at[part], load_sem.at[13 + f]))
    late = [
        pltpu.make_async_copy(ker.at[i], wt.at[:, :, i * C : i * C + C], load_sem.at[17 + i])
        for i in range(9)
    ]
    for load in loads:
        load.start()

    barrier = pltpu.get_barrier_semaphore()
    column = zh * 2 + zl
    group = x * 2 + zl
    partners = [at(zh_=lax.rem(zh + k, 4), zl_=side) for k in (2, 1, 3) for side in (zl, other)]
    partners += [at(x_=lax.rem(x + k, 4)) for k in (2, 1, 3)]
    partners += [at(x_=lax.rem(x + k, 4), zl_=other) for k in (2, 1, 3)]
    partners += [at(y_=lax.rem(y + k, 4)) for k in (2, 1, 3)]
    partners += [at(zl_=other)]
    partners += [at(core_=1 - core)]
    for partner in partners:
        pl.semaphore_signal(barrier, inc=1, device_id=partner, device_id_type=MESH)

    row_zeros = jnp.zeros((10, COLS, C), BF)
    xp[:, 0] = row_zeros
    xp[:, 9] = row_zeros
    gp[:, 9 * zl] = row_zeros
    xp[0:2, 1:9] = jnp.zeros((2, 8, COLS, C), BF)

    @pl.when(x == 3)
    def _():
        gp[8:10] = jnp.zeros((2, 10, COLS, C), BF)

    row = 7 * other
    into_row = 9 * zl
    recv_row = 9 * other
    later = jnp.minimum(x + 1, 3)
    halo_rows = remote(act.at[0, :, row], hrow, halo_send.at[0], halo_recv.at[0], at(zl_=other))
    halo_frames = remote(
        act.at[0, 6:8], hframes, halo_send.at[1], halo_recv.at[1], at(x_=later)
    )
    halo_corner = remote(
        act.at[0, 6:8, row], hcorner, halo_send.at[2], halo_recv.at[2], at(x_=later, zl_=other)
    )
    for load in loads:
        load.wait()
    for load in late:
        load.start()

    forward = (xp, wf, bias, ctv, bov, gp, gt, bsum, row)
    for t in range(2, 8):
        forward_frame(t, *forward, t == 2)
        if t == 3:
            pl.semaphore_wait(barrier, len(partners))

            @pl.when(x < 3)
            def _():
                halo_frames.start()
                halo_corner.start()

            halo_rows.start()

    for d in range(5):
        early_taps(d, xp, gt, wacc)

    halo_rows.wait_recv()
    xp[2:10, recv_row] = hrow[...]

    @pl.when(x > 0)
    def _():
        halo_frames.wait_recv()
        halo_corner.wait_recv()
        xp[0:2, 1:9] = hframes[...]
        xp[0:2, recv_row] = hcorner[...]

    forward_seam(*forward)
    forward_frame(0, *forward, False)
    forward_frame(1, *forward, False)
    outs = [pltpu.make_async_copy(bov, block_out.at[0], out_sem.at[0])]
    outs[-1].start()

    earlier = jnp.maximum(x - 1, 0)
    ghalo_rows = remote(
        gp.at[0:8, 1 + row], gp.at[0:8, into_row], ghalo_send.at[0], ghalo_recv.at[0],
        at(zl_=other),
    )
    ghalo_frames = remote(
        gp.at[0:2, 1:9], gp.at[8:10, 1:9], ghalo_send.at[1], ghalo_recv.at[1], at(x_=earlier)
    )
    ghalo_corner = remote(
        gp.at[0:2, 1 + row], gp.at[8:10, into_row], ghalo_send.at[2], ghalo_recv.at[2],
        at(x_=earlier, zl_=other),
    )

    total_bias = jnp.sum(bsum[...], axis=0, keepdims=True)
    bias_hi = total_bias.astype(BF).astype(F32)
    bias_lo = total_bias - bias_hi
    line = lax.broadcasted_iota(jnp.int32, (BLOCK, C), 0)
    tail = jnp.where(line == SHARD, bias_hi, jnp.where(line == SHARD + 1, bias_lo, 0.0))

    def pack(i):
        q, y_, core_ = i // 8, (i // 2) % 4, i % 2
        rows = jnp.where(line < SHARD, dw[SHARD * i : SHARD * i + BLOCK], tail)
        pk[q, core_, y_] = rows.astype(BF)

    def core_copy(q):
        return remote(
            pk.at[q, 1 - core], cr.at[q], core_send.at[q], core_recv.at[q], at(core_=1 - core)
        )

    def y_copy(q, k):
        return remote(
            ys.at[q, k - 1], yr.at[q, k - 1], y_send.at[q, k - 1], y_recv.at[q, k - 1],
            at(y_=lax.rem(y + k, 4)),
        )

    def y_stage(q):
        core_copy(q).wait_recv()
        for k in (2, 1, 3):
            to = lax.rem(y + k, 4)
            ys[q, k - 1] = (pk[q, core, to].astype(F32) + cr[q, to].astype(F32)).astype(BF)
            y_copy(q, k).start()
        yown[q] = pk[q, core, y].astype(F32) + cr[q, y].astype(F32)

    def z_copy(q, half):
        rows = pl.ds(HALF_AT[half], HALF)
        return remote(
            zs.at[q, rows], zr.at[column], z_send.at[q, half], z_recv.at[column],
            at(zh_=q, zl_=half),
        )

    def away(q, half):
        return jnp.logical_or(zh != q, zl != half)

    def z_stage(q):
        total = yown[q]
        for k in (1, 3, 2):
            y_copy(q, k).wait_recv()
            total = total + yr[q, k - 1].astype(F32)
        zs[q] = total.astype(BF)
        for half in range(2):

            @pl.when(away(q, half))
            def _():
                z_copy(q, half).start()

            @pl.when(jnp.logical_not(away(q, half)))
            def _():
                zr[column] = zs[q, HALF_AT[half] : HALF_AT[half] + HALF]

    packed, sent = 0, 0
    for d in range(5):
        late_taps(d, xp, gt, wacc, dw, row)
        ready = min(9, 2 * d + 2) * 3 * C
        while packed < 32 and SHARD * (packed + 1) <= ready:
            pack(packed)
            packed += 1
        while sent < 4 and packed >= 8 * (sent + 1):
            core_copy(sent).start()
            sent += 1
    @pl.when(x > 0)
    def _():
        ghalo_frames.start()
        ghalo_corner.start()

    ghalo_rows.start()

    for q in range(4):
        y_stage(q)

    for load in late:
        load.wait()
    remote(
        gp.at[0:8, 1 + row], gp.at[0:8, recv_row], ghalo_send.at[0], ghalo_recv.at[0],
        at(zl_=other),
    ).wait_recv()
    backward_frames(0, 2, gp, wt, ctv, giv)
    z_stage(0)
    backward_frames(2, 2, gp, wt, ctv, giv)
    z_stage(1)
    z_stage(2)
    z_stage(3)

    @pl.when(x < 3)
    def _():
        ghalo_frames.wait_recv()
        remote(
            gp.at[0:2, 1 + row], gp.at[8:10, recv_row], ghalo_send.at[2], ghalo_recv.at[2],
            at(x_=later, zl_=other),
        ).wait_recv()

    backward_frames(4, 2, gp, wt, ctv, giv)
    backward_frames(6, 2, gp, wt, ctv, giv)
    outs.append(pltpu.make_async_copy(giv, grad_input.at[0], out_sem.at[1]))
    outs[-1].start()

    for k in range(1, 8):
        slot = lax.rem(column + k, 8)
        remote(
            zs.at[0, 0:HALF], zr.at[slot], z_send.at[0, 1], z_recv.at[slot], at(zl_=other)
        ).wait_recv()
    total = zr[0].astype(F32)
    for slot in range(1, 8):
        total = total + zr[slot].astype(F32)
    fr[group] = total.astype(BF)

    def f_copy(k, slot):
        to = lax.rem(group + k, 8)
        return remote(
            fr.at[group], fr.at[slot], f_send.at[k - 1], f_recv.at[slot],
            at(x_=to // 2, zl_=lax.rem(to, 2)),
        )

    for k in (4, 5, 3, 2, 6, 1, 7):
        f_copy(k, group).start()
    for k in range(1, 8):
        f_copy(k, lax.rem(group + k, 8)).wait_recv()
    halves = []
    for half in range(2):
        total = fr[half].astype(F32)
        for g in range(1, 4):
            total = total + fr[2 * g + half].astype(F32)
        halves.append(total * SCALE)
    low = HALF - HALF_AT[1]
    end = SHARD - HALF_AT[1]
    weight_grad[0:HALF] = halves[0]
    weight_grad[HALF:SHARD] = halves[1][low:end]
    whole_bias = halves[1][end : end + 1] + halves[1][end + 1 : end + 2]
    whole_bias = jnp.broadcast_to(whole_bias, (8, C))
    bias_grad[...] = pltpu.roll(whole_bias, lax.rem(C - 4 * dp, C), 1)[0:1]

    halo_rows.wait_send()
    ghalo_rows.wait_send()

    @pl.when(x < 3)
    def _():
        halo_frames.wait_send()
        halo_corner.wait_send()

    @pl.when(x > 0)
    def _():
        ghalo_frames.wait_send()
        ghalo_corner.wait_send()

    for q in range(4):
        core_copy(q).wait_send()
        for k in range(1, 4):
            y_copy(q, k).wait_send()

        for half in range(2):

            @pl.when(away(q, half))
            def _():
                z_copy(q, half).wait_send()

    for k in range(1, 8):
        f_copy(k, group).wait_send()
    for out in outs:
        out.wait()


def hand_over(*refs):
    sem = refs[8]
    parts = [(refs[2], refs[6])]
    for i in range(2):
        for f in range(0, FRAMES, 2):
            parts.append((refs[i].at[0, f : f + 2], refs[4 + i].at[0, f : f + 2]))
    copies = [pltpu.make_async_copy(a, b, sem.at[n]) for n, (a, b) in enumerate(parts)]
    for copy in copies:
        copy.start()
    refs[7][...] = refs[3][0, 0:4]
    for copy in copies:
        copy.wait()


def body(activations, weights, conv_bias, cotangent):
    hbm = pl.BlockSpec(memory_space=pltpu.HBM)
    anywhere = pl.BlockSpec(memory_space=pl.ANY)
    vmem = pl.BlockSpec(memory_space=pltpu.VMEM)
    dma = pltpu.SemaphoreType.DMA
    shape = (1, FRAMES, ROWS, COLS, C)
    results = pl.pallas_call(
        kernel,
        out_shape=[
            jax.ShapeDtypeStruct(shape, BF),
            jax.ShapeDtypeStruct(shape, BF),
            jax.ShapeDtypeStruct((SHARD, C), F32),
            jax.ShapeDtypeStruct((1, C), F32),
        ],
        in_specs=[hbm, hbm, vmem, hbm],
        out_specs=[anywhere, anywhere, vmem, vmem],
        scratch_shapes=[
            pltpu.VMEM((10, 10, COLS, C), BF),
            pltpu.VMEM((10, 10, COLS, C), BF),
            pltpu.VMEM((9, C, 3 * C), BF),
            pltpu.VMEM((3, C, 9 * C), BF),
            pltpu.VMEM((FRAMES, ROWS, COLS, C), BF),
            pltpu.VMEM((FRAMES, ROWS, COLS, C), BF),
            pltpu.VMEM((FRAMES, ROWS, COLS, C), BF),
            pltpu.VMEM((3 * C, EARLY + 6 * AREA), BF),
            pltpu.VMEM((3 * C, 9 * C), F32),
            pltpu.VMEM((27 * C + 24, C), F32),
            pltpu.VMEM((8, C), F32),
            pltpu.VMEM((FRAMES, COLS, C), BF),
            pltpu.VMEM((2, ROWS, COLS, C), BF),
            pltpu.VMEM((2, COLS, C), BF),
            pltpu.VMEM((4, 2, 4, BLOCK, C), BF),
            pltpu.VMEM((4, 4, BLOCK, C), BF),
            pltpu.VMEM((4, 3, BLOCK, C), BF),
            pltpu.VMEM((4, 3, BLOCK, C), BF),
            pltpu.VMEM((4, BLOCK, C), F32),
            pltpu.VMEM((4, BLOCK, C), BF),
            pltpu.VMEM((8, HALF, C), BF),
            pltpu.VMEM((8, HALF, C), BF),
            dma((26,)),
            dma((2,)),
            dma((3,)),
            dma((3,)),
            dma((3,)),
            dma((3,)),
            dma((4,)),
            dma((4,)),
            dma((4, 3)),
            dma((4, 3)),
            dma((4, 2)),
            dma((8,)),
            dma((7,)),
            dma((8,)),
        ],
        compiler_params=pltpu.CompilerParams(
            collective_id=0, has_side_effects=True, vmem_limit_bytes=54000 * 1024
        ),
    )(activations, weights.reshape(9, 3, C, C), conv_bias.reshape(1, C), cotangent)
    block_out, grad_input, weight_grad, bias_grad = pl.pallas_call(
        hand_over,
        out_shape=[
            jax.ShapeDtypeStruct(shape, BF),
            jax.ShapeDtypeStruct(shape, BF),
            jax.ShapeDtypeStruct((SHARD, C), F32),
            jax.ShapeDtypeStruct((4,), F32),
        ],
        in_specs=[vmem, vmem, vmem, vmem],
        out_specs=[hbm, hbm, hbm, vmem],
        scratch_shapes=[dma((9,))],
        compiler_params=pltpu.CompilerParams(vmem_limit_bytes=8 * 2**20),
    )(*results)
    return block_out, grad_input, weight_grad, bias_grad


def solution(mesh):
    return jax.shard_map(
        body,
        mesh=mesh,
        in_specs=(P("dp", "tm", "tile", None, None), P(), P(), P("dp", "tm", "tile", None, None)),
        out_specs=(
            P("dp", "tm", "tile", None, None),
            P("dp", "tm", "tile", None, None),
            P("dp", None),
            P("dp"),
        ),
        check_vma=False,
    )
```

```python
import math

import jax
import jax.numpy as jnp
from jax import lax
from jax.experimental import pallas as pl
from jax.experimental.pallas import tpu as pltpu
from jax.sharding import PartitionSpec as P

F32 = jnp.float32
BF = jnp.bfloat16
MESH = pl.DeviceIdType.MESH

C = 128
FRAMES, ROWS, COLS = 8, 8, 32
AREA = ROWS * COLS
POSITIONS = FRAMES * AREA
TAPS_AB = [(a, b) for a in range(3) for b in range(3)]
SHARD = 108
BLOCK = 112
HALF = 64
HALF_AT = (0, BLOCK - HALF)
EARLY = 3 * AREA
SCALE = 1.0 / math.sqrt(524288.0)


def shift_columns(values, by):
    rows = values.shape[0]
    rolled = pltpu.roll(values, by % rows, 0)
    column = lax.broadcasted_iota(jnp.int32, values.shape, 0) & (COLS - 1)
    return jnp.where(column == (0 if by == 1 else COLS - 1), 0.0, rolled)


def forward_block(lhs, center, upstream, wf, bias):
    y = jnp.dot(lhs, wf[...].reshape(9 * C, 3 * C), preferred_element_type=F32)
    pre = y[:, C : 2 * C] + shift_columns(y[:, :C], 1) + shift_columns(y[:, 2 * C :], -1)
    pre = pre + bias[...]
    sig = 0.5 * jnp.tanh(0.5 * pre) + 0.5
    out = (center.astype(F32) + pre * sig).astype(BF)
    grad = upstream.astype(F32) * (sig * (1.0 + pre * (1.0 - sig)))
    return out, grad.astype(BF)


def keep_turned(grad, start, gt, bsum, first):
    part = jnp.sum(grad.reshape(AREA // 8, 8, C), axis=0)
    if first:
        bsum[...] = part
    else:
        bsum[...] += part
    turned = jnp.transpose(grad)
    lane = lax.broadcasted_iota(jnp.int32, (C, C), 1) & (COLS - 1)
    gt[C : 2 * C, start : start + AREA] = turned.astype(BF)
    for half in range(2):
        piece = turned[:, half * C : half * C + C]
        at = start + half * C
        ahead = jnp.where(lane == COLS - 1, 0.0, pltpu.roll(piece, C - 1, 1))
        behind = jnp.where(lane == 0, 0.0, pltpu.roll(piece, 1, 1))
        gt[0:C, at : at + C] = ahead.astype(BF)
        gt[2 * C : 3 * C, at : at + C] = behind.astype(BF)


def forward_frame(t, xp, wf, bias, ctv, bov, gp, gt, bsum, row, first):
    lhs = jnp.concatenate(
        [xp[t + a, b : b + ROWS].reshape(AREA, C) for a, b in TAPS_AB], axis=1
    )
    out, grad = forward_block(
        lhs, xp[t + 2, 1 : 1 + ROWS].reshape(AREA, C), ctv[t].reshape(AREA, C), wf, bias
    )
    bov[t] = out.reshape(ROWS, COLS, C)
    gp[t, 1 : 1 + ROWS] = grad.reshape(ROWS, COLS, C)
    at_row = lax.broadcasted_iota(jnp.int32, (AREA, C), 0) // COLS
    start = t * AREA if t < 2 else EARLY + (t - 2) * AREA
    keep_turned(jnp.where(at_row == row, 0.0, grad.astype(F32)), start, gt, bsum, first)


def forward_seam(xp, wf, bias, ctv, bov, gp, gt, bsum, row):
    lhs = jnp.concatenate(
        [xp[a : a + FRAMES, row + b].reshape(AREA, C) for a, b in TAPS_AB], axis=1
    )
    out, grad = forward_block(
        lhs, xp[2 : 2 + FRAMES, row + 1].reshape(AREA, C), ctv[:, row].reshape(AREA, C), wf, bias
    )
    bov[:, row] = out.reshape(FRAMES, COLS, C)
    gp[0:FRAMES, row + 1] = grad.reshape(FRAMES, COLS, C)
    keep_turned(grad.astype(F32), 2 * AREA, gt, bsum, False)


def early_taps(d, xp, gt, wacc):
    pairs = TAPS_AB[2 * d : 2 * d + 2]
    rhs = jnp.concatenate(
        [xp[a + 2 : a + FRAMES, b : b + ROWS].reshape(6 * AREA, C) for a, b in pairs], axis=1
    )
    lhs = gt[:, EARLY : EARLY + 6 * AREA]
    wacc[:, 2 * C * d : 2 * C * d + len(pairs) * C] = jnp.dot(
        lhs, rhs, preferred_element_type=F32
    )


def late_taps(d, xp, gt, wacc, dw, row):
    pairs = TAPS_AB[2 * d : 2 * d + 2]
    rhs = jnp.concatenate(
        [
            jnp.concatenate(
                [
                    xp[a : a + 2, b : b + ROWS].reshape(2 * AREA, C),
                    xp[a : a + FRAMES, row + b].reshape(AREA, C),
                ],
                axis=0,
            )
            for a, b in pairs
        ],
        axis=1,
    )
    out = jnp.dot(gt[:, :EARLY], rhs, preferred_element_type=F32)
    out = out + wacc[:, 2 * C * d : 2 * C * d + len(pairs) * C]
    for j in range(len(pairs)):
        for e in range(3):
            tap = (2 * d + j) * 3 + e
            dw[tap * C : tap * C + C] = jnp.transpose(
                out[e * C : e * C + C, j * C : j * C + C]
            )


def backward_frames(t, n, gp, wt, ctv, giv):
    rows = n * AREA
    lhs = jnp.concatenate(
        [gp[t + 2 - a : t + 2 - a + n, 2 - b : 2 - b + ROWS].reshape(rows, C) for a, b in TAPS_AB],
        axis=1,
    )
    y = lax.dot_general(
        lhs,
        wt[...].reshape(3 * C, 9 * C),
        (((1,), (1,)), ((), ())),
        preferred_element_type=F32,
    )
    out = y[:, C : 2 * C] + shift_columns(y[:, :C], -1) + shift_columns(y[:, 2 * C :], 1)
    out = out + ctv[t : t + n].reshape(rows, C).astype(F32)
    giv[t : t + n] = out.astype(BF).reshape(n, ROWS, COLS, C)


def kernel(
    act, ker, bias, cot, block_out, grad_input, weight_grad, bias_grad,
    xp, gp, wf, wt, ctv, bov, giv, gt, wacc, dw, bsum, hrow, hframes, hcorner,
    pk, cr, ys, yr, yown, zs, zr, fr,
    load_sem, out_sem, halo_send, halo_recv, ghalo_send, ghalo_recv,
    core_send, core_recv, y_send, y_recv, z_send, z_recv, f_send, f_recv,
):
    dp = lax.axis_index("dp")
    x = lax.axis_index("tm")
    zl = lax.axis_index("tile")
    core = lax.rem(dp, 2)
    y = lax.rem(dp // 2, 4)
    zh = dp // 8
    other = 1 - zl

    def at(zh_=None, y_=None, core_=None, x_=None, zl_=None):
        zh_ = zh if zh_ is None else zh_
        y_ = y if y_ is None else y_
        core_ = core if core_ is None else core_
        return {
            "dp": (zh_ * 4 + y_) * 2 + core_,
            "tm": x if x_ is None else x_,
            "tile": zl if zl_ is None else zl_,
        }

    def remote(src, dst, send, recv, where):
        return pltpu.make_async_remote_copy(
            src_ref=src, dst_ref=dst, send_sem=send, recv_sem=recv,
            device_id=where, device_id_type=MESH,
        )

    loads = []
    for f in range(4):
        part = pl.ds(2 * f, 2)
        loads.append(
            pltpu.make_async_copy(
                act.at[0, part], xp.at[2 + 2 * f : 4 + 2 * f, 1:9], load_sem.at[f]
            )
        )
    for a in range(3):
        for e in range(3):
            loads.append(
                pltpu.make_async_copy(
                    ker.at[3 * a : 3 * a + 3, e],
                    wf.at[3 * a : 3 * a + 3, :, e * C : e * C + C],
                    load_sem.at[4 + 3 * a + e],
                )
            )
    for f in range(4):
        part = pl.ds(2 * f, 2)
        loads.append(pltpu.make_async_copy(cot.at[0, part], ctv.at[part], load_sem.at[13 + f]))
    late = [
        pltpu.make_async_copy(ker.at[i], wt.at[:, :, i * C : i * C + C], load_sem.at[17 + i])
        for i in range(9)
    ]
    for load in loads:
        load.start()

    barrier = pltpu.get_barrier_semaphore()
    column = zh * 2 + zl
    group = x * 2 + zl
    partners = [at(zh_=lax.rem(zh + k, 4), zl_=side) for k in (2, 1, 3) for side in (zl, other)]
    partners += [at(x_=lax.rem(x + k, 4)) for k in (2, 1, 3)]
    partners += [at(x_=lax.rem(x + k, 4), zl_=other) for k in (2, 1, 3)]
    partners += [at(y_=lax.rem(y + k, 4)) for k in (2, 1, 3)]
    partners += [at(zl_=other)]
    partners += [at(core_=1 - core)]
    for partner in partners:
        pl.semaphore_signal(barrier, inc=1, device_id=partner, device_id_type=MESH)

    row_zeros = jnp.zeros((10, COLS, C), BF)
    xp[:, 0] = row_zeros
    xp[:, 9] = row_zeros
    gp[:, 9 * zl] = row_zeros
    xp[0:2, 1:9] = jnp.zeros((2, 8, COLS, C), BF)

    @pl.when(x == 3)
    def _():
        gp[8:10] = jnp.zeros((2, 10, COLS, C), BF)

    row = 7 * other
    into_row = 9 * zl
    recv_row = 9 * other
    later = jnp.minimum(x + 1, 3)
    halo_rows = remote(act.at[0, :, row], hrow, halo_send.at[0], halo_recv.at[0], at(zl_=other))
    halo_frames = remote(
        act.at[0, 6:8], hframes, halo_send.at[1], halo_recv.at[1], at(x_=later)
    )
    halo_corner = remote(
        act.at[0, 6:8, row], hcorner, halo_send.at[2], halo_recv.at[2], at(x_=later, zl_=other)
    )
    for load in loads:
        load.wait()
    for load in late:
        load.start()

    forward = (xp, wf, bias, ctv, bov, gp, gt, bsum, row)
    for t in range(2, 8):
        forward_frame(t, *forward, t == 2)
        if t == 3:
            pl.semaphore_wait(barrier, len(partners))

            @pl.when(x < 3)
            def _():
                halo_frames.start()
                halo_corner.start()

            halo_rows.start()

    for d in range(5):
        early_taps(d, xp, gt, wacc)

    halo_rows.wait_recv()
    xp[2:10, recv_row] = hrow[...]

    @pl.when(x > 0)
    def _():
        halo_frames.wait_recv()
        halo_corner.wait_recv()
        xp[0:2, 1:9] = hframes[...]
        xp[0:2, recv_row] = hcorner[...]

    forward_seam(*forward)
    forward_frame(0, *forward, False)
    forward_frame(1, *forward, False)
    outs = [pltpu.make_async_copy(bov, block_out.at[0], out_sem.at[0])]
    outs[-1].start()

    earlier = jnp.maximum(x - 1, 0)
    ghalo_rows = remote(
        gp.at[0:8, 1 + row], gp.at[0:8, into_row], ghalo_send.at[0], ghalo_recv.at[0],
        at(zl_=other),
    )
    ghalo_frames = remote(
        gp.at[0:2, 1:9], gp.at[8:10, 1:9], ghalo_send.at[1], ghalo_recv.at[1], at(x_=earlier)
    )
    ghalo_corner = remote(
        gp.at[0:2, 1 + row], gp.at[8:10, into_row], ghalo_send.at[2], ghalo_recv.at[2],
        at(x_=earlier, zl_=other),
    )

    total_bias = jnp.sum(bsum[...], axis=0, keepdims=True)
    bias_hi = total_bias.astype(BF).astype(F32)
    bias_lo = total_bias - bias_hi
    line = lax.broadcasted_iota(jnp.int32, (BLOCK, C), 0)
    tail = jnp.where(line == SHARD, bias_hi, jnp.where(line == SHARD + 1, bias_lo, 0.0))

    def pack(i):
        q, y_, core_ = i // 8, (i // 2) % 4, i % 2
        rows = jnp.where(line < SHARD, dw[SHARD * i : SHARD * i + BLOCK], tail)
        pk[q, core_, y_] = rows.astype(BF)

    def core_copy(q):
        return remote(
            pk.at[q, 1 - core], cr.at[q], core_send.at[q], core_recv.at[q], at(core_=1 - core)
        )

    def y_copy(q, k):
        return remote(
            ys.at[q, k - 1], yr.at[q, k - 1], y_send.at[q, k - 1], y_recv.at[q, k - 1],
            at(y_=lax.rem(y + k, 4)),
        )

    def y_stage(q):
        core_copy(q).wait_recv()
        for k in (2, 1, 3):
            to = lax.rem(y + k, 4)
            ys[q, k - 1] = (pk[q, core, to].astype(F32) + cr[q, to].astype(F32)).astype(BF)
            y_copy(q, k).start()
        yown[q] = pk[q, core, y].astype(F32) + cr[q, y].astype(F32)

    def z_copy(q, half):
        rows = pl.ds(HALF_AT[half], HALF)
        return remote(
            zs.at[q, rows], zr.at[column], z_send.at[q, half], z_recv.at[column],
            at(zh_=q, zl_=half),
        )

    def away(q, half):
        return jnp.logical_or(zh != q, zl != half)

    def z_stage(q):
        total = yown[q]
        for k in (1, 3, 2):
            y_copy(q, k).wait_recv()
            total = total + yr[q, k - 1].astype(F32)
        zs[q] = total.astype(BF)
        for half in range(2):

            @pl.when(away(q, half))
            def _():
                z_copy(q, half).start()

            @pl.when(jnp.logical_not(away(q, half)))
            def _():
                zr[column] = zs[q, HALF_AT[half] : HALF_AT[half] + HALF]

    packed, sent = 0, 0
    for d in range(5):
        late_taps(d, xp, gt, wacc, dw, row)
        ready = min(9, 2 * d + 2) * 3 * C
        while packed < 32 and SHARD * (packed + 1) <= ready:
            pack(packed)
            packed += 1
        while sent < 4 and packed >= 8 * (sent + 1):
            core_copy(sent).start()
            sent += 1
    @pl.when(x > 0)
    def _():
        ghalo_frames.start()
        ghalo_corner.start()

    ghalo_rows.start()

    for q in range(4):
        y_stage(q)

    for q in range(4):
        z_stage(q)

    def give(t):
        outs.append(
            pltpu.make_async_copy(
                giv.at[t : t + 2], grad_input.at[0, t : t + 2], out_sem.at[1 + t // 2]
            )
        )
        outs[-1].start()

    for load in late:
        load.wait()
    remote(
        gp.at[0:8, 1 + row], gp.at[0:8, recv_row], ghalo_send.at[0], ghalo_recv.at[0],
        at(zl_=other),
    ).wait_recv()
    for t in (0, 2, 4):
        backward_frames(t, 2, gp, wt, ctv, giv)
        give(t)

    for k in range(1, 8):
        slot = lax.rem(column + k, 8)
        remote(
            zs.at[0, 0:HALF], zr.at[slot], z_send.at[0, 1], z_recv.at[slot], at(zl_=other)
        ).wait_recv()
    total = zr[0].astype(F32)
    for slot in range(1, 8):
        total = total + zr[slot].astype(F32)
    fr[group] = total.astype(BF)

    def f_copy(k, slot):
        to = lax.rem(group + k, 8)
        return remote(
            fr.at[group], fr.at[slot], f_send.at[k - 1], f_recv.at[slot],
            at(x_=to // 2, zl_=lax.rem(to, 2)),
        )

    for k in (4, 5, 3, 2, 6, 1, 7):
        f_copy(k, group).start()

    @pl.when(x < 3)
    def _():
        ghalo_frames.wait_recv()
        remote(
            gp.at[0:2, 1 + row], gp.at[8:10, recv_row], ghalo_send.at[2], ghalo_recv.at[2],
            at(x_=later, zl_=other),
        ).wait_recv()

    backward_frames(6, 2, gp, wt, ctv, giv)
    give(6)

    for k in range(1, 8):
        f_copy(k, lax.rem(group + k, 8)).wait_recv()
    halves = []
    for half in range(2):
        total = fr[half].astype(F32)
        for g in range(1, 4):
            total = total + fr[2 * g + half].astype(F32)
        halves.append(total * SCALE)
    low = HALF - HALF_AT[1]
    end = SHARD - HALF_AT[1]
    weight_grad[0:HALF] = halves[0]
    weight_grad[HALF:SHARD] = halves[1][low:end]
    whole_bias = halves[1][end : end + 1] + halves[1][end + 1 : end + 2]
    whole_bias = jnp.broadcast_to(whole_bias, (8, C))
    bias_grad[...] = pltpu.roll(whole_bias, lax.rem(C - 4 * dp, C), 1)[0:1]

    halo_rows.wait_send()
    ghalo_rows.wait_send()

    @pl.when(x < 3)
    def _():
        halo_frames.wait_send()
        halo_corner.wait_send()

    @pl.when(x > 0)
    def _():
        ghalo_frames.wait_send()
        ghalo_corner.wait_send()

    for q in range(4):
        core_copy(q).wait_send()
        for k in range(1, 4):
            y_copy(q, k).wait_send()

        for half in range(2):

            @pl.when(away(q, half))
            def _():
                z_copy(q, half).wait_send()

    for k in range(1, 8):
        f_copy(k, group).wait_send()
    for out in outs:
        out.wait()


def hand_over(*refs):
    sem = refs[8]
    parts = [(refs[2], refs[6])]
    for i in range(2):
        for f in range(0, FRAMES, 2):
            parts.append((refs[i].at[0, f : f + 2], refs[4 + i].at[0, f : f + 2]))
    copies = [pltpu.make_async_copy(a, b, sem.at[n]) for n, (a, b) in enumerate(parts)]
    for copy in copies:
        copy.start()
    refs[7][...] = refs[3][0, 0:4]
    for copy in copies:
        copy.wait()


def body(activations, weights, conv_bias, cotangent):
    hbm = pl.BlockSpec(memory_space=pltpu.HBM)
    anywhere = pl.BlockSpec(memory_space=pl.ANY)
    vmem = pl.BlockSpec(memory_space=pltpu.VMEM)
    dma = pltpu.SemaphoreType.DMA
    shape = (1, FRAMES, ROWS, COLS, C)
    results = pl.pallas_call(
        kernel,
        out_shape=[
            jax.ShapeDtypeStruct(shape, BF),
            jax.ShapeDtypeStruct(shape, BF),
            jax.ShapeDtypeStruct((SHARD, C), F32),
            jax.ShapeDtypeStruct((1, C), F32),
        ],
        in_specs=[hbm, hbm, vmem, hbm],
        out_specs=[anywhere, anywhere, vmem, vmem],
        scratch_shapes=[
            pltpu.VMEM((10, 10, COLS, C), BF),
            pltpu.VMEM((10, 10, COLS, C), BF),
            pltpu.VMEM((9, C, 3 * C), BF),
            pltpu.VMEM((3, C, 9 * C), BF),
            pltpu.VMEM((FRAMES, ROWS, COLS, C), BF),
            pltpu.VMEM((FRAMES, ROWS, COLS, C), BF),
            pltpu.VMEM((FRAMES, ROWS, COLS, C), BF),
            pltpu.VMEM((3 * C, EARLY + 6 * AREA), BF),
            pltpu.VMEM((3 * C, 9 * C), F32),
            pltpu.VMEM((27 * C + 24, C), F32),
            pltpu.VMEM((8, C), F32),
            pltpu.VMEM((FRAMES, COLS, C), BF),
            pltpu.VMEM((2, ROWS, COLS, C), BF),
            pltpu.VMEM((2, COLS, C), BF),
            pltpu.VMEM((4, 2, 4, BLOCK, C), BF),
            pltpu.VMEM((4, 4, BLOCK, C), BF),
            pltpu.VMEM((4, 3, BLOCK, C), BF),
            pltpu.VMEM((4, 3, BLOCK, C), BF),
            pltpu.VMEM((4, BLOCK, C), F32),
            pltpu.VMEM((4, BLOCK, C), BF),
            pltpu.VMEM((8, HALF, C), BF),
            pltpu.VMEM((8, HALF, C), BF),
            dma((26,)),
            dma((5,)),
            dma((3,)),
            dma((3,)),
            dma((3,)),
            dma((3,)),
            dma((4,)),
            dma((4,)),
            dma((4, 3)),
            dma((4, 3)),
            dma((4, 2)),
            dma((8,)),
            dma((7,)),
            dma((8,)),
        ],
        compiler_params=pltpu.CompilerParams(
            collective_id=0, has_side_effects=True, vmem_limit_bytes=54000 * 1024
        ),
    )(activations, weights.reshape(9, 3, C, C), conv_bias.reshape(1, C), cotangent)
    block_out, grad_input, weight_grad, bias_grad = pl.pallas_call(
        hand_over,
        out_shape=[
            jax.ShapeDtypeStruct(shape, BF),
            jax.ShapeDtypeStruct(shape, BF),
            jax.ShapeDtypeStruct((SHARD, C), F32),
            jax.ShapeDtypeStruct((4,), F32),
        ],
        in_specs=[vmem, vmem, vmem, vmem],
        out_specs=[hbm, hbm, hbm, vmem],
        scratch_shapes=[dma((9,))],
        compiler_params=pltpu.CompilerParams(vmem_limit_bytes=8 * 2**20),
    )(*results)
    return block_out, grad_input, weight_grad, bias_grad


def solution(mesh):
    return jax.shard_map(
        body,
        mesh=mesh,
        in_specs=(P("dp", "tm", "tile", None, None), P(), P(), P("dp", "tm", "tile", None, None)),
        out_specs=(
            P("dp", "tm", "tile", None, None),
            P("dp", "tm", "tile", None, None),
            P("dp", None),
            P("dp"),
        ),
        check_vma=False,
    )
```

```python
import math

import jax
import jax.numpy as jnp
from jax import lax
from jax.experimental import pallas as pl
from jax.experimental.pallas import tpu as pltpu
from jax.sharding import PartitionSpec as P

F32 = jnp.float32
BF = jnp.bfloat16
MESH = pl.DeviceIdType.MESH

C = 128
FRAMES, ROWS, COLS = 8, 8, 32
AREA = ROWS * COLS
POSITIONS = FRAMES * AREA
TAPS_AB = [(a, b) for a in range(3) for b in range(3)]
SHARD = 108
BLOCK = 112
HALF = 64
HALF_AT = (0, BLOCK - HALF)
EARLY = 3 * AREA
SCALE = 1.0 / math.sqrt(524288.0)


def shift_columns(values, by):
    rows = values.shape[0]
    rolled = pltpu.roll(values, by % rows, 0)
    column = lax.broadcasted_iota(jnp.int32, values.shape, 0) & (COLS - 1)
    return jnp.where(column == (0 if by == 1 else COLS - 1), 0.0, rolled)


def forward_block(lhs, center, upstream, wf, bias):
    y = jnp.dot(lhs, wf[...].reshape(9 * C, 3 * C), preferred_element_type=F32)
    pre = y[:, C : 2 * C] + shift_columns(y[:, :C], 1) + shift_columns(y[:, 2 * C :], -1)
    pre = pre + bias[...]
    sig = 0.5 * jnp.tanh(0.5 * pre) + 0.5
    out = (center.astype(F32) + pre * sig).astype(BF)
    grad = upstream.astype(F32) * (sig * (1.0 + pre * (1.0 - sig)))
    return out, grad.astype(BF)


def keep_turned(grad, start, gt, bsum, first):
    part = jnp.sum(grad.reshape(AREA // 8, 8, C), axis=0)
    if first:
        bsum[...] = part
    else:
        bsum[...] += part
    turned = jnp.transpose(grad)
    lane = lax.broadcasted_iota(jnp.int32, (C, C), 1) & (COLS - 1)
    gt[C : 2 * C, start : start + AREA] = turned.astype(BF)
    for half in range(2):
        piece = turned[:, half * C : half * C + C]
        at = start + half * C
        ahead = jnp.where(lane == COLS - 1, 0.0, pltpu.roll(piece, C - 1, 1))
        behind = jnp.where(lane == 0, 0.0, pltpu.roll(piece, 1, 1))
        gt[0:C, at : at + C] = ahead.astype(BF)
        gt[2 * C : 3 * C, at : at + C] = behind.astype(BF)


def forward_frame(t, xp, wf, bias, ctv, bov, gp, gt, bsum, row, first):
    lhs = jnp.concatenate(
        [xp[t + a, b : b + ROWS].reshape(AREA, C) for a, b in TAPS_AB], axis=1
    )
    out, grad = forward_block(
        lhs, xp[t + 2, 1 : 1 + ROWS].reshape(AREA, C), ctv[t].reshape(AREA, C), wf, bias
    )
    bov[t] = out.reshape(ROWS, COLS, C)
    gp[t, 1 : 1 + ROWS] = grad.reshape(ROWS, COLS, C)
    at_row = lax.broadcasted_iota(jnp.int32, (AREA, C), 0) // COLS
    start = t * AREA if t < 2 else EARLY + (t - 2) * AREA
    keep_turned(jnp.where(at_row == row, 0.0, grad.astype(F32)), start, gt, bsum, first)


def forward_seam(xp, wf, bias, ctv, bov, gp, gt, bsum, row):
    lhs = jnp.concatenate(
        [xp[a : a + FRAMES, row + b].reshape(AREA, C) for a, b in TAPS_AB], axis=1
    )
    out, grad = forward_block(
        lhs, xp[2 : 2 + FRAMES, row + 1].reshape(AREA, C), ctv[:, row].reshape(AREA, C), wf, bias
    )
    bov[:, row] = out.reshape(FRAMES, COLS, C)
    gp[0:FRAMES, row + 1] = grad.reshape(FRAMES, COLS, C)
    keep_turned(grad.astype(F32), 2 * AREA, gt, bsum, False)


def early_taps(d, xp, gt, wacc):
    pairs = TAPS_AB[2 * d : 2 * d + 2]
    rhs = jnp.concatenate(
        [xp[a + 2 : a + FRAMES, b : b + ROWS].reshape(6 * AREA, C) for a, b in pairs], axis=1
    )
    lhs = gt[:, EARLY : EARLY + 6 * AREA]
    wacc[:, 2 * C * d : 2 * C * d + len(pairs) * C] = jnp.dot(
        lhs, rhs, preferred_element_type=F32
    )


def late_taps(d, xp, gt, wacc, dw, row):
    pairs = TAPS_AB[2 * d : 2 * d + 2]
    rhs = jnp.concatenate(
        [
            jnp.concatenate(
                [
                    xp[a : a + 2, b : b + ROWS].reshape(2 * AREA, C),
                    xp[a : a + FRAMES, row + b].reshape(AREA, C),
                ],
                axis=0,
            )
            for a, b in pairs
        ],
        axis=1,
    )
    out = jnp.dot(gt[:, :EARLY], rhs, preferred_element_type=F32)
    out = out + wacc[:, 2 * C * d : 2 * C * d + len(pairs) * C]
    for j in range(len(pairs)):
        for e in range(3):
            tap = (2 * d + j) * 3 + e
            dw[tap * C : tap * C + C] = jnp.transpose(
                out[e * C : e * C + C, j * C : j * C + C]
            )


def backward_frames(t, n, gp, wt, ctv, giv):
    rows = n * AREA
    lhs = jnp.concatenate(
        [gp[t + 2 - a : t + 2 - a + n, 2 - b : 2 - b + ROWS].reshape(rows, C) for a, b in TAPS_AB],
        axis=1,
    )
    y = lax.dot_general(
        lhs,
        wt[...].reshape(3 * C, 9 * C),
        (((1,), (1,)), ((), ())),
        preferred_element_type=F32,
    )
    out = y[:, C : 2 * C] + shift_columns(y[:, :C], -1) + shift_columns(y[:, 2 * C :], 1)
    out = out + ctv[t : t + n].reshape(rows, C).astype(F32)
    giv[t : t + n] = out.astype(BF).reshape(n, ROWS, COLS, C)


def kernel(
    act, ker, bias, cot, block_out, grad_input, weight_grad, bias_grad,
    xp, gp, wf, wt, ctv, bov, giv, gt, wacc, dw, bsum, hrow, hframes, hcorner,
    pk, cr, ys, yr, yown, zs, zr, fr,
    load_sem, out_sem, halo_send, halo_recv, ghalo_send, ghalo_recv,
    core_send, core_recv, y_send, y_recv, z_send, z_recv, f_send, f_recv,
):
    dp = lax.axis_index("dp")
    x = lax.axis_index("tm")
    zl = lax.axis_index("tile")
    core = lax.rem(dp, 2)
    y = lax.rem(dp // 2, 4)
    zh = dp // 8
    other = 1 - zl

    def at(zh_=None, y_=None, core_=None, x_=None, zl_=None):
        zh_ = zh if zh_ is None else zh_
        y_ = y if y_ is None else y_
        core_ = core if core_ is None else core_
        return {
            "dp": (zh_ * 4 + y_) * 2 + core_,
            "tm": x if x_ is None else x_,
            "tile": zl if zl_ is None else zl_,
        }

    def remote(src, dst, send, recv, where):
        return pltpu.make_async_remote_copy(
            src_ref=src, dst_ref=dst, send_sem=send, recv_sem=recv,
            device_id=where, device_id_type=MESH,
        )

    loads = []
    for f in range(4):
        part = pl.ds(2 * f, 2)
        loads.append(
            pltpu.make_async_copy(
                act.at[0, part], xp.at[2 + 2 * f : 4 + 2 * f, 1:9], load_sem.at[f]
            )
        )
    for a in range(3):
        for e in range(3):
            loads.append(
                pltpu.make_async_copy(
                    ker.at[3 * a : 3 * a + 3, e],
                    wf.at[3 * a : 3 * a + 3, :, e * C : e * C + C],
                    load_sem.at[4 + 3 * a + e],
                )
            )
    for f in range(4):
        part = pl.ds(2 * f, 2)
        loads.append(pltpu.make_async_copy(cot.at[0, part], ctv.at[part], load_sem.at[13 + f]))
    late = [
        pltpu.make_async_copy(ker.at[i], wt.at[:, :, i * C : i * C + C], load_sem.at[17 + i])
        for i in range(9)
    ]
    for load in loads:
        load.start()

    barrier = pltpu.get_barrier_semaphore()
    column = zh * 2 + zl
    group = x * 2 + zl
    partners = [at(zh_=lax.rem(zh + k, 4), zl_=side) for k in (2, 1, 3) for side in (zl, other)]
    partners += [at(x_=lax.rem(x + k, 4)) for k in (2, 1, 3)]
    partners += [at(x_=lax.rem(x + k, 4), zl_=other) for k in (2, 1, 3)]
    partners += [at(y_=lax.rem(y + k, 4)) for k in (2, 1, 3)]
    partners += [at(zl_=other)]
    partners += [at(core_=1 - core)]
    for partner in partners:
        pl.semaphore_signal(barrier, inc=1, device_id=partner, device_id_type=MESH)

    row_zeros = jnp.zeros((10, COLS, C), BF)
    xp[:, 0] = row_zeros
    xp[:, 9] = row_zeros
    gp[:, 9 * zl] = row_zeros
    xp[0:2, 1:9] = jnp.zeros((2, 8, COLS, C), BF)

    @pl.when(x == 3)
    def _():
        gp[8:10] = jnp.zeros((2, 10, COLS, C), BF)

    row = 7 * other
    into_row = 9 * zl
    recv_row = 9 * other
    later = jnp.minimum(x + 1, 3)
    halo_rows = remote(act.at[0, :, row], hrow, halo_send.at[0], halo_recv.at[0], at(zl_=other))
    halo_frames = remote(
        act.at[0, 6:8], hframes, halo_send.at[1], halo_recv.at[1], at(x_=later)
    )
    halo_corner = remote(
        act.at[0, 6:8, row], hcorner, halo_send.at[2], halo_recv.at[2], at(x_=later, zl_=other)
    )
    for load in loads:
        load.wait()
    for load in late:
        load.start()

    forward = (xp, wf, bias, ctv, bov, gp, gt, bsum, row)
    for t in range(2, 8):
        forward_frame(t, *forward, t == 2)
        if t == 3:
            pl.semaphore_wait(barrier, len(partners))

            @pl.when(x < 3)
            def _():
                halo_frames.start()
                halo_corner.start()

            halo_rows.start()

    for d in range(5):
        early_taps(d, xp, gt, wacc)

    halo_rows.wait_recv()
    xp[2:10, recv_row] = hrow[...]

    @pl.when(x > 0)
    def _():
        halo_frames.wait_recv()
        halo_corner.wait_recv()
        xp[0:2, 1:9] = hframes[...]
        xp[0:2, recv_row] = hcorner[...]

    forward_seam(*forward)
    forward_frame(0, *forward, False)
    forward_frame(1, *forward, False)
    outs = [pltpu.make_async_copy(bov, block_out.at[0], out_sem.at[0])]
    outs[-1].start()

    earlier = jnp.maximum(x - 1, 0)
    ghalo_rows = remote(
        gp.at[0:8, 1 + row], gp.at[0:8, into_row], ghalo_send.at[0], ghalo_recv.at[0],
        at(zl_=other),
    )
    ghalo_frames = remote(
        gp.at[0:2, 1:9], gp.at[8:10, 1:9], ghalo_send.at[1], ghalo_recv.at[1], at(x_=earlier)
    )
    ghalo_corner = remote(
        gp.at[0:2, 1 + row], gp.at[8:10, into_row], ghalo_send.at[2], ghalo_recv.at[2],
        at(x_=earlier, zl_=other),
    )

    total_bias = jnp.sum(bsum[...], axis=0, keepdims=True)
    bias_hi = total_bias.astype(BF).astype(F32)
    bias_lo = total_bias - bias_hi
    line = lax.broadcasted_iota(jnp.int32, (BLOCK, C), 0)
    tail = jnp.where(line == SHARD, bias_hi, jnp.where(line == SHARD + 1, bias_lo, 0.0))

    def pack(i):
        q, y_, core_ = i // 8, (i // 2) % 4, i % 2
        rows = jnp.where(line < SHARD, dw[SHARD * i : SHARD * i + BLOCK], tail)
        pk[q, core_, y_] = rows.astype(BF)

    def core_copy(q):
        return remote(
            pk.at[q, 1 - core], cr.at[q], core_send.at[q], core_recv.at[q], at(core_=1 - core)
        )

    def y_copy(q, k):
        return remote(
            ys.at[q, k - 1], yr.at[q, k - 1], y_send.at[q, k - 1], y_recv.at[q, k - 1],
            at(y_=lax.rem(y + k, 4)),
        )

    def y_stage(q):
        core_copy(q).wait_recv()
        for k in (2, 1, 3):
            to = lax.rem(y + k, 4)
            ys[q, k - 1] = (pk[q, core, to].astype(F32) + cr[q, to].astype(F32)).astype(BF)
            y_copy(q, k).start()
        yown[q] = pk[q, core, y].astype(F32) + cr[q, y].astype(F32)

    def z_copy(q, half):
        rows = pl.ds(HALF_AT[half], HALF)
        return remote(
            zs.at[q, rows], zr.at[column], z_send.at[q, half], z_recv.at[column],
            at(zh_=q, zl_=half),
        )

    def away(q, half):
        return jnp.logical_or(zh != q, zl != half)

    def z_stage(q):
        total = yown[q]
        for k in (1, 3, 2):
            y_copy(q, k).wait_recv()
            total = total + yr[q, k - 1].astype(F32)
        zs[q] = total.astype(BF)
        for half in range(2):

            @pl.when(away(q, half))
            def _():
                z_copy(q, half).start()

            @pl.when(jnp.logical_not(away(q, half)))
            def _():
                zr[column] = zs[q, HALF_AT[half] : HALF_AT[half] + HALF]

    packed, sent = 0, 0
    for d in range(5):
        late_taps(d, xp, gt, wacc, dw, row)
        ready = min(9, 2 * d + 2) * 3 * C
        while packed < 32 and SHARD * (packed + 1) <= ready:
            pack(packed)
            packed += 1
        while sent < 4 and packed >= 8 * (sent + 1):
            core_copy(sent).start()
            sent += 1
    @pl.when(x > 0)
    def _():
        ghalo_frames.start()
        ghalo_corner.start()

    ghalo_rows.start()

    for q in range(4):
        y_stage(q)

    z_stage(0)

    def give(t):
        outs.append(
            pltpu.make_async_copy(
                giv.at[t : t + 2], grad_input.at[0, t : t + 2], out_sem.at[1 + t // 2]
            )
        )
        outs[-1].start()

    for load in late:
        load.wait()
    remote(
        gp.at[0:8, 1 + row], gp.at[0:8, recv_row], ghalo_send.at[0], ghalo_recv.at[0],
        at(zl_=other),
    ).wait_recv()
    backward_frames(0, 2, gp, wt, ctv, giv)
    give(0)
    z_stage(1)
    backward_frames(2, 2, gp, wt, ctv, giv)
    give(2)
    z_stage(2)
    z_stage(3)
    backward_frames(4, 2, gp, wt, ctv, giv)
    give(4)

    for k in range(1, 8):
        slot = lax.rem(column + k, 8)
        remote(
            zs.at[0, 0:HALF], zr.at[slot], z_send.at[0, 1], z_recv.at[slot], at(zl_=other)
        ).wait_recv()
    total = zr[0].astype(F32)
    for slot in range(1, 8):
        total = total + zr[slot].astype(F32)
    fr[group] = total.astype(BF)

    def f_copy(k, slot):
        to = lax.rem(group + k, 8)
        return remote(
            fr.at[group], fr.at[slot], f_send.at[k - 1], f_recv.at[slot],
            at(x_=to // 2, zl_=lax.rem(to, 2)),
        )

    for k in (4, 5, 3, 2, 6, 1, 7):
        f_copy(k, group).start()

    @pl.when(x < 3)
    def _():
        ghalo_frames.wait_recv()
        remote(
            gp.at[0:2, 1 + row], gp.at[8:10, recv_row], ghalo_send.at[2], ghalo_recv.at[2],
            at(x_=later, zl_=other),
        ).wait_recv()

    backward_frames(6, 2, gp, wt, ctv, giv)
    give(6)

    for k in range(1, 8):
        f_copy(k, lax.rem(group + k, 8)).wait_recv()
    halves = []
    for half in range(2):
        total = fr[half].astype(F32)
        for g in range(1, 4):
            total = total + fr[2 * g + half].astype(F32)
        halves.append(total * SCALE)
    low = HALF - HALF_AT[1]
    end = SHARD - HALF_AT[1]
    weight_grad[0:HALF] = halves[0]
    weight_grad[HALF:SHARD] = halves[1][low:end]
    whole_bias = halves[1][end : end + 1] + halves[1][end + 1 : end + 2]
    whole_bias = jnp.broadcast_to(whole_bias, (8, C))
    bias_grad[...] = pltpu.roll(whole_bias, lax.rem(C - 4 * dp, C), 1)[0:1]

    halo_rows.wait_send()
    ghalo_rows.wait_send()

    @pl.when(x < 3)
    def _():
        halo_frames.wait_send()
        halo_corner.wait_send()

    @pl.when(x > 0)
    def _():
        ghalo_frames.wait_send()
        ghalo_corner.wait_send()

    for q in range(4):
        core_copy(q).wait_send()
        for k in range(1, 4):
            y_copy(q, k).wait_send()

        for half in range(2):

            @pl.when(away(q, half))
            def _():
                z_copy(q, half).wait_send()

    for k in range(1, 8):
        f_copy(k, group).wait_send()
    for out in outs:
        out.wait()


def hand_over(*refs):
    sem = refs[8]
    parts = [(refs[2], refs[6])]
    for i in range(2):
        for f in range(0, FRAMES, 2):
            parts.append((refs[i].at[0, f : f + 2], refs[4 + i].at[0, f : f + 2]))
    copies = [pltpu.make_async_copy(a, b, sem.at[n]) for n, (a, b) in enumerate(parts)]
    for copy in copies:
        copy.start()
    refs[7][...] = refs[3][0, 0:4]
    for copy in copies:
        copy.wait()


def body(activations, weights, conv_bias, cotangent):
    hbm = pl.BlockSpec(memory_space=pltpu.HBM)
    anywhere = pl.BlockSpec(memory_space=pl.ANY)
    vmem = pl.BlockSpec(memory_space=pltpu.VMEM)
    dma = pltpu.SemaphoreType.DMA
    shape = (1, FRAMES, ROWS, COLS, C)
    results = pl.pallas_call(
        kernel,
        out_shape=[
            jax.ShapeDtypeStruct(shape, BF),
            jax.ShapeDtypeStruct(shape, BF),
            jax.ShapeDtypeStruct((SHARD, C), F32),
            jax.ShapeDtypeStruct((1, C), F32),
        ],
        in_specs=[hbm, hbm, vmem, hbm],
        out_specs=[anywhere, anywhere, vmem, vmem],
        scratch_shapes=[
            pltpu.VMEM((10, 10, COLS, C), BF),
            pltpu.VMEM((10, 10, COLS, C), BF),
            pltpu.VMEM((9, C, 3 * C), BF),
            pltpu.VMEM((3, C, 9 * C), BF),
            pltpu.VMEM((FRAMES, ROWS, COLS, C), BF),
            pltpu.VMEM((FRAMES, ROWS, COLS, C), BF),
            pltpu.VMEM((FRAMES, ROWS, COLS, C), BF),
            pltpu.VMEM((3 * C, EARLY + 6 * AREA), BF),
            pltpu.VMEM((3 * C, 9 * C), F32),
            pltpu.VMEM((27 * C + 24, C), F32),
            pltpu.VMEM((8, C), F32),
            pltpu.VMEM((FRAMES, COLS, C), BF),
            pltpu.VMEM((2, ROWS, COLS, C), BF),
            pltpu.VMEM((2, COLS, C), BF),
            pltpu.VMEM((4, 2, 4, BLOCK, C), BF),
            pltpu.VMEM((4, 4, BLOCK, C), BF),
            pltpu.VMEM((4, 3, BLOCK, C), BF),
            pltpu.VMEM((4, 3, BLOCK, C), BF),
            pltpu.VMEM((4, BLOCK, C), F32),
            pltpu.VMEM((4, BLOCK, C), BF),
            pltpu.VMEM((8, HALF, C), BF),
            pltpu.VMEM((8, HALF, C), BF),
            dma((26,)),
            dma((5,)),
            dma((3,)),
            dma((3,)),
            dma((3,)),
            dma((3,)),
            dma((4,)),
            dma((4,)),
            dma((4, 3)),
            dma((4, 3)),
            dma((4, 2)),
            dma((8,)),
            dma((7,)),
            dma((8,)),
        ],
        compiler_params=pltpu.CompilerParams(
            collective_id=0, has_side_effects=True, vmem_limit_bytes=54000 * 1024
        ),
    )(activations, weights.reshape(9, 3, C, C), conv_bias.reshape(1, C), cotangent)
    block_out, grad_input, weight_grad, bias_grad = pl.pallas_call(
        hand_over,
        out_shape=[
            jax.ShapeDtypeStruct(shape, BF),
            jax.ShapeDtypeStruct(shape, BF),
            jax.ShapeDtypeStruct((SHARD, C), F32),
            jax.ShapeDtypeStruct((4,), F32),
        ],
        in_specs=[vmem, vmem, vmem, vmem],
        out_specs=[hbm, hbm, hbm, vmem],
        scratch_shapes=[dma((9,))],
        compiler_params=pltpu.CompilerParams(vmem_limit_bytes=8 * 2**20),
    )(*results)
    return block_out, grad_input, weight_grad, bias_grad


def solution(mesh):
    return jax.shard_map(
        body,
        mesh=mesh,
        in_specs=(P("dp", "tm", "tile", None, None), P(), P(), P("dp", "tm", "tile", None, None)),
        out_specs=(
            P("dp", "tm", "tile", None, None),
            P("dp", "tm", "tile", None, None),
            P("dp", None),
            P("dp"),
        ),
        check_vma=False,
    )
```

```python
import math

import jax
import jax.numpy as jnp
from jax import lax
from jax.experimental import pallas as pl
from jax.experimental.pallas import tpu as pltpu
from jax.sharding import PartitionSpec as P

F32 = jnp.float32
BF = jnp.bfloat16
MESH = pl.DeviceIdType.MESH

C = 128
FRAMES, ROWS, COLS = 8, 8, 32
AREA = ROWS * COLS
POSITIONS = FRAMES * AREA
TAPS_AB = [(a, b) for a in range(3) for b in range(3)]
SHARD = 108
BLOCK = 112
HALF = 64
HALF_AT = (0, BLOCK - HALF)
EARLY = 3 * AREA
SCALE = 1.0 / math.sqrt(524288.0)


def shift_columns(values, by):
    rows = values.shape[0]
    rolled = pltpu.roll(values, by % rows, 0)
    column = lax.broadcasted_iota(jnp.int32, values.shape, 0) & (COLS - 1)
    return jnp.where(column == (0 if by == 1 else COLS - 1), 0.0, rolled)


def forward_block(lhs, center, upstream, wf, bias):
    y = jnp.dot(lhs, wf[...].reshape(9 * C, 3 * C), preferred_element_type=F32)
    pre = y[:, C : 2 * C] + shift_columns(y[:, :C], 1) + shift_columns(y[:, 2 * C :], -1)
    pre = pre + bias[...]
    sig = 0.5 * jnp.tanh(0.5 * pre) + 0.5
    out = (center.astype(F32) + pre * sig).astype(BF)
    grad = upstream.astype(F32) * (sig * (1.0 + pre * (1.0 - sig)))
    return out, grad.astype(BF)


def keep_turned(grad, start, gt, bsum, first):
    part = jnp.sum(grad.reshape(AREA // 8, 8, C), axis=0)
    if first:
        bsum[...] = part
    else:
        bsum[...] += part
    turned = jnp.transpose(grad)
    lane = lax.broadcasted_iota(jnp.int32, (C, C), 1) & (COLS - 1)
    gt[C : 2 * C, start : start + AREA] = turned.astype(BF)
    for half in range(2):
        piece = turned[:, half * C : half * C + C]
        at = start + half * C
        ahead = jnp.where(lane == COLS - 1, 0.0, pltpu.roll(piece, C - 1, 1))
        behind = jnp.where(lane == 0, 0.0, pltpu.roll(piece, 1, 1))
        gt[0:C, at : at + C] = ahead.astype(BF)
        gt[2 * C : 3 * C, at : at + C] = behind.astype(BF)


def forward_frame(t, xp, wf, bias, ctv, bov, gp, gt, bsum, row, first):
    lhs = jnp.concatenate(
        [xp[t + a, b : b + ROWS].reshape(AREA, C) for a, b in TAPS_AB], axis=1
    )
    out, grad = forward_block(
        lhs, xp[t + 2, 1 : 1 + ROWS].reshape(AREA, C), ctv[t].reshape(AREA, C), wf, bias
    )
    bov[t] = out.reshape(ROWS, COLS, C)
    gp[t, 1 : 1 + ROWS] = grad.reshape(ROWS, COLS, C)
    at_row = lax.broadcasted_iota(jnp.int32, (AREA, C), 0) // COLS
    start = t * AREA if t < 2 else EARLY + (t - 2) * AREA
    keep_turned(jnp.where(at_row == row, 0.0, grad.astype(F32)), start, gt, bsum, first)


def forward_seam(xp, wf, bias, ctv, bov, gp, gt, bsum, row):
    lhs = jnp.concatenate(
        [xp[a : a + FRAMES, row + b].reshape(AREA, C) for a, b in TAPS_AB], axis=1
    )
    out, grad = forward_block(
        lhs, xp[2 : 2 + FRAMES, row + 1].reshape(AREA, C), ctv[:, row].reshape(AREA, C), wf, bias
    )
    bov[:, row] = out.reshape(FRAMES, COLS, C)
    gp[0:FRAMES, row + 1] = grad.reshape(FRAMES, COLS, C)
    keep_turned(grad.astype(F32), 2 * AREA, gt, bsum, False)


def early_taps(d, xp, gt, wacc):
    pairs = TAPS_AB[2 * d : 2 * d + 2]
    rhs = jnp.concatenate(
        [xp[a + 2 : a + FRAMES, b : b + ROWS].reshape(6 * AREA, C) for a, b in pairs], axis=1
    )
    lhs = gt[:, EARLY : EARLY + 6 * AREA]
    wacc[:, 2 * C * d : 2 * C * d + len(pairs) * C] = jnp.dot(
        lhs, rhs, preferred_element_type=F32
    )


def late_taps(d, xp, gt, wacc, dw, row):
    pairs = TAPS_AB[2 * d : 2 * d + 2]
    rhs = jnp.concatenate(
        [
            jnp.concatenate(
                [
                    xp[a : a + 2, b : b + ROWS].reshape(2 * AREA, C),
                    xp[a : a + FRAMES, row + b].reshape(AREA, C),
                ],
                axis=0,
            )
            for a, b in pairs
        ],
        axis=1,
    )
    out = jnp.dot(gt[:, :EARLY], rhs, preferred_element_type=F32)
    out = out + wacc[:, 2 * C * d : 2 * C * d + len(pairs) * C]
    for j in range(len(pairs)):
        for e in range(3):
            tap = (2 * d + j) * 3 + e
            dw[tap * C : tap * C + C] = jnp.transpose(
                out[e * C : e * C + C, j * C : j * C + C]
            )


def backward_frames(t, n, gp, wt, ctv, giv):
    rows = n * AREA
    lhs = jnp.concatenate(
        [gp[t + 2 - a : t + 2 - a + n, 2 - b : 2 - b + ROWS].reshape(rows, C) for a, b in TAPS_AB],
        axis=1,
    )
    y = lax.dot_general(
        lhs,
        wt[...].reshape(3 * C, 9 * C),
        (((1,), (1,)), ((), ())),
        preferred_element_type=F32,
    )
    out = y[:, C : 2 * C] + shift_columns(y[:, :C], -1) + shift_columns(y[:, 2 * C :], 1)
    out = out + ctv[t : t + n].reshape(rows, C).astype(F32)
    giv[t : t + n] = out.astype(BF).reshape(n, ROWS, COLS, C)


def kernel(
    act, ker, bias, cot, block_out, grad_input, weight_grad, bias_grad,
    xp, gp, wf, wt, ctv, bov, giv, gt, wacc, dw, bsum, hrow, hframes, hcorner,
    pk, cr, ys, yr, yown, zs, zr, fr,
    load_sem, out_sem, halo_send, halo_recv, ghalo_send, ghalo_recv,
    core_send, core_recv, y_send, y_recv, z_send, z_recv, f_send, f_recv,
):
    dp = lax.axis_index("dp")
    x = lax.axis_index("tm")
    zl = lax.axis_index("tile")
    core = lax.rem(dp, 2)
    y = lax.rem(dp // 2, 4)
    zh = dp // 8
    other = 1 - zl

    def at(zh_=None, y_=None, core_=None, x_=None, zl_=None):
        zh_ = zh if zh_ is None else zh_
        y_ = y if y_ is None else y_
        core_ = core if core_ is None else core_
        return {
            "dp": (zh_ * 4 + y_) * 2 + core_,
            "tm": x if x_ is None else x_,
            "tile": zl if zl_ is None else zl_,
        }

    def remote(src, dst, send, recv, where):
        return pltpu.make_async_remote_copy(
            src_ref=src, dst_ref=dst, send_sem=send, recv_sem=recv,
            device_id=where, device_id_type=MESH,
        )

    loads = []
    for f in range(4):
        part = pl.ds(2 * f, 2)
        loads.append(
            pltpu.make_async_copy(
                act.at[0, part], xp.at[2 + 2 * f : 4 + 2 * f, 1:9], load_sem.at[f]
            )
        )
    for a in range(3):
        for e in range(3):
            loads.append(
                pltpu.make_async_copy(
                    ker.at[3 * a : 3 * a + 3, e],
                    wf.at[3 * a : 3 * a + 3, :, e * C : e * C + C],
                    load_sem.at[4 + 3 * a + e],
                )
            )
    for f in range(4):
        part = pl.ds(2 * f, 2)
        loads.append(pltpu.make_async_copy(cot.at[0, part], ctv.at[part], load_sem.at[13 + f]))
    late = [
        pltpu.make_async_copy(ker.at[i], wt.at[:, :, i * C : i * C + C], load_sem.at[17 + i])
        for i in range(9)
    ]
    for load in loads:
        load.start()

    barrier = pltpu.get_barrier_semaphore()
    column = zh * 2 + zl
    group = x * 2 + zl
    partners = [at(zh_=lax.rem(zh + k, 4), zl_=side) for k in (2, 1, 3) for side in (zl, other)]
    partners += [at(x_=lax.rem(x + k, 4)) for k in (2, 1, 3)]
    partners += [at(x_=lax.rem(x + k, 4), zl_=other) for k in (2, 1, 3)]
    partners += [at(y_=lax.rem(y + k, 4)) for k in (2, 1, 3)]
    partners += [at(zl_=other)]
    partners += [at(core_=1 - core)]
    for partner in partners:
        pl.semaphore_signal(barrier, inc=1, device_id=partner, device_id_type=MESH)

    row_zeros = jnp.zeros((10, COLS, C), BF)
    xp[:, 0] = row_zeros
    xp[:, 9] = row_zeros
    gp[:, 9 * zl] = row_zeros
    xp[0:2, 1:9] = jnp.zeros((2, 8, COLS, C), BF)

    @pl.when(x == 3)
    def _():
        gp[8:10] = jnp.zeros((2, 10, COLS, C), BF)

    row = 7 * other
    into_row = 9 * zl
    recv_row = 9 * other
    later = jnp.minimum(x + 1, 3)
    halo_rows = remote(act.at[0, :, row], hrow, halo_send.at[0], halo_recv.at[0], at(zl_=other))
    halo_frames = remote(
        act.at[0, 6:8], hframes, halo_send.at[1], halo_recv.at[1], at(x_=later)
    )
    halo_corner = remote(
        act.at[0, 6:8, row], hcorner, halo_send.at[2], halo_recv.at[2], at(x_=later, zl_=other)
    )
    for load in loads:
        load.wait()
    for load in late:
        load.start()

    forward = (xp, wf, bias, ctv, bov, gp, gt, bsum, row)
    for t in range(2, 8):
        forward_frame(t, *forward, t == 2)
        if t == 4:
            pl.semaphore_wait(barrier, len(partners))

            @pl.when(x < 3)
            def _():
                halo_frames.start()
                halo_corner.start()

            halo_rows.start()

    for d in range(5):
        early_taps(d, xp, gt, wacc)

    halo_rows.wait_recv()
    xp[2:10, recv_row] = hrow[...]

    @pl.when(x > 0)
    def _():
        halo_frames.wait_recv()
        halo_corner.wait_recv()
        xp[0:2, 1:9] = hframes[...]
        xp[0:2, recv_row] = hcorner[...]

    forward_seam(*forward)
    forward_frame(0, *forward, False)
    forward_frame(1, *forward, False)
    outs = [pltpu.make_async_copy(bov, block_out.at[0], out_sem.at[0])]
    outs[-1].start()

    earlier = jnp.maximum(x - 1, 0)
    ghalo_rows = remote(
        gp.at[0:8, 1 + row], gp.at[0:8, into_row], ghalo_send.at[0], ghalo_recv.at[0],
        at(zl_=other),
    )
    ghalo_frames = remote(
        gp.at[0:2, 1:9], gp.at[8:10, 1:9], ghalo_send.at[1], ghalo_recv.at[1], at(x_=earlier)
    )
    ghalo_corner = remote(
        gp.at[0:2, 1 + row], gp.at[8:10, into_row], ghalo_send.at[2], ghalo_recv.at[2],
        at(x_=earlier, zl_=other),
    )

    total_bias = jnp.sum(bsum[...], axis=0, keepdims=True)
    bias_hi = total_bias.astype(BF).astype(F32)
    bias_lo = total_bias - bias_hi
    line = lax.broadcasted_iota(jnp.int32, (BLOCK, C), 0)
    tail = jnp.where(line == SHARD, bias_hi, jnp.where(line == SHARD + 1, bias_lo, 0.0))

    def pack(i):
        q, y_, core_ = i // 8, (i // 2) % 4, i % 2
        rows = jnp.where(line < SHARD, dw[SHARD * i : SHARD * i + BLOCK], tail)
        pk[q, core_, y_] = rows.astype(BF)

    def core_copy(q):
        return remote(
            pk.at[q, 1 - core], cr.at[q], core_send.at[q], core_recv.at[q], at(core_=1 - core)
        )

    def y_copy(q, k):
        return remote(
            ys.at[q, k - 1], yr.at[q, k - 1], y_send.at[q, k - 1], y_recv.at[q, k - 1],
            at(y_=lax.rem(y + k, 4)),
        )

    def y_stage(q):
        core_copy(q).wait_recv()
        for k in (2, 1, 3):
            to = lax.rem(y + k, 4)
            ys[q, k - 1] = (pk[q, core, to].astype(F32) + cr[q, to].astype(F32)).astype(BF)
            y_copy(q, k).start()
        yown[q] = pk[q, core, y].astype(F32) + cr[q, y].astype(F32)

    def z_copy(q, half):
        rows = pl.ds(HALF_AT[half], HALF)
        return remote(
            zs.at[q, rows], zr.at[column], z_send.at[q, half], z_recv.at[column],
            at(zh_=q, zl_=half),
        )

    def away(q, half):
        return jnp.logical_or(zh != q, zl != half)

    def z_stage(q):
        total = yown[q]
        for k in (1, 3, 2):
            y_copy(q, k).wait_recv()
            total = total + yr[q, k - 1].astype(F32)
        zs[q] = total.astype(BF)
        for half in range(2):

            @pl.when(away(q, half))
            def _():
                z_copy(q, half).start()

            @pl.when(jnp.logical_not(away(q, half)))
            def _():
                zr[column] = zs[q, HALF_AT[half] : HALF_AT[half] + HALF]

    packed, sent = 0, 0
    for d in range(5):
        late_taps(d, xp, gt, wacc, dw, row)
        ready = min(9, 2 * d + 2) * 3 * C
        while packed < 32 and SHARD * (packed + 1) <= ready:
            pack(packed)
            packed += 1
        while sent < 4 and packed >= 8 * (sent + 1):
            core_copy(sent).start()
            sent += 1
    @pl.when(x > 0)
    def _():
        ghalo_frames.start()
        ghalo_corner.start()

    ghalo_rows.start()

    for q in range(4):
        y_stage(q)

    z_stage(0)

    def give(t):
        outs.append(
            pltpu.make_async_copy(
                giv.at[t : t + 2], grad_input.at[0, t : t + 2], out_sem.at[1 + t // 2]
            )
        )
        outs[-1].start()

    for load in late:
        load.wait()
    remote(
        gp.at[0:8, 1 + row], gp.at[0:8, recv_row], ghalo_send.at[0], ghalo_recv.at[0],
        at(zl_=other),
    ).wait_recv()
    backward_frames(0, 2, gp, wt, ctv, giv)
    give(0)
    z_stage(1)
    backward_frames(2, 2, gp, wt, ctv, giv)
    give(2)
    z_stage(2)
    z_stage(3)
    backward_frames(4, 2, gp, wt, ctv, giv)
    give(4)

    for k in range(1, 8):
        slot = lax.rem(column + k, 8)
        remote(
            zs.at[0, 0:HALF], zr.at[slot], z_send.at[0, 1], z_recv.at[slot], at(zl_=other)
        ).wait_recv()
    total = zr[0].astype(F32)
    for slot in range(1, 8):
        total = total + zr[slot].astype(F32)
    fr[group] = total.astype(BF)

    def f_copy(k, slot):
        to = lax.rem(group + k, 8)
        return remote(
            fr.at[group], fr.at[slot], f_send.at[k - 1], f_recv.at[slot],
            at(x_=to // 2, zl_=lax.rem(to, 2)),
        )

    for k in (4, 5, 3, 2, 6, 1, 7):
        f_copy(k, group).start()

    @pl.when(x < 3)
    def _():
        ghalo_frames.wait_recv()
        remote(
            gp.at[0:2, 1 + row], gp.at[8:10, recv_row], ghalo_send.at[2], ghalo_recv.at[2],
            at(x_=later, zl_=other),
        ).wait_recv()

    backward_frames(6, 2, gp, wt, ctv, giv)
    give(6)

    for k in range(1, 8):
        f_copy(k, lax.rem(group + k, 8)).wait_recv()
    halves = []
    for half in range(2):
        total = fr[half].astype(F32)
        for g in range(1, 4):
            total = total + fr[2 * g + half].astype(F32)
        halves.append(total * SCALE)
    low = HALF - HALF_AT[1]
    end = SHARD - HALF_AT[1]
    weight_grad[0:HALF] = halves[0]
    weight_grad[HALF:SHARD] = halves[1][low:end]
    whole_bias = halves[1][end : end + 1] + halves[1][end + 1 : end + 2]
    whole_bias = jnp.broadcast_to(whole_bias, (8, C))
    bias_grad[...] = pltpu.roll(whole_bias, lax.rem(C - 4 * dp, C), 1)[0:1]

    halo_rows.wait_send()
    ghalo_rows.wait_send()

    @pl.when(x < 3)
    def _():
        halo_frames.wait_send()
        halo_corner.wait_send()

    @pl.when(x > 0)
    def _():
        ghalo_frames.wait_send()
        ghalo_corner.wait_send()

    for q in range(4):
        core_copy(q).wait_send()
        for k in range(1, 4):
            y_copy(q, k).wait_send()

        for half in range(2):

            @pl.when(away(q, half))
            def _():
                z_copy(q, half).wait_send()

    for k in range(1, 8):
        f_copy(k, group).wait_send()
    for out in outs:
        out.wait()


def hand_over(*refs):
    sem = refs[8]
    parts = [(refs[2], refs[6])]
    for i in range(2):
        for f in range(0, FRAMES, 2):
            parts.append((refs[i].at[0, f : f + 2], refs[4 + i].at[0, f : f + 2]))
    copies = [pltpu.make_async_copy(a, b, sem.at[n]) for n, (a, b) in enumerate(parts)]
    for copy in copies:
        copy.start()
    refs[7][...] = refs[3][0, 0:4]
    for copy in copies:
        copy.wait()


def body(activations, weights, conv_bias, cotangent):
    hbm = pl.BlockSpec(memory_space=pltpu.HBM)
    anywhere = pl.BlockSpec(memory_space=pl.ANY)
    vmem = pl.BlockSpec(memory_space=pltpu.VMEM)
    dma = pltpu.SemaphoreType.DMA
    shape = (1, FRAMES, ROWS, COLS, C)
    results = pl.pallas_call(
        kernel,
        out_shape=[
            jax.ShapeDtypeStruct(shape, BF),
            jax.ShapeDtypeStruct(shape, BF),
            jax.ShapeDtypeStruct((SHARD, C), F32),
            jax.ShapeDtypeStruct((1, C), F32),
        ],
        in_specs=[hbm, hbm, vmem, hbm],
        out_specs=[anywhere, anywhere, vmem, vmem],
        scratch_shapes=[
            pltpu.VMEM((10, 10, COLS, C), BF),
            pltpu.VMEM((10, 10, COLS, C), BF),
            pltpu.VMEM((9, C, 3 * C), BF),
            pltpu.VMEM((3, C, 9 * C), BF),
            pltpu.VMEM((FRAMES, ROWS, COLS, C), BF),
            pltpu.VMEM((FRAMES, ROWS, COLS, C), BF),
            pltpu.VMEM((FRAMES, ROWS, COLS, C), BF),
            pltpu.VMEM((3 * C, EARLY + 6 * AREA), BF),
            pltpu.VMEM((3 * C, 9 * C), F32),
            pltpu.VMEM((27 * C + 24, C), F32),
            pltpu.VMEM((8, C), F32),
            pltpu.VMEM((FRAMES, COLS, C), BF),
            pltpu.VMEM((2, ROWS, COLS, C), BF),
            pltpu.VMEM((2, COLS, C), BF),
            pltpu.VMEM((4, 2, 4, BLOCK, C), BF),
            pltpu.VMEM((4, 4, BLOCK, C), BF),
            pltpu.VMEM((4, 3, BLOCK, C), BF),
            pltpu.VMEM((4, 3, BLOCK, C), BF),
            pltpu.VMEM((4, BLOCK, C), F32),
            pltpu.VMEM((4, BLOCK, C), BF),
            pltpu.VMEM((8, HALF, C), BF),
            pltpu.VMEM((8, HALF, C), BF),
            dma((26,)),
            dma((5,)),
            dma((3,)),
            dma((3,)),
            dma((3,)),
            dma((3,)),
            dma((4,)),
            dma((4,)),
            dma((4, 3)),
            dma((4, 3)),
            dma((4, 2)),
            dma((8,)),
            dma((7,)),
            dma((8,)),
        ],
        compiler_params=pltpu.CompilerParams(
            collective_id=0, has_side_effects=True, vmem_limit_bytes=54000 * 1024
        ),
    )(activations, weights.reshape(9, 3, C, C), conv_bias.reshape(1, C), cotangent)
    block_out, grad_input, weight_grad, bias_grad = pl.pallas_call(
        hand_over,
        out_shape=[
            jax.ShapeDtypeStruct(shape, BF),
            jax.ShapeDtypeStruct(shape, BF),
            jax.ShapeDtypeStruct((SHARD, C), F32),
            jax.ShapeDtypeStruct((4,), F32),
        ],
        in_specs=[vmem, vmem, vmem, vmem],
        out_specs=[hbm, hbm, hbm, vmem],
        scratch_shapes=[dma((9,))],
        compiler_params=pltpu.CompilerParams(vmem_limit_bytes=8 * 2**20),
    )(*results)
    return block_out, grad_input, weight_grad, bias_grad


def solution(mesh):
    return jax.shard_map(
        body,
        mesh=mesh,
        in_specs=(P("dp", "tm", "tile", None, None), P(), P(), P("dp", "tm", "tile", None, None)),
        out_specs=(
            P("dp", "tm", "tile", None, None),
            P("dp", "tm", "tile", None, None),
            P("dp", None),
            P("dp"),
        ),
        check_vma=False,
    )
```

```python
import math

import jax
import jax.numpy as jnp
from jax import lax
from jax.experimental import pallas as pl
from jax.experimental.pallas import tpu as pltpu
from jax.sharding import PartitionSpec as P

F32 = jnp.float32
BF = jnp.bfloat16
MESH = pl.DeviceIdType.MESH

C = 128
FRAMES, ROWS, COLS = 8, 8, 32
AREA = ROWS * COLS
POSITIONS = FRAMES * AREA
TAPS_AB = [(a, b) for a in range(3) for b in range(3)]
SHARD = 108
BLOCK = 112
HALF = 64
HALF_AT = (0, BLOCK - HALF)
EARLY = 3 * AREA
SCALE = 1.0 / math.sqrt(524288.0)


def shift_columns(values, by):
    rows = values.shape[0]
    rolled = pltpu.roll(values, by % rows, 0)
    column = lax.broadcasted_iota(jnp.int32, values.shape, 0) & (COLS - 1)
    return jnp.where(column == (0 if by == 1 else COLS - 1), 0.0, rolled)


def forward_block(lhs, center, upstream, wf, bias):
    y = jnp.dot(lhs, wf[...].reshape(9 * C, 3 * C), preferred_element_type=F32)
    pre = y[:, C : 2 * C] + shift_columns(y[:, :C], 1) + shift_columns(y[:, 2 * C :], -1)
    pre = pre + bias[...]
    sig = 0.5 * jnp.tanh(0.5 * pre) + 0.5
    out = (center.astype(F32) + pre * sig).astype(BF)
    grad = upstream.astype(F32) * (sig * (1.0 + pre * (1.0 - sig)))
    return out, grad.astype(BF)


def keep_turned(grad, start, gt, bsum, first):
    part = jnp.sum(grad.reshape(AREA // 8, 8, C), axis=0)
    if first:
        bsum[...] = part
    else:
        bsum[...] += part
    turned = jnp.transpose(grad)
    lane = lax.broadcasted_iota(jnp.int32, (C, C), 1) & (COLS - 1)
    gt[C : 2 * C, start : start + AREA] = turned.astype(BF)
    for half in range(2):
        piece = turned[:, half * C : half * C + C]
        at = start + half * C
        ahead = jnp.where(lane == COLS - 1, 0.0, pltpu.roll(piece, C - 1, 1))
        behind = jnp.where(lane == 0, 0.0, pltpu.roll(piece, 1, 1))
        gt[0:C, at : at + C] = ahead.astype(BF)
        gt[2 * C : 3 * C, at : at + C] = behind.astype(BF)


def forward_frame(t, xp, wf, bias, ctv, bov, gp, gt, bsum, row, first):
    lhs = jnp.concatenate(
        [xp[t + a, b : b + ROWS].reshape(AREA, C) for a, b in TAPS_AB], axis=1
    )
    out, grad = forward_block(
        lhs, xp[t + 2, 1 : 1 + ROWS].reshape(AREA, C), ctv[t].reshape(AREA, C), wf, bias
    )
    bov[t] = out.reshape(ROWS, COLS, C)
    gp[t, 1 : 1 + ROWS] = grad.reshape(ROWS, COLS, C)
    at_row = lax.broadcasted_iota(jnp.int32, (AREA, C), 0) // COLS
    start = t * AREA if t < 2 else EARLY + (t - 2) * AREA
    keep_turned(jnp.where(at_row == row, 0.0, grad.astype(F32)), start, gt, bsum, first)


def forward_seam(xp, wf, bias, ctv, bov, gp, gt, bsum, row):
    lhs = jnp.concatenate(
        [xp[a : a + FRAMES, row + b].reshape(AREA, C) for a, b in TAPS_AB], axis=1
    )
    out, grad = forward_block(
        lhs, xp[2 : 2 + FRAMES, row + 1].reshape(AREA, C), ctv[:, row].reshape(AREA, C), wf, bias
    )
    bov[:, row] = out.reshape(FRAMES, COLS, C)
    gp[0:FRAMES, row + 1] = grad.reshape(FRAMES, COLS, C)
    keep_turned(grad.astype(F32), 2 * AREA, gt, bsum, False)


def early_taps(d, xp, gt, wacc):
    pairs = TAPS_AB[2 * d : 2 * d + 2]
    rhs = jnp.concatenate(
        [xp[a + 2 : a + FRAMES, b : b + ROWS].reshape(6 * AREA, C) for a, b in pairs], axis=1
    )
    lhs = gt[:, EARLY : EARLY + 6 * AREA]
    wacc[:, 2 * C * d : 2 * C * d + len(pairs) * C] = jnp.dot(
        lhs, rhs, preferred_element_type=F32
    )


def late_taps(d, xp, gt, wacc, dw, row):
    pairs = TAPS_AB[2 * d : 2 * d + 2]
    rhs = jnp.concatenate(
        [
            jnp.concatenate(
                [
                    xp[a : a + 2, b : b + ROWS].reshape(2 * AREA, C),
                    xp[a : a + FRAMES, row + b].reshape(AREA, C),
                ],
                axis=0,
            )
            for a, b in pairs
        ],
        axis=1,
    )
    out = jnp.dot(gt[:, :EARLY], rhs, preferred_element_type=F32)
    out = out + wacc[:, 2 * C * d : 2 * C * d + len(pairs) * C]
    for j in range(len(pairs)):
        for e in range(3):
            tap = (2 * d + j) * 3 + e
            dw[tap * C : tap * C + C] = jnp.transpose(
                out[e * C : e * C + C, j * C : j * C + C]
            )


def backward_frames(t, n, gp, wt, ctv, giv):
    rows = n * AREA
    lhs = jnp.concatenate(
        [gp[t + 2 - a : t + 2 - a + n, 2 - b : 2 - b + ROWS].reshape(rows, C) for a, b in TAPS_AB],
        axis=1,
    )
    y = lax.dot_general(
        lhs,
        wt[...].reshape(3 * C, 9 * C),
        (((1,), (1,)), ((), ())),
        preferred_element_type=F32,
    )
    out = y[:, C : 2 * C] + shift_columns(y[:, :C], -1) + shift_columns(y[:, 2 * C :], 1)
    out = out + ctv[t : t + n].reshape(rows, C).astype(F32)
    giv[t : t + n] = out.astype(BF).reshape(n, ROWS, COLS, C)


def kernel(
    act, ker, bias, cot, block_out, grad_input, weight_grad, bias_grad,
    xp, gp, wf, wt, ctv, bov, giv, gt, wacc, dw, bsum, hrow, hframes, hcorner,
    pk, cr, ys, yr, yown, zs, zr, fr,
    load_sem, out_sem, halo_send, halo_recv, ghalo_send, ghalo_recv,
    core_send, core_recv, y_send, y_recv, z_send, z_recv, f_send, f_recv,
):
    dp = lax.axis_index("dp")
    x = lax.axis_index("tm")
    zl = lax.axis_index("tile")
    core = lax.rem(dp, 2)
    y = lax.rem(dp // 2, 4)
    zh = dp // 8
    other = 1 - zl

    def at(zh_=None, y_=None, core_=None, x_=None, zl_=None):
        zh_ = zh if zh_ is None else zh_
        y_ = y if y_ is None else y_
        core_ = core if core_ is None else core_
        return {
            "dp": (zh_ * 4 + y_) * 2 + core_,
            "tm": x if x_ is None else x_,
            "tile": zl if zl_ is None else zl_,
        }

    def remote(src, dst, send, recv, where):
        return pltpu.make_async_remote_copy(
            src_ref=src, dst_ref=dst, send_sem=send, recv_sem=recv,
            device_id=where, device_id_type=MESH,
        )

    loads = []
    for f in range(4):
        part = pl.ds(2 * f, 2)
        loads.append(
            pltpu.make_async_copy(
                act.at[0, part], xp.at[2 + 2 * f : 4 + 2 * f, 1:9], load_sem.at[f]
            )
        )
    for a in range(3):
        for e in range(3):
            loads.append(
                pltpu.make_async_copy(
                    ker.at[3 * a : 3 * a + 3, e],
                    wf.at[3 * a : 3 * a + 3, :, e * C : e * C + C],
                    load_sem.at[4 + 3 * a + e],
                )
            )
    for f in range(4):
        part = pl.ds(2 * f, 2)
        loads.append(pltpu.make_async_copy(cot.at[0, part], ctv.at[part], load_sem.at[13 + f]))
    late = [
        pltpu.make_async_copy(ker.at[i], wt.at[:, :, i * C : i * C + C], load_sem.at[17 + i])
        for i in range(9)
    ]
    for load in loads:
        load.start()

    barrier = pltpu.get_barrier_semaphore()
    column = zh * 2 + zl
    group = x * 2 + zl
    partners = [at(zh_=lax.rem(zh + k, 4), zl_=side) for k in (2, 1, 3) for side in (zl, other)]
    partners += [at(x_=lax.rem(x + k, 4)) for k in (2, 1, 3)]
    partners += [at(x_=lax.rem(x + k, 4), zl_=other) for k in (2, 1, 3)]
    partners += [at(y_=lax.rem(y + k, 4)) for k in (2, 1, 3)]
    partners += [at(zl_=other)]
    partners += [at(core_=1 - core)]
    for partner in partners:
        pl.semaphore_signal(barrier, inc=1, device_id=partner, device_id_type=MESH)

    row_zeros = jnp.zeros((10, COLS, C), BF)
    xp[:, 0] = row_zeros
    xp[:, 9] = row_zeros
    gp[:, 9 * zl] = row_zeros
    xp[0:2, 1:9] = jnp.zeros((2, 8, COLS, C), BF)

    @pl.when(x == 3)
    def _():
        gp[8:10] = jnp.zeros((2, 10, COLS, C), BF)

    row = 7 * other
    into_row = 9 * zl
    recv_row = 9 * other
    later = jnp.minimum(x + 1, 3)
    halo_rows = remote(act.at[0, :, row], hrow, halo_send.at[0], halo_recv.at[0], at(zl_=other))
    halo_frames = remote(
        act.at[0, 6:8], hframes, halo_send.at[1], halo_recv.at[1], at(x_=later)
    )
    halo_corner = remote(
        act.at[0, 6:8, row], hcorner, halo_send.at[2], halo_recv.at[2], at(x_=later, zl_=other)
    )
    for load in loads:
        load.wait()
    for load in late:
        load.start()

    forward = (xp, wf, bias, ctv, bov, gp, gt, bsum, row)
    for t in range(2, 8):
        forward_frame(t, *forward, t == 2)
        if t == 3:
            pl.semaphore_wait(barrier, len(partners))

            @pl.when(x < 3)
            def _():
                halo_frames.start()
                halo_corner.start()

            halo_rows.start()

    for d in range(5):
        early_taps(d, xp, gt, wacc)

    halo_rows.wait_recv()
    xp[2:10, recv_row] = hrow[...]

    @pl.when(x > 0)
    def _():
        halo_frames.wait_recv()
        halo_corner.wait_recv()
        xp[0:2, 1:9] = hframes[...]
        xp[0:2, recv_row] = hcorner[...]

    forward_seam(*forward)
    forward_frame(0, *forward, False)
    forward_frame(1, *forward, False)
    outs = [pltpu.make_async_copy(bov, block_out.at[0], out_sem.at[0])]
    outs[-1].start()

    earlier = jnp.maximum(x - 1, 0)
    ghalo_rows = remote(
        gp.at[0:8, 1 + row], gp.at[0:8, into_row], ghalo_send.at[0], ghalo_recv.at[0],
        at(zl_=other),
    )
    ghalo_frames = remote(
        gp.at[0:2, 1:9], gp.at[8:10, 1:9], ghalo_send.at[1], ghalo_recv.at[1], at(x_=earlier)
    )
    ghalo_corner = remote(
        gp.at[0:2, 1 + row], gp.at[8:10, into_row], ghalo_send.at[2], ghalo_recv.at[2],
        at(x_=earlier, zl_=other),
    )

    total_bias = jnp.sum(bsum[...], axis=0, keepdims=True)
    bias_hi = total_bias.astype(BF).astype(F32)
    bias_lo = total_bias - bias_hi
    line = lax.broadcasted_iota(jnp.int32, (BLOCK, C), 0)
    tail = jnp.where(line == SHARD, bias_hi, jnp.where(line == SHARD + 1, bias_lo, 0.0))

    def pack(i):
        q, y_, core_ = i // 8, (i // 2) % 4, i % 2
        rows = jnp.where(line < SHARD, dw[SHARD * i : SHARD * i + BLOCK], tail)
        pk[q, core_, y_] = rows.astype(BF)

    def core_copy(q):
        return remote(
            pk.at[q, 1 - core], cr.at[q], core_send.at[q], core_recv.at[q], at(core_=1 - core)
        )

    def y_copy(q, k):
        return remote(
            ys.at[q, k - 1], yr.at[q, k - 1], y_send.at[q, k - 1], y_recv.at[q, k - 1],
            at(y_=lax.rem(y + k, 4)),
        )

    def y_stage(q):
        core_copy(q).wait_recv()
        for k in (2, 1, 3):
            to = lax.rem(y + k, 4)
            ys[q, k - 1] = (pk[q, core, to].astype(F32) + cr[q, to].astype(F32)).astype(BF)
            y_copy(q, k).start()
        yown[q] = pk[q, core, y].astype(F32) + cr[q, y].astype(F32)

    def z_copy(q, half):
        rows = pl.ds(HALF_AT[half], HALF)
        return remote(
            zs.at[q, rows], zr.at[column], z_send.at[q, half], z_recv.at[column],
            at(zh_=q, zl_=half),
        )

    def away(q, half):
        return jnp.logical_or(zh != q, zl != half)

    def z_stage(q):
        total = yown[q]
        for k in (1, 3, 2):
            y_copy(q, k).wait_recv()
            total = total + yr[q, k - 1].astype(F32)
        zs[q] = total.astype(BF)
        for half in range(2):

            @pl.when(away(q, half))
            def _():
                z_copy(q, half).start()

            @pl.when(jnp.logical_not(away(q, half)))
            def _():
                zr[column] = zs[q, HALF_AT[half] : HALF_AT[half] + HALF]

    packed, sent = 0, 0
    for d in range(5):
        late_taps(d, xp, gt, wacc, dw, row)
        ready = min(9, 2 * d + 2) * 3 * C
        while packed < 32 and SHARD * (packed + 1) <= ready:
            pack(packed)
            packed += 1
        while sent < 4 and packed >= 8 * (sent + 1):
            core_copy(sent).start()
            sent += 1
    for q in range(4):
        y_stage(q)

    @pl.when(x > 0)
    def _():
        ghalo_frames.start()
        ghalo_corner.start()

    ghalo_rows.start()


    z_stage(0)

    def give(t):
        outs.append(
            pltpu.make_async_copy(
                giv.at[t : t + 2], grad_input.at[0, t : t + 2], out_sem.at[1 + t // 2]
            )
        )
        outs[-1].start()

    for load in late:
        load.wait()
    remote(
        gp.at[0:8, 1 + row], gp.at[0:8, recv_row], ghalo_send.at[0], ghalo_recv.at[0],
        at(zl_=other),
    ).wait_recv()
    backward_frames(0, 2, gp, wt, ctv, giv)
    give(0)
    z_stage(1)
    backward_frames(2, 2, gp, wt, ctv, giv)
    give(2)
    z_stage(2)
    z_stage(3)
    backward_frames(4, 2, gp, wt, ctv, giv)
    give(4)

    for k in range(1, 8):
        slot = lax.rem(column + k, 8)
        remote(
            zs.at[0, 0:HALF], zr.at[slot], z_send.at[0, 1], z_recv.at[slot], at(zl_=other)
        ).wait_recv()
    total = zr[0].astype(F32)
    for slot in range(1, 8):
        total = total + zr[slot].astype(F32)
    fr[group] = total.astype(BF)

    def f_copy(k, slot):
        to = lax.rem(group + k, 8)
        return remote(
            fr.at[group], fr.at[slot], f_send.at[k - 1], f_recv.at[slot],
            at(x_=to // 2, zl_=lax.rem(to, 2)),
        )

    for k in (4, 5, 3, 2, 6, 1, 7):
        f_copy(k, group).start()

    @pl.when(x < 3)
    def _():
        ghalo_frames.wait_recv()
        remote(
            gp.at[0:2, 1 + row], gp.at[8:10, recv_row], ghalo_send.at[2], ghalo_recv.at[2],
            at(x_=later, zl_=other),
        ).wait_recv()

    backward_frames(6, 2, gp, wt, ctv, giv)
    give(6)

    for k in range(1, 8):
        f_copy(k, lax.rem(group + k, 8)).wait_recv()
    halves = []
    for half in range(2):
        total = fr[half].astype(F32)
        for g in range(1, 4):
            total = total + fr[2 * g + half].astype(F32)
        halves.append(total * SCALE)
    low = HALF - HALF_AT[1]
    end = SHARD - HALF_AT[1]
    weight_grad[0:HALF] = halves[0]
    weight_grad[HALF:SHARD] = halves[1][low:end]
    whole_bias = halves[1][end : end + 1] + halves[1][end + 1 : end + 2]
    whole_bias = jnp.broadcast_to(whole_bias, (8, C))
    bias_grad[...] = pltpu.roll(whole_bias, lax.rem(C - 4 * dp, C), 1)[0:1]

    halo_rows.wait_send()
    ghalo_rows.wait_send()

    @pl.when(x < 3)
    def _():
        halo_frames.wait_send()
        halo_corner.wait_send()

    @pl.when(x > 0)
    def _():
        ghalo_frames.wait_send()
        ghalo_corner.wait_send()

    for q in range(4):
        core_copy(q).wait_send()
        for k in range(1, 4):
            y_copy(q, k).wait_send()

        for half in range(2):

            @pl.when(away(q, half))
            def _():
                z_copy(q, half).wait_send()

    for k in range(1, 8):
        f_copy(k, group).wait_send()
    for out in outs:
        out.wait()


def hand_over(*refs):
    sem = refs[8]
    parts = [(refs[2], refs[6])]
    for i in range(2):
        for f in range(0, FRAMES, 2):
            parts.append((refs[i].at[0, f : f + 2], refs[4 + i].at[0, f : f + 2]))
    copies = [pltpu.make_async_copy(a, b, sem.at[n]) for n, (a, b) in enumerate(parts)]
    for copy in copies:
        copy.start()
    refs[7][...] = refs[3][0, 0:4]
    for copy in copies:
        copy.wait()


def body(activations, weights, conv_bias, cotangent):
    hbm = pl.BlockSpec(memory_space=pltpu.HBM)
    anywhere = pl.BlockSpec(memory_space=pl.ANY)
    vmem = pl.BlockSpec(memory_space=pltpu.VMEM)
    dma = pltpu.SemaphoreType.DMA
    shape = (1, FRAMES, ROWS, COLS, C)
    results = pl.pallas_call(
        kernel,
        out_shape=[
            jax.ShapeDtypeStruct(shape, BF),
            jax.ShapeDtypeStruct(shape, BF),
            jax.ShapeDtypeStruct((SHARD, C), F32),
            jax.ShapeDtypeStruct((1, C), F32),
        ],
        in_specs=[hbm, hbm, vmem, hbm],
        out_specs=[anywhere, anywhere, vmem, vmem],
        scratch_shapes=[
            pltpu.VMEM((10, 10, COLS, C), BF),
            pltpu.VMEM((10, 10, COLS, C), BF),
            pltpu.VMEM((9, C, 3 * C), BF),
            pltpu.VMEM((3, C, 9 * C), BF),
            pltpu.VMEM((FRAMES, ROWS, COLS, C), BF),
            pltpu.VMEM((FRAMES, ROWS, COLS, C), BF),
            pltpu.VMEM((FRAMES, ROWS, COLS, C), BF),
            pltpu.VMEM((3 * C, EARLY + 6 * AREA), BF),
            pltpu.VMEM((3 * C, 9 * C), F32),
            pltpu.VMEM((27 * C + 24, C), F32),
            pltpu.VMEM((8, C), F32),
            pltpu.VMEM((FRAMES, COLS, C), BF),
            pltpu.VMEM((2, ROWS, COLS, C), BF),
            pltpu.VMEM((2, COLS, C), BF),
            pltpu.VMEM((4, 2, 4, BLOCK, C), BF),
            pltpu.VMEM((4, 4, BLOCK, C), BF),
            pltpu.VMEM((4, 3, BLOCK, C), BF),
            pltpu.VMEM((4, 3, BLOCK, C), BF),
            pltpu.VMEM((4, BLOCK, C), F32),
            pltpu.VMEM((4, BLOCK, C), BF),
            pltpu.VMEM((8, HALF, C), BF),
            pltpu.VMEM((8, HALF, C), BF),
            dma((26,)),
            dma((5,)),
            dma((3,)),
            dma((3,)),
            dma((3,)),
            dma((3,)),
            dma((4,)),
            dma((4,)),
            dma((4, 3)),
            dma((4, 3)),
            dma((4, 2)),
            dma((8,)),
            dma((7,)),
            dma((8,)),
        ],
        compiler_params=pltpu.CompilerParams(
            collective_id=0, has_side_effects=True, vmem_limit_bytes=54000 * 1024
        ),
    )(activations, weights.reshape(9, 3, C, C), conv_bias.reshape(1, C), cotangent)
    block_out, grad_input, weight_grad, bias_grad = pl.pallas_call(
        hand_over,
        out_shape=[
            jax.ShapeDtypeStruct(shape, BF),
            jax.ShapeDtypeStruct(shape, BF),
            jax.ShapeDtypeStruct((SHARD, C), F32),
            jax.ShapeDtypeStruct((4,), F32),
        ],
        in_specs=[vmem, vmem, vmem, vmem],
        out_specs=[hbm, hbm, hbm, vmem],
        scratch_shapes=[dma((9,))],
        compiler_params=pltpu.CompilerParams(vmem_limit_bytes=8 * 2**20),
    )(*results)
    return block_out, grad_input, weight_grad, bias_grad


def solution(mesh):
    return jax.shard_map(
        body,
        mesh=mesh,
        in_specs=(P("dp", "tm", "tile", None, None), P(), P(), P("dp", "tm", "tile", None, None)),
        out_specs=(
            P("dp", "tm", "tile", None, None),
            P("dp", "tm", "tile", None, None),
            P("dp", None),
            P("dp"),
        ),
        check_vma=False,
    )
```
